32 devices in a mesh: batch: 16 (over z, y, x), rows: 2 (over core).
Axes of the slice: x: 2, y: 2, z: 4, core: 2. Of those that a mesh axis runs over, the one named last changes fastest.
Arguments:
- images: bfloat16 [512, 28, 28, 512], P('batch', 'rows'), may hold values from -6 to 6
- counts: int32 [16], P('batch'), may hold values from 16 to 32, as said below
- w_in: bfloat16 [512, 128], replicated, may hold values from -0.25 to 0.25
- gain_a: float32 [128], replicated, may hold values from 0.5 to 1.5
- shift_a: float32 [128], replicated, may hold values from -3 to 3
- w_mid: bfloat16 [3, 3, 128, 128], replicated, may hold values from -0.1875 to 0.1875
- gain_b: float32 [128], replicated, may hold values from 0.5 to 1.5
- shift_b: float32 [128], replicated, may hold values from -3 to 3
- w_out: bfloat16 [128, 512], replicated, may hold values from -0.5 to 0.5
- gain_c: float32 [512], replicated, may hold values from 0.5 to 1.5
- shift_c: float32 [512], replicated, may hold values from -3 to 3
- cotangent: bfloat16 [512, 28, 28, 512], P('batch', 'rows'), may hold values from -8 to 8
Outputs:
- block_out: bfloat16 [512, 28, 28, 512], P('batch', 'rows')
- grad_images: bfloat16 [512, 28, 28, 512], P('batch', 'rows')
- grad_w_in: float32 [512, 128], replicated
- grad_gain_a: float32 [128], replicated
- grad_shift_a: float32 [128], replicated
- grad_w_mid: float32 [3, 3, 128, 128], replicated
- grad_gain_b: float32 [128], replicated
- grad_shift_b: float32 [128], replicated
- grad_w_out: float32 [128, 512], replicated
- grad_gain_c: float32 [512], replicated
- grad_shift_c: float32 [512], replicated
The draws below stay inside these ranges and needn't reach their ends.
Inputs may be any that keep to these rules, and one draw needn't show every extreme that they name: Each entry counts the live leading slots of its batch index; at least one index is full.
All inputs are finite; a program needn't handle non-finite values.
Results may differ from the reference program's by a relative error of at most 0.0068.
Values may be sent and summed in bfloat16 or wider, within the bound.
No kernel may reach another device: no remote copies, remote signals or barrier semaphores. Data moves between devices by JAX's collectives and lax.ppermute only.
A program may use at most 256 MiB of HBM per device.

```python
import jax
import jax.numpy as jnp
from jax import lax

C = 512
MID = 128
H = 28
W = 28
IMG_DEV = 32
IMAGES = 512
N_BATCH = 16


def common_field(key):
    return jax.random.normal(key, (IMAGES, H, W, C), jnp.float32)


def draw_images(key, part):
    base = common_field(key)
    key = jax.random.fold_in(key, 11)
    scale_key = jax.random.fold_in(key, 1)
    global_key = jax.random.fold_in(key, 2)
    device_key = jax.random.fold_in(key, 3)
    pixel_key = jax.random.fold_in(key, 4)
    loading_key = jax.random.fold_in(key, 5)
    device_scale = jnp.exp(jax.random.uniform(scale_key, (N_BATCH,), jnp.float32, -0.7, 0.4))
    global_offset = 0.5 * jax.random.normal(global_key, (C,), jnp.float32)
    device_offset = 0.4 * jax.random.normal(device_key, (N_BATCH, C), jnp.float32)
    pixel_common = 0.4 * jax.random.normal(pixel_key, (IMAGES, H, W, 1), jnp.float32)
    loading = jax.random.normal(loading_key, (C,), jnp.float32)
    slot_scale = jnp.repeat(device_scale, IMG_DEV)[:, None, None, None]
    slot_offset = jnp.repeat(device_offset, IMG_DEV, axis=0)[:, None, None, :]
    rough_part = base
    values = rough_part * slot_scale + global_offset + slot_offset + pixel_common * loading
    return jnp.clip(values, -6.0, 6.0).astype(jnp.bfloat16)


def draw_cotangent(key, part):
    base = common_field(key)
    key = jax.random.fold_in(key, 13)
    offset_key, noise_key = jax.random.split(key)
    offset = 0.7 * jax.random.normal(offset_key, (C,), jnp.float32)
    noise = jax.random.normal(noise_key, (IMAGES, H, W, C), jnp.float32)
    values = noise + offset + 0.5 * base
    return jnp.clip(values, -8.0, 8.0).astype(jnp.bfloat16)


def draw_counts(key, part):
    key = jax.random.fold_in(key, 5)
    first_key, pick_key = jax.random.split(key)
    lowest = max(1, IMG_DEV // 2)
    drawn = jax.random.randint(first_key, (N_BATCH,), lowest, IMG_DEV + 1)
    chosen = jax.random.randint(pick_key, (), 0, N_BATCH)
    return jnp.where(jnp.arange(N_BATCH) == chosen, IMG_DEV, drawn).astype(jnp.int32)


def bell_draw(stream_key, dims, width, reach, held_as=jnp.bfloat16):
    entries = jax.random.normal(stream_key, dims, jnp.float32) * width
    return jnp.minimum(jnp.maximum(entries, -reach), reach).astype(held_as)


def setup_inputs(seed: int = 0) -> dict:
    keys = jax.random.split(jax.random.key(seed), 13)
    images = draw_images(jax.random.fold_in(keys[12], 71), 0)
    counts = draw_counts(jax.random.fold_in(keys[12], 71), 0)
    w_in = bell_draw(keys[2], (C, MID), C ** -0.5, 0.25)
    gain_a = jnp.clip(jax.random.uniform(keys[3], (MID,), jnp.float32, 0.5, 1.5), 0.5, 1.5)
    shift_a = bell_draw(keys[4], (MID,), 0.5, 3.0, jnp.float32)
    w_mid = bell_draw(keys[5], (3, 3, MID, MID), (9 * MID) ** -0.5, 0.1875)
    gain_b = jnp.clip(jax.random.uniform(keys[6], (MID,), jnp.float32, 0.5, 1.5), 0.5, 1.5)
    shift_b = bell_draw(keys[7], (MID,), 0.5, 3.0, jnp.float32)
    w_out = bell_draw(keys[8], (MID, C), MID ** -0.5, 0.5)
    gain_c = jnp.clip(jax.random.uniform(keys[9], (C,), jnp.float32, 0.5, 1.5), 0.5, 1.5)
    shift_c = bell_draw(keys[10], (C,), 0.5, 3.0, jnp.float32)
    cotangent = draw_cotangent(jax.random.fold_in(keys[12], 71), 0)
    return dict(images=images, counts=counts, w_in=w_in, gain_a=gain_a, shift_a=shift_a, w_mid=w_mid, gain_b=gain_b, shift_b=shift_b, w_out=w_out, gain_c=gain_c, shift_c=shift_c, cotangent=cotangent)


epsilon = 1e-05

@jax.custom_vjp
def low(v):
    return lax.optimization_barrier(v.astype(jnp.bfloat16)).astype(jnp.float32)

@jax.custom_vjp
def low_back(v):
    return v

def low_keep(v):
    return (low(v), None)

def low_pass(kept, grad):
    return (grad,)

def back_keep(v):
    return (v, None)

def back_low(kept, grad):
    return (low(grad),)
low.defvjp(low_keep, low_pass)
low_back.defvjp(back_keep, back_low)

def batch_norm(values, valid_mask, pixel_total, gain_value, shift_value):
    mean_value = lax.optimization_barrier(jnp.sum(values * valid_mask, axis=(0, 1, 2))) / pixel_total
    square_mean = lax.optimization_barrier(jnp.sum(values * values * valid_mask, axis=(0, 1, 2))) / pixel_total
    inv_std = lax.rsqrt(square_mean - mean_value * mean_value + epsilon)
    return (values - mean_value) * inv_std * gain_value + shift_value

def reference(images, counts, w_in, gain_a, shift_a, w_mid, gain_b, shift_b, w_out, gain_c, shift_c, cotangent):
    slots = jnp.arange(IMAGES, dtype=jnp.int32)
    owners = (slots // IMG_DEV).astype(jnp.int32)
    live = slots % IMG_DEV < counts[owners]
    valid_mask = live.astype(jnp.float32)[:, None, None, None]
    pixel_total = jnp.sum(counts).astype(jnp.float32) * float(H * W)
    highest = lax.Precision.HIGHEST

    def forward(image_f, win, gaina, shifta, wmid, gainb, shiftb, wout, gainc, shiftc):
        masked = image_f * valid_mask
        conv_first = low_back(jnp.einsum('bhwc,cd->bhwd', masked, win, precision=highest))
        act_first = low(jax.nn.gelu(batch_norm(conv_first, valid_mask, pixel_total, gaina, shifta)))
        conv_mid = low_back(lax.conv_general_dilated(act_first, wmid, (1, 1), 'SAME', dimension_numbers=('NHWC', 'HWIO', 'NHWC'), precision=highest))
        act_mid = low(jax.nn.gelu(batch_norm(conv_mid, valid_mask, pixel_total, gainb, shiftb)))
        conv_last = low_back(jnp.einsum('bhwc,cd->bhwd', act_mid, wout, precision=highest))
        return jax.nn.gelu(batch_norm(conv_last, valid_mask, pixel_total, gainc, shiftc) + masked)
    primal = (images.astype(jnp.float32), w_in.astype(jnp.float32), gain_a, shift_a, w_mid.astype(jnp.float32), gain_b, shift_b, w_out.astype(jnp.float32), gain_c, shift_c)
    result, pullback = jax.vjp(forward, *primal)
    grads = pullback(cotangent.astype(jnp.float32) * valid_mask)
    return (result.astype(jnp.bfloat16), grads[0].astype(jnp.bfloat16), grads[1], grads[2], grads[3], grads[4], grads[5], grads[6], grads[7], grads[8], grads[9])
```

```python
import functools
import math

import jax
import jax.numpy as jnp
from jax import lax
from jax.experimental import pallas as pl
from jax.experimental.pallas import tpu as pltpu
from jax.sharding import PartitionSpec as P

epsilon = 1e-05
axes = ("batch", "rows")
f32 = jnp.float32
bf16 = jnp.bfloat16
C0 = math.sqrt(2.0 / math.pi)
C1 = C0 * 0.044715
HIGH = lax.Precision.HIGHEST


def partner(block, mask):
    total = lax.axis_size("batch") * lax.axis_size("rows")
    return lax.ppermute(block, axes, [(i, i ^ mask) for i in range(total)])


def swapped_sum(block, groups):
    size = len(groups[0])
    spread = jnp.broadcast_to(block[None], (size,) + block.shape)
    arrived = lax.all_to_all(spread, "batch", 0, 0, axis_index_groups=groups, tiled=True)
    return jnp.sum(arrived, axis=0)


def summed_at_once(block):
    total = lax.axis_size("batch") * lax.axis_size("rows")
    spread = jnp.broadcast_to(block[None], (total,) + block.shape)
    return jnp.sum(lax.all_to_all(spread, axes, 0, 0, tiled=True), axis=0)


def summed_by_swap(block, near=None):
    block = block + partner(block, 1)
    count = lax.axis_size("batch")
    if near is None or count % near:
        return swapped_sum(block, [list(range(count))])
    block = swapped_sum(block, [list(range(i, i + near)) for i in range(0, count, near)])
    return swapped_sum(block, [list(range(i, count, near)) for i in range(near)])


def gelu_terms(u):
    square = u * u
    inner = C0 + C1 * square
    half = 0.5 * jnp.tanh(u * inner) + 0.5
    value = u * half
    slope = half + value * (1.0 - half) * (6.0 * inner - 4.0 * C0)
    return value, slope


def gelu_value(u):
    return u * (0.5 * jnp.tanh(u * (C0 + C1 * u * u)) + 0.5)


def moments(total, squares, pixels):
    mean = total / pixels
    return mean, lax.rsqrt(squares / pixels - mean * mean + epsilon)


def fold8(values):
    lanes = values.shape[-1]
    return jnp.sum(values.reshape(values.size // (8 * lanes), 8, lanes), axis=0)


def total_row(values):
    return jnp.sum(values, axis=0, keepdims=True)


def wide(ref, start):
    return jnp.concatenate([ref[start + i : start + i + 1, :] for i in range(4)], axis=1)


def put_wide(ref, start, row):
    for i in range(4):
        ref[start + i : start + i + 1, :] = row[:, i * 128 : (i + 1) * 128]


def dot_tn(a, b):
    return lax.dot_general(a, b, (((0,), (0,)), ((), ())), preferred_element_type=f32)


def dot_nt(a, b, precision=None):
    return lax.dot_general(
        a, b, (((1,), (1,)), ((), ())), preferred_element_type=f32, precision=precision
    )


def dot(a, b, precision=None):
    return jnp.dot(a, b, preferred_element_type=f32, precision=precision)


def split_two(values):
    high = values.astype(bf16)
    return high, (values - high.astype(f32)).astype(bf16)


def dot_halves(a, b):
    high, low = split_two(a)
    return dot(high, b) + dot(low, b)


def row_of_sums(values):
    high, low = split_two(values)
    one = jnp.ones((16, values.shape[1]), bf16)
    return (dot_nt(one, high) + dot_nt(one, low))[0:8, :]


def call(body, grid, ins, outs, scratch, name, flops, bytes_moved, aliases=None):
    return pl.pallas_call(
        body,
        grid=(grid,),
        in_specs=ins,
        out_specs=[spec for spec, _ in outs],
        out_shape=[shape for _, shape in outs],
        scratch_shapes=scratch,
        name=name,
        input_output_aliases=aliases or {},
        compiler_params=pltpu.CompilerParams(
            dimension_semantics=("arbitrary",), vmem_limit_bytes=52 << 20
        ),
        cost_estimate=pl.CostEstimate(
            flops=int(flops), bytes_accessed=int(bytes_moved), transcendentals=0
        ),
    )


SMEM = pl.BlockSpec(memory_space=pltpu.SMEM)
ANY = pl.BlockSpec(memory_space=pl.ANY)


def whole_spec(shape):
    return pl.BlockSpec(tuple(shape), lambda i: (0,) * len(shape))


def step_spec(shape, place=lambda i: i):
    return pl.BlockSpec(tuple(shape), lambda i: (place(i),) + (0,) * (len(shape) - 1))


def whole_out(shape, dtype=f32):
    return (whole_spec(shape), jax.ShapeDtypeStruct(shape, dtype))


def step_out(count, shape, dtype, place=lambda i: i):
    return (
        step_spec(shape, place),
        jax.ShapeDtypeStruct((count,) + tuple(shape[1:]), dtype),
    )


def live(info, images, lanes):
    return lax.broadcasted_iota(jnp.int32, (images, lanes), 0) < info[0]


def groups(columns):
    return [(c, min(4, columns - c)) for c in range(0, columns, 4)]


def take_edge(info, edge_ref, ref):
    step = pl.program_id(0)

    @pl.when((step == 0) & (info[1] == 1))
    def _():
        edge_ref[...] = ref[0].astype(edge_ref.dtype)

    @pl.when((step == pl.num_programs(0) - 1) & (info[1] == 0))
    def _():
        edge_ref[...] = ref[ref.shape[0] - 1].astype(edge_ref.dtype)


def first_body(info, x_ref, w_ref, z_ref, edge_ref, stat_ref, zacc):
    step = pl.program_id(0)
    tall, columns, images = x_ref.shape[:3]
    area = columns * images

    @pl.when(step == 0)
    def _():
        zacc[...] = jnp.zeros_like(zacc)

    mask = live(info, images, 128)
    for r in range(tall):
        x = x_ref[r].reshape(area, 512)
        z = dot(x, w_ref[...]).reshape(columns, images, 128)
        z = jnp.where(mask, z, 0.0)
        z_ref[r] = z
        zacc[0] += fold8(z)
        zacc[1] += fold8(z * z)
    take_edge(info, edge_ref, z_ref)

    @pl.when(step == pl.num_programs(0) - 1)
    def _():
        pixels = (info[0] * (pl.num_programs(0) * tall * columns)).astype(f32)
        stat_ref[...] = jnp.zeros_like(stat_ref)
        stat_ref[0:1, :] = total_row(zacc[0])
        stat_ref[1:2, :] = total_row(zacc[1])
        stat_ref[2:3, :] = jnp.full((1, 128), pixels, f32)


def cross_body(x_ref, z_ref, xz_ref, acc):
    step = pl.program_id(0)
    tall, columns, images = x_ref.shape[:3]
    area = columns * images

    @pl.when(step == 0)
    def _():
        acc[...] = jnp.zeros_like(acc)

    for r in range(tall):
        z = z_ref[r].astype(bf16).reshape(area, 128)
        acc[...] += dot_tn(z, x_ref[r].reshape(area, 512))

    @pl.when(step == pl.num_programs(0) - 1)
    def _():
        for i in range(4):
            xz_ref[i * 128 : (i + 1) * 128, :] = acc[:, i * 128 : (i + 1) * 128]


def paired_weights(w_ref, target):
    for r in range(4):
        for u in range(3):
            for o in range(2):
                t = r - o
                base = (r * 3 + u) * 128
                if 0 <= t <= 2:
                    block = w_ref[t, u]
                else:
                    block = jnp.zeros((128, 128), bf16)
                target[base : base + 128, o * 128 : (o + 1) * 128] = block


def window(frame, pair):
    columns, images = frame.shape[1] - 2, frame.shape[2]
    parts = [
        frame[2 * pair + r, u : u + columns].reshape(columns * images, 128)
        for r in range(4)
        for u in range(3)
    ]
    return jnp.concatenate(parts, axis=1)


def clear_frame(frame):
    tall, wide_columns = frame.shape[:2]
    zero = jnp.zeros(frame.shape[2:], frame.dtype)
    for e in range(tall):
        frame[e, 0] = zero
        frame[e, wide_columns - 1] = zero
    for c in range(wide_columns):
        frame[0, c] = zero
        frame[tall - 1, c] = zero


def middle_body(
    info, st1, ga, sa, z_ref, edge_ref, w_ref, xz_ref,
    z2_ref, a_ref, stat_ref, frame, wide_w, coef, zacc,
):
    step = pl.program_id(0)
    last = pl.num_programs(0) - 1
    columns, images = z_ref.shape[1:3]
    area = columns * images

    def activated(z):
        return gelu_value(z * coef[0:1, :] + coef[1:2, :]).astype(bf16)

    @pl.when(step == 0)
    def _():
        mean, inv = moments(st1[0:1, :], st1[1:2, :], st1[2:3, :])
        scale = ga[...] * inv
        coef[0:1, :] = scale
        coef[1:2, :] = sa[...] - mean * scale
        paired_weights(w_ref, wide_w)
        zacc[...] = jnp.zeros_like(zacc)
        clear_frame(frame)
        place = (1 - info[1]) * (frame.shape[0] - 1)
        for c, n in groups(columns):
            frame[place, 1 + c : 1 + c + n] = activated(edge_ref[c : c + n])

    @pl.when(step < last)
    def _():
        for r in range(2):
            for c, n in groups(columns):
                value = activated(z_ref[r, c : c + n])
                frame[2 * step + 1 + r, 1 + c : 1 + c + n] = value
                a_ref[r, c : c + n] = value

    @pl.when(step > 0)
    def _():
        mask = live(info, images, 128)
        y = dot(window(frame, step - 1), wide_w[...])
        for r in range(2):
            z = y[:, r * 128 : (r + 1) * 128].reshape(columns, images, 128)
            z2_ref[r] = z
            z = jnp.where(mask, z, 0.0)
            zacc[0] += fold8(z)
            zacc[1] += fold8(z * z)

    @pl.when(step == last)
    def _():
        stat_ref[...] = jnp.zeros_like(stat_ref)
        for k in range(2):
            stat_ref[k : k + 1, :] = total_row(zacc[k])


def second_coef(st1, st2, gb, sb, coef):
    mean, inv = moments(st2[0:1, :], st2[1:2, :], st1[2:3, :])
    scale = gb[...] * inv
    coef[0:1, :] = scale
    coef[1:2, :] = sb[...] - mean * scale
    coef[2:3, :] = inv
    coef[3:4, :] = -mean * inv


def second_body(
    info, st1, st2, gb, sb, z_ref, wo_ref,
    act_ref, g_ref, gx_ref, ye_ref, ze_ref, st_ref, gram_ref, coef, cross, sums,
):
    step = pl.program_id(0)
    tall, columns, images = z_ref.shape[:3]
    area = columns * images

    @pl.when(step == 0)
    def _():
        second_coef(st1, st2, gb, sb, coef)
        cross[...] = jnp.zeros_like(cross)
        sums[...] = jnp.zeros_like(sums)

    mask = live(info, images, 128)
    scale, bias, inv, shift = (coef[i : i + 1, :] for i in range(4))
    edge_row = (1 - info[1]) * (tall - 1)
    at_edge = step == (1 - info[1]) * (pl.num_programs(0) - 1)
    totals = [jnp.zeros((8, 128), f32) for _ in range(3)]
    for r in range(tall):
        acts, others = [], []
        for c, n in groups(columns):
            z = z_ref[r, c : c + n]
            value, slope = gelu_terms(z * scale + bias)
            dotted = jnp.where(mask, slope * (z * inv + shift), 0.0).astype(bf16)
            slope = jnp.where(mask, slope, 0.0).astype(bf16)
            g_ref[r, c : c + n] = slope
            gx_ref[r, c : c + n] = dotted
            value = value.astype(bf16)
            act_ref[r, c : c + n] = value
            value = jnp.where(mask, value, jnp.zeros((), bf16))
            acts.append(value.reshape(n * images, 128))
            for k, part in enumerate((slope, dotted, value)):
                totals[k] += fold8(part.astype(f32))
        acts = jnp.concatenate(acts, axis=0)
        cross[...] += dot_tn(
            acts,
            jnp.concatenate(
                [acts, g_ref[r].reshape(area, 128), gx_ref[r].reshape(area, 128)], axis=1
            ),
        )

        @pl.when(at_edge & (edge_row == r))
        def _():
            ye_ref[:, :, 0:128] = act_ref[r]
            ye_ref[:, :, 128:256] = g_ref[r]
            ze_ref[...] = z_ref[r]

    for k in range(3):
        sums[k] += totals[k]

    @pl.when(step == pl.num_programs(0) - 1)
    def _():
        gram = cross[:, 0:128]
        gram_ref[0:128, :] = gram
        st_ref[8:16, :] = jnp.zeros((8, 128), f32)
        st_ref[8:9, :] = total_row(sums[2])
        gram_ref[128:136, :] = st_ref[8:16, :]
        spread = dot_halves(gram_ref[...], wo_ref[...])
        put_wide(st_ref, 0, spread[128:129, :])
        put_wide(st_ref, 4, total_row(spread[0:128, :] * wo_ref[...].astype(f32)))
        st_ref[9:16, :] = jnp.zeros((7, 128), f32)
        for k in range(2):
            st_ref[9 + k : 10 + k, :] = total_row(sums[k])
        st_ref[16:144, :] = cross[:, 128:256]
        st_ref[144:272, :] = cross[:, 256:384]


def last_body(
    info, st1, st3, gc, sc, y_ref, g_ref, gx_ref, x_ref, cot_ref, wo_ref,
    out_ref, e_ref, t_ref, te_ref, st_ref, u_ref, ws_ref,
    coef, w_two, w_turn, z_buf, cross, sums, sums_b,
):
    step = pl.program_id(0)
    tall, columns, images = x_ref.shape[:3]
    area = columns * images

    @pl.when(step == 0)
    def _():
        mean, inv = moments(wide(st3, 0), wide(st3, 4), st1[2:3, 0:1])
        scale = gc[...] * inv
        coef[0:1, :] = sc[...] - mean * scale
        high, low = split_two(wo_ref[...].astype(f32) * scale)
        w_two[0:128, :] = high
        w_two[128:256, :] = low
        ws_ref[...] = w_two[...]
        w_turn[:, 0:128] = jnp.transpose(w_two[0:128, :])
        w_turn[:, 128:256] = jnp.transpose(w_two[128:256, :])
        cross[...] = jnp.zeros_like(cross)
        sums[...] = jnp.zeros_like(sums)
        sums_b[...] = jnp.zeros_like(sums_b)

    mask = live(info, images, 512)
    bias = coef[0:1, :]
    zero = jnp.zeros((), bf16)
    half = columns // 2
    parts = [(r, c) for r in range(tall) for c in range(0, columns, half)]
    n = half * images

    def product(r, c):
        act = y_ref[r, c : c + half].reshape(n, 128)
        z = dot(jnp.concatenate([act, act], axis=1), w_two[...])
        z_buf[r, c : c + half] = z.reshape(half, images, 512)

    def pointwise(r, first):
        total_e = jnp.zeros((8, 512), f32)
        total_x = jnp.zeros((8, 512), f32)
        for c in range(first, first + half):
            x = jnp.where(mask, x_ref[r, c], zero).astype(f32)
            total_x += fold8(x)
            value, slope = gelu_terms(z_buf[r, c] + (bias + x))
            out_ref[r, c] = value.astype(bf16)
            cot = jnp.where(mask, cot_ref[r, c], zero).astype(f32)
            e = slope * cot
            total_e += fold8(e)
            e_ref[r, c] = e.astype(bf16)
        sums[0] += total_e
        sums[1] += total_x

    def collect(r, c):
        e = e_ref[r, c : c + half].reshape(n, 512)
        cross[...] += dot_tn(y_ref[r, c : c + half].reshape(n, 128), e)
        y = dot(e, w_turn[...])
        t = (y[:, 0:128] + y[:, 128:256]).reshape(half, images, 128)
        t_ref[r, c : c + half] = t
        sums_b[0] += fold8(t * g_ref[r, c : c + half].astype(f32))
        sums_b[1] += fold8(t * gx_ref[r, c : c + half].astype(f32))

    product(*parts[0])
    for k in range(len(parts) + 1):
        if k + 1 < len(parts):
            product(*parts[k + 1])
        if k > 0:
            collect(*parts[k - 1])
        if k < len(parts):
            pointwise(*parts[k])
    take_edge(info, te_ref, t_ref)

    @pl.when(step == pl.num_programs(0) - 1)
    def _():
        u_ref[...] = cross[...]
        put_wide(st_ref, 0, total_row(sums[0]))
        put_wide(st_ref, 4, total_row(wo_ref[...].astype(f32) * cross[...]))
        put_wide(st_ref, 10, total_row(sums[1]))
        for k in range(2):
            st_ref[8 + k : 9 + k, :] = total_row(sums_b[k])
            st_ref[14 + k : 15 + k, :] = jnp.zeros((1, 128), f32)


def back_body(
    info, st1, st2, st3, st4, kept_ref, other_ref, own4, xz_ref, gram_ref, u_ref, ga, sa, gb, gc, wo_ref, ws_ref, wt_ref,
    y_ref, s_ref, ye_ref, z2_ref, ze_ref, t_ref, te_ref, a_ref, z1_ref, x_ref,
    h_ref, mine_ref, sent_ref, small_ref,
    coef, mm, wide_w, frame, dacc, vacc, sums, packed,
):
    step = pl.program_id(0)
    last = pl.num_programs(0) - 1
    columns, images = z1_ref.shape[1:3]
    area = columns * images
    mask = live(info, images, 128)

    def second_back(t, product, slope, z):
        kappa, scale_b, beta, alpha = (coef[i : i + 1, :] for i in range(4))
        through = t - kappa - product[..., 0:128] - product[..., 128:256]
        grad = scale_b * (slope.astype(f32) * through) - (alpha + beta * z)
        return jnp.where(mask, grad, 0.0).astype(bf16)

    @pl.when(step == 0)
    def _():
        pixels = st1[2:3, :]
        pixel = st1[2:3, 0:1]
        mean_a, inv_a = moments(st1[0:1, :], st1[1:2, :], pixels)
        mean_b, inv_b = moments(st2[0:1, :], st2[1:2, :], pixels)
        mean_c, inv_c = moments(wide(st3, 0), wide(st3, 4), pixel)
        total_c = wide(st4, 0)
        dot_c = inv_c * (wide(st4, 4) - mean_c * total_c)
        weights = wo_ref[...].astype(f32)
        scaled = ws_ref[0:128, :].astype(f32) + ws_ref[128:256, :].astype(f32)
        near, far = split_two(weights * (inv_c * dot_c / pixel))
        mat = dot_nt(near, ws_ref[0:128, :]) + dot_nt(near, ws_ref[128:256, :])
        mat = mat + dot_nt(far, ws_ref[0:128, :])
        high, low = split_two(mat)
        mm[:, 0:128] = high
        mm[:, 128:256] = low
        kappa = row_of_sums(scaled * (total_c / pixel))[0:1, :]
        mean_act = jnp.transpose(jnp.broadcast_to(st3[8:9, :] / pixels, (8, 128)))[:, 0:1]
        kappa = kappa - total_row(mean_act * mat)
        p_sum = jnp.where(info[1] == 0, kept_ref[...], other_ref[...])
        q_sum = jnp.where(info[1] == 0, other_ref[...], kept_ref[...])
        total_b = st4[8:9, :] - kappa * st3[9:10, :] - total_row(mat * p_sum)
        dot_b = st4[9:10, :] - kappa * st3[10:11, :] - total_row(mat * q_sum)
        scale_b = gb[...] * inv_b
        scale_a = ga[...] * inv_a
        coef[0:1, :] = kappa
        coef[1:2, :] = scale_b
        coef[2:3, :] = scale_b * inv_b * dot_b / pixels
        coef[3:4, :] = scale_b * (total_b - mean_b * inv_b * dot_b) / pixels
        coef[4:5, :] = scale_a
        coef[5:6, :] = sa[...] - mean_a * scale_a
        small_ref[...] = jnp.zeros_like(small_ref)
        put_wide(small_ref, 0, total_c)
        put_wide(small_ref, 4, dot_c)
        small_ref[8:9, :] = total_b
        small_ref[9:10, :] = dot_b
        column = jnp.transpose(gram_ref[128:136, :])[:, 0:1]
        product = dot_halves(gram_ref[0:128, :], wo_ref[...])
        grad = u_ref[...] - column * (total_c / pixel) - (product - column * mean_c) * (
            inv_c * dot_c / pixel
        )
        grad = grad * (gc[...] * inv_c)
        for i in range(4):
            packed[1152 + i * 128 : 1280 + i * 128, :] = grad[:, i * 128 : (i + 1) * 128]
        paired_weights(wt_ref, wide_w)
        dacc[...] = jnp.zeros_like(dacc)
        vacc[...] = jnp.zeros_like(vacc)
        sums[...] = jnp.zeros_like(sums)
        clear_frame(frame)
        place = (1 - info[1]) * (frame.shape[0] - 1)
        for c, n in groups(columns):
            act = ye_ref[c : c + n, :, 0:128].reshape(n * images, 128)
            extra = dot(act, mm[...]).reshape(n, images, 256)
            frame[place, 1 + c : 1 + c + n] = second_back(
                te_ref[c : c + n], extra, ye_ref[c : c + n, :, 128:256], ze_ref[c : c + n]
            )

    @pl.when(step < last)
    def _():
        for r in range(2):
            act = y_ref[r].reshape(area, 128)
            extra = dot(act, mm[...]).reshape(columns, images, 256)
            for c, n in groups(columns):
                frame[2 * step + 1 + r, 1 + c : 1 + c + n] = second_back(
                    t_ref[r, c : c + n],
                    extra[c : c + n],
                    s_ref[r, c : c + n],
                    z2_ref[r, c : c + n],
                )

    @pl.when(step > 0)
    def _():
        scale_a, bias_a = coef[4:5, :], coef[5:6, :]
        near = window(frame, step - 1)
        through = dot(near, wide_w[...])
        act = jnp.concatenate([a_ref[r].reshape(area, 128) for r in range(2)], axis=1)
        dacc[...] += dot_tn(act, near)
        total = jnp.zeros((8, 128), f32)
        dots = jnp.zeros((8, 128), f32)
        for r in range(2):
            part = through[:, r * 128 : (r + 1) * 128].reshape(columns, images, 128)
            for c, n in groups(columns):
                z = z1_ref[r, c : c + n]
                slope = gelu_terms(z * scale_a + bias_a)[1]
                grad = jnp.where(mask, part[c : c + n] * slope, 0.0)
                total += fold8(grad)
                dots += fold8(grad * z)
                h_ref[r, c : c + n] = grad.astype(bf16)
        sums[0] += total
        sums[1] += dots
        vacc[...] += dot_tn(h_ref[...].reshape(2 * area, 128), x_ref[...].reshape(2 * area, 512))

    @pl.when(step == last)
    def _():
        pixels = st1[2:3, :]
        total_h, dot_h = total_row(sums[0]), total_row(sums[1])
        tail = jnp.concatenate(
            [total_h, dot_h, st1[0:1, :] / pixels, jnp.zeros((5, 128), f32)], axis=0
        )
        columns2 = jnp.transpose(tail)
        column_h, mean_a = columns2[:, 0:1], columns2[:, 2:3]
        for i in range(4):
            lanes = slice(i * 128, (i + 1) * 128)
            center = st4[10 + i : 11 + i, :] / pixels
            packed[1664 + i * 128 : 1792 + i * 128, :] = vacc[:, lanes] - column_h * center
            packed[2176 + i * 128 : 2304 + i * 128, :] = (
                xz_ref[lanes, :] - mean_a * own4[10 + i : 11 + i, :]
            )
        for t in range(3):
            for u in range(3):
                parts = []
                for o in range(2):
                    base = ((o + 2 - t) * 3 + 2 - u) * 128
                    parts.append(dacc[o * 128 : (o + 1) * 128, base : base + 128])
                packed[(t * 3 + u) * 128 : (t * 3 + u + 1) * 128, :] = parts[0] + parts[1]
        if packed.shape[0] > 2688:
            packed[2688:, :] = jnp.zeros((packed.shape[0] - 2688, 128), f32)
        half = packed.shape[0] // 2
        low = info[1] == 0
        mine_ref[0:half, :] = jnp.where(low, packed[0:half, :], packed[half:, :])
        sent_ref[0:half, :] = jnp.where(low, packed[half:, :], packed[0:half, :])
        mine_ref[half : half + 8, :] = tail
        sent_ref[half : half + 8, :] = tail


def pack_body(mine_ref, arrived_ref, out_ref):
    shares, block = out_ref.shape[:2]
    share = (mine_ref.shape[0] - 8) // shares
    small = mine_ref[shares * share :, :] + arrived_ref[shares * share :, :]
    high = small.astype(bf16).astype(f32)
    middle = (small - high).astype(bf16).astype(f32)
    low = small - high - middle
    tail = jnp.concatenate(
        [high[0:2], middle[0:2], low[0:2], jnp.zeros((block - share - 6, 128), f32)], axis=0
    )
    for k in range(shares):
        rows = slice(k * share, (k + 1) * share)
        total = mine_ref[rows, :] + arrived_ref[rows, :]
        out_ref[k] = jnp.concatenate([total, tail], axis=0).astype(bf16)


def share_body(share, in_ref, small_ref, out_ref):
    total = in_ref[0].astype(f32)
    for k in range(1, in_ref.shape[0]):
        total = total + in_ref[k].astype(f32)
    sums = total[share : share + 2] + total[share + 2 : share + 4] + total[share + 4 : share + 6]
    small_ref[...] = jnp.concatenate([sums, jnp.zeros((6, 128), f32)], axis=0)
    for k in range(out_ref.shape[0]):
        out_ref[k] = total.astype(bf16)


def input_body(info, st1, st5, ga, wi_ref, h_ref, z_ref, e_ref, g_ref, coef, w_turn):
    step = pl.program_id(0)
    tall, columns, images = z_ref.shape[:3]
    area = columns * images

    @pl.when(step == 0)
    def _():
        pixels = st1[2:3, :]
        mean, inv = moments(st1[0:1, :], st1[1:2, :], pixels)
        scale = ga[...] * inv
        w_turn[...] = jnp.transpose(wi_ref[...])
        total = st5[0:1, :]
        dot_a = inv * (st5[1:2, :] - mean * total)
        coef[0:1, :] = scale
        coef[1:2, :] = scale * inv * dot_a / pixels
        coef[2:3, :] = scale * (total - mean * inv * dot_a) / pixels

    mask = live(info, images, 128)
    scale, beta, alpha = (coef[i : i + 1, :] for i in range(3))
    for r in range(tall):
        parts = []
        for c, n in groups(columns):
            grad = scale * h_ref[r, c : c + n].astype(f32) - (alpha + beta * z_ref[r, c : c + n])
            parts.append(jnp.where(mask, grad, 0.0).astype(bf16).reshape(n * images, 128))
        through = dot(jnp.concatenate(parts, axis=0), w_turn[...])
        through = through.reshape(columns, images, 512)
        for c in range(columns):
            g_ref[r, c] = (through[c] + e_ref[r, c].astype(f32)).astype(bf16)


def final_body(
    share, info, st1, st5, ga, small_ref, mine_ref, other_ref,
    gwi_ref, gga_ref, gsa_ref, gwm_ref, ggb_ref, gsb_ref, gwo_ref, ggc_ref, gsc_ref, total_ref,
):
    shares = mine_ref.shape[0]
    for k in range(shares):
        mine, other = mine_ref[k].astype(f32), other_ref[k].astype(f32)
        low = jnp.where(info[1] == 0, mine, other)
        high = jnp.where(info[1] == 0, other, mine)
        total_ref[k * share : (k + 1) * share, :] = low[0:share]
        total_ref[(shares + k) * share : (shares + k + 1) * share, :] = high[0:share]
    pixels = st1[2:3, :]
    mean, inv = moments(st1[0:1, :], st1[1:2, :], pixels)
    total = st5[0:1, :]
    dot = inv * (st5[1:2, :] - mean * total)
    gsa_ref[...] = total
    gga_ref[...] = dot
    gsb_ref[...] = small_ref[8:9, :]
    ggb_ref[...] = small_ref[9:10, :]
    gsc_ref[...] = wide(small_ref, 0)
    ggc_ref[...] = wide(small_ref, 4)
    gwm_ref[...] = total_ref[0:1152, :]
    for i in range(4):
        gwo_ref[:, i * 128 : (i + 1) * 128] = total_ref[1152 + i * 128 : 1280 + i * 128, :]
        v = jnp.transpose(total_ref[1664 + i * 128 : 1792 + i * 128, :])
        xz = jnp.transpose(total_ref[2176 + i * 128 : 2304 + i * 128, :])
        gwi_ref[i * 128 : (i + 1) * 128, :] = (ga[...] * inv) * (v - xz * (inv * dot / pixels))


def local(
    images, counts, w_in, gain_a, shift_a, w_mid, gain_b, shift_b, w_out, gain_c, shift_c, cotangent
):
    count, rows, columns, channels = images.shape
    steps = rows // 2
    info = jnp.stack([counts[0], lax.axis_index("rows").astype(jnp.int32)])
    images = jnp.transpose(images, (1, 2, 0, 3))
    cotangent = jnp.transpose(cotangent, (1, 2, 0, 3))
    ga, sa, gb, sb = (v.reshape(1, 128) for v in (gain_a, shift_a, gain_b, shift_b))
    gc, sc = gain_c.reshape(1, 512), shift_c.reshape(1, 512)
    small = whole_spec((1, 128))
    large = whole_spec((1, 512))
    eight = whole_spec((8, 128))
    taps = whole_spec((3, 3, 128, 128))

    def tile(lanes):
        return (2, columns, count, lanes)

    def edge(lanes):
        return (columns, count, lanes)

    def ahead(i):
        return jnp.minimum(i, steps - 1)

    def behind(i):
        return jnp.maximum(i - 1, 0)

    def frame_like():
        return pltpu.VMEM((rows + 2, columns + 2, count, 128), bf16)

    pixels = count * rows * columns

    z1, z1_edge, st1 = call(
        first_body,
        steps,
        [SMEM, step_spec(tile(512)), whole_spec((512, 128))],
        [
            step_out(rows, tile(128), f32),
            whole_out(edge(128)),
            whole_out((8, 128)),
        ],
        [pltpu.VMEM((2, 8, 128), f32)],
        "first_norm_sums",
        pixels * 512 * 128 * 2,
        pixels * 1536,
    )(info, images, w_in)
    z1_edge = partner(z1_edge, 1)
    st1 = summed_at_once(st1)
    xz = call(
        cross_body,
        steps,
        [step_spec(tile(512)), step_spec(tile(128))],
        [whole_out((512, 128))],
        [pltpu.VMEM((128, 512), f32)],
        "input_cross",
        pixels * 512 * 128 * 2,
        pixels * 1536,
    )(images, z1)[0]

    everyone = [list(range(lax.axis_size("batch")))]
    z2, act_a, st2 = call(
        middle_body,
        steps + 1,
        [
            SMEM, eight, small, small, step_spec(tile(128), ahead), whole_spec(edge(128)), taps,
            whole_spec((512, 128)),
        ],
        [
            step_out(rows, tile(128), f32, behind),
            step_out(rows, tile(128), bf16, ahead),
            whole_out((8, 128)),
        ],
        [
            frame_like(),
            pltpu.VMEM((1536, 256), bf16),
            pltpu.VMEM((8, 128), f32),
            pltpu.VMEM((2, 8, 128), f32),
        ],
        "middle_conv",
        pixels * 12 * 128 * 128 * 2,
        pixels * 1280,
    )(info, st1, ga, sa, z1, z1_edge, w_mid, xz)
    st2 = summed_by_swap(st2)

    act_b, slope_b, dotted_b, y_edge, z2_edge, st3, gram = call(
        second_body,
        steps,
        [SMEM, eight, eight, small, small, step_spec(tile(128)), whole_spec((128, 512))],
        [
            step_out(rows, tile(128), bf16),
            step_out(rows, tile(128), bf16),
            step_out(rows, tile(128), bf16),
            whole_out(edge(256), bf16),
            whole_out(edge(128)),
            whole_out((272, 128)),
            whole_out((136, 128)),
        ],
        [pltpu.VMEM((8, 128), f32), pltpu.VMEM((128, 384), f32), pltpu.VMEM((3, 8, 128), f32)],
        "second_norm",
        pixels * 384 * 128 * 2,
        pixels * 1280,
    )(info, st1, st2, gb, sb, z2, w_out)
    on_low = info[1] == 0
    kept = jnp.where(on_low, st3[16:144], st3[144:272])
    sent = jnp.where(on_low, st3[144:272], st3[16:144])
    arrived = partner(jnp.concatenate([st3[:16], sent]), 1)
    st3 = swapped_sum(st3[:16] + arrived[:16], everyone)
    kept = kept + arrived[16:]
    kept = swapped_sum(kept, everyone)
    y_edge = partner(y_edge, 1)
    z2_edge = partner(z2_edge, 1)

    block_out, e, t, t_edge, own4, u_local, w_scaled = call(
        last_body,
        steps,
        [
            SMEM, eight, whole_spec((16, 128)), large, large, step_spec(tile(128)),
            step_spec(tile(128)), step_spec(tile(128)), step_spec(tile(512)),
            step_spec(tile(512)), whole_spec((128, 512)),
        ],
        [
            step_out(rows, tile(512), bf16),
            step_out(rows, tile(512), bf16),
            step_out(rows, tile(128), f32),
            whole_out(edge(128)),
            whole_out((16, 128)),
            whole_out((128, 512)),
            whole_out((256, 512), bf16),
        ],
        [
            pltpu.VMEM((8, 512), f32),
            pltpu.VMEM((256, 512), bf16),
            pltpu.VMEM((512, 256), bf16),
            pltpu.VMEM(tile(512), f32),
            pltpu.VMEM((128, 512), f32),
            pltpu.VMEM((2, 8, 512), f32),
            pltpu.VMEM((2, 8, 128), f32),
        ],
        "last_norm",
        pixels * 512 * 128 * 10,
        pixels * 4864,
    )(info, st1, st3, gc, sc, act_b, slope_b, dotted_b, images, cotangent, w_out)

    own4, kept = lax.optimization_barrier((own4, kept))
    st4 = swapped_sum(own4 + partner(own4, 1), everyone)
    other = partner(kept, 1)
    t_edge = partner(t_edge, 1)

    w_back = jnp.swapaxes(w_mid[::-1, ::-1], 2, 3)
    shares = lax.axis_size("batch")
    share = -(-1344 // (8 * shares)) * 8
    half = share * shares
    block = -(-(share + 6) // 16) * 16
    h, mine, sent, small_sums = call(
        back_body,
        steps + 1,
        [
            SMEM, eight, eight, whole_spec((16, 128)), whole_spec((16, 128)),
            whole_spec((128, 128)), whole_spec((128, 128)), whole_spec((16, 128)),
            whole_spec((512, 128)), whole_spec((136, 128)),
            whole_spec((128, 512)), small, small, small, large, whole_spec((128, 512)),
            whole_spec((256, 512)), taps,
            step_spec(tile(128), ahead), step_spec(tile(128), ahead), whole_spec(edge(256)),
            step_spec(tile(128), ahead), whole_spec(edge(128)),
            step_spec(tile(128), ahead), whole_spec(edge(128)),
            step_spec(tile(128), behind), step_spec(tile(128), behind),
            step_spec(tile(512), behind),
        ],
        [
            step_out(rows, tile(128), bf16, behind),
            whole_out((half + 8, 128)),
            whole_out((half + 8, 128)),
            whole_out((16, 128)),
        ],
        [
            pltpu.VMEM((8, 128), f32),
            pltpu.VMEM((128, 256), bf16),
            pltpu.VMEM((1536, 256), bf16),
            frame_like(),
            pltpu.VMEM((256, 1536), f32),
            pltpu.VMEM((128, 512), f32),
            pltpu.VMEM((2, 8, 128), f32),
            pltpu.VMEM((2 * half, 128), f32),
        ],
        "middle_back",
        pixels * 32 * 128 * 128 * 2,
        pixels * 4000,
    )(
        info, st1, st2, st3, st4, kept, other, own4, xz, gram, u_local, ga, sa, gb, gc,
        w_out, w_scaled, w_back,
        act_b, slope_b, y_edge, z2, z2_edge, t, t_edge, act_a, z1, images,
    )
    arrived = partner(sent, 1)
    spread = call(
        pack_body,
        1,
        [whole_spec((half + 8, 128)), whole_spec((half + 8, 128))],
        [whole_out((shares, block, 128), bf16)],
        [],
        "pack_shares",
        1e6,
        2e6,
    )(mine, arrived)[0]
    spread = lax.all_to_all(spread, "batch", 0, 0, tiled=True)
    st5, spread = call(
        functools.partial(share_body, share),
        1,
        [whole_spec((shares, block, 128))],
        [whole_out((8, 128)), whole_out((shares, block, 128), bf16)],
        [],
        "sum_shares",
        1e6,
        1e6,
    )(spread)
    gathered = lax.all_to_all(spread, "batch", 0, 0, tiled=True)

    grad_images = call(
        input_body,
        steps,
        [
            SMEM, eight, eight, small, whole_spec((512, 128)),
            step_spec(tile(128)), step_spec(tile(128)), step_spec(tile(512)),
        ],
        [step_out(rows, tile(512), bf16)],
        [pltpu.VMEM((8, 128), f32), pltpu.VMEM((128, 512), bf16)],
        "input_grad",
        pixels * 512 * 128 * 2,
        pixels * 2816,
    )(info, st1, st5, ga, w_in, h, z1, e)[0]

    gathered, grad_images = lax.optimization_barrier((gathered, grad_images))
    shared = whole_spec((shares, block, 128))
    gwi, gga, gsa, gwm, ggb, gsb, gwo, ggc, gsc = call(
        functools.partial(final_body, share),
        1,
        [SMEM, eight, eight, small, whole_spec((16, 128)), shared, shared],
        [
            whole_out((512, 128)), whole_out((1, 128)), whole_out((1, 128)),
            whole_out((1152, 128)), whole_out((1, 128)), whole_out((1, 128)),
            whole_out((128, 512)), whole_out((1, 512)), whole_out((1, 512)),
        ],
        [pltpu.VMEM((2 * half, 128), f32)],
        "replicated_grads",
        1e6,
        3e6,
    )(info, st1, st5, ga, small_sums, gathered, partner(gathered, 1))
    return (
        jnp.transpose(block_out, (2, 0, 1, 3)),
        jnp.transpose(grad_images, (2, 0, 1, 3)),
        gwi,
        gga.reshape(128),
        gsa.reshape(128),
        gwm.reshape(3, 3, 128, 128),
        ggb.reshape(128),
        gsb.reshape(128),
        gwo,
        ggc.reshape(512),
        gsc.reshape(512),
    )


def solution(mesh):
    split = P("batch", "rows", None, None)
    placed = (split, P("batch"), P(), P(), P(), P(), P(), P(), P(), P(), P(), split)
    return jax.shard_map(
        local,
        mesh=mesh,
        in_specs=placed,
        out_specs=(split, split) + (P(),) * 9,
        check_vma=False,
    )
```

```python
import functools
import math

import jax
import jax.numpy as jnp
from jax import lax
from jax.experimental import pallas as pl
from jax.experimental.pallas import tpu as pltpu
from jax.sharding import PartitionSpec as P

epsilon = 1e-05
axes = ("batch", "rows")
f32 = jnp.float32
bf16 = jnp.bfloat16
C0 = math.sqrt(2.0 / math.pi)
C1 = C0 * 0.044715
HIGH = lax.Precision.HIGHEST


def partner(block, mask):
    total = lax.axis_size("batch") * lax.axis_size("rows")
    return lax.ppermute(block, axes, [(i, i ^ mask) for i in range(total)])


def swapped_sum(block, groups):
    size = len(groups[0])
    spread = jnp.broadcast_to(block[None], (size,) + block.shape)
    arrived = lax.all_to_all(spread, "batch", 0, 0, axis_index_groups=groups, tiled=True)
    return jnp.sum(arrived, axis=0)


def summed_at_once(block):
    total = lax.axis_size("batch") * lax.axis_size("rows")
    spread = jnp.broadcast_to(block[None], (total,) + block.shape)
    return jnp.sum(lax.all_to_all(spread, axes, 0, 0, tiled=True), axis=0)


def summed_by_swap(block, near=None):
    block = block + partner(block, 1)
    count = lax.axis_size("batch")
    if near is None or count % near:
        return swapped_sum(block, [list(range(count))])
    block = swapped_sum(block, [list(range(i, i + near)) for i in range(0, count, near)])
    return swapped_sum(block, [list(range(i, count, near)) for i in range(near)])


def gelu_terms(u):
    square = u * u
    inner = C0 + C1 * square
    half = 0.5 * jnp.tanh(u * inner) + 0.5
    value = u * half
    slope = half + value * (1.0 - half) * (6.0 * inner - 4.0 * C0)
    return value, slope


def gelu_value(u):
    return u * (0.5 * jnp.tanh(u * (C0 + C1 * u * u)) + 0.5)


def moments(total, squares, pixels):
    mean = total / pixels
    return mean, lax.rsqrt(squares / pixels - mean * mean + epsilon)


def fold8(values):
    lanes = values.shape[-1]
    return jnp.sum(values.reshape(values.size // (8 * lanes), 8, lanes), axis=0)


def total_row(values):
    return jnp.sum(values, axis=0, keepdims=True)


def wide(ref, start):
    return jnp.concatenate([ref[start + i : start + i + 1, :] for i in range(4)], axis=1)


def put_wide(ref, start, row):
    for i in range(4):
        ref[start + i : start + i + 1, :] = row[:, i * 128 : (i + 1) * 128]


def dot_tn(a, b):
    return lax.dot_general(a, b, (((0,), (0,)), ((), ())), preferred_element_type=f32)


def dot_nt(a, b, precision=None):
    return lax.dot_general(
        a, b, (((1,), (1,)), ((), ())), preferred_element_type=f32, precision=precision
    )


def dot(a, b, precision=None):
    return jnp.dot(a, b, preferred_element_type=f32, precision=precision)


def split_two(values):
    high = values.astype(bf16)
    return high, (values - high.astype(f32)).astype(bf16)


def dot_halves(a, b):
    high, low = split_two(a)
    return dot(high, b) + dot(low, b)


def row_of_sums(values):
    high, low = split_two(values)
    one = jnp.ones((16, values.shape[1]), bf16)
    return (dot_nt(one, high) + dot_nt(one, low))[0:8, :]


def call(body, grid, ins, outs, scratch, name, flops, bytes_moved, aliases=None):
    return pl.pallas_call(
        body,
        grid=(grid,),
        in_specs=ins,
        out_specs=[spec for spec, _ in outs],
        out_shape=[shape for _, shape in outs],
        scratch_shapes=scratch,
        name=name,
        input_output_aliases=aliases or {},
        compiler_params=pltpu.CompilerParams(
            dimension_semantics=("arbitrary",), vmem_limit_bytes=52 << 20
        ),
        cost_estimate=pl.CostEstimate(
            flops=int(flops), bytes_accessed=int(bytes_moved), transcendentals=0
        ),
    )


SMEM = pl.BlockSpec(memory_space=pltpu.SMEM)
ANY = pl.BlockSpec(memory_space=pl.ANY)


def whole_spec(shape):
    return pl.BlockSpec(tuple(shape), lambda i: (0,) * len(shape))


def step_spec(shape, place=lambda i: i):
    return pl.BlockSpec(tuple(shape), lambda i: (place(i),) + (0,) * (len(shape) - 1))


def whole_out(shape, dtype=f32):
    return (whole_spec(shape), jax.ShapeDtypeStruct(shape, dtype))


def step_out(count, shape, dtype, place=lambda i: i):
    return (
        step_spec(shape, place),
        jax.ShapeDtypeStruct((count,) + tuple(shape[1:]), dtype),
    )


def live(info, images, lanes):
    return lax.broadcasted_iota(jnp.int32, (images, lanes), 0) < info[0]


def groups(columns):
    return [(c, min(4, columns - c)) for c in range(0, columns, 4)]


def take_edge(info, edge_ref, ref):
    step = pl.program_id(0)

    @pl.when((step == 0) & (info[1] == 1))
    def _():
        edge_ref[...] = ref[0].astype(edge_ref.dtype)

    @pl.when((step == pl.num_programs(0) - 1) & (info[1] == 0))
    def _():
        edge_ref[...] = ref[ref.shape[0] - 1].astype(edge_ref.dtype)


def first_body(info, x_ref, w_ref, z_ref, edge_ref, stat_ref, zacc):
    step = pl.program_id(0)
    tall, columns, images = x_ref.shape[:3]
    area = columns * images

    @pl.when(step == 0)
    def _():
        zacc[...] = jnp.zeros_like(zacc)

    mask = live(info, images, 128)
    for r in range(tall):
        x = x_ref[r].reshape(area, 512)
        z = dot(x, w_ref[...]).reshape(columns, images, 128)
        z = jnp.where(mask, z, 0.0)
        z_ref[r] = z
        zacc[0] += fold8(z)
        zacc[1] += fold8(z * z)
    take_edge(info, edge_ref, z_ref)

    @pl.when(step == pl.num_programs(0) - 1)
    def _():
        pixels = (info[0] * (pl.num_programs(0) * tall * columns)).astype(f32)
        stat_ref[...] = jnp.zeros_like(stat_ref)
        stat_ref[0:1, :] = total_row(zacc[0])
        stat_ref[1:2, :] = total_row(zacc[1])
        stat_ref[2:3, :] = jnp.full((1, 128), pixels, f32)


def cross_body(x_ref, z_ref, xz_ref, acc):
    step = pl.program_id(0)
    tall, columns, images = x_ref.shape[:3]
    area = columns * images

    @pl.when(step == 0)
    def _():
        acc[...] = jnp.zeros_like(acc)

    for r in range(tall):
        z = z_ref[r].astype(bf16).reshape(area, 128)
        acc[...] += dot_tn(z, x_ref[r].reshape(area, 512))

    @pl.when(step == pl.num_programs(0) - 1)
    def _():
        for i in range(4):
            xz_ref[i * 128 : (i + 1) * 128, :] = acc[:, i * 128 : (i + 1) * 128]


def paired_weights(w_ref, target):
    for r in range(4):
        for u in range(3):
            for o in range(2):
                t = r - o
                base = (r * 3 + u) * 128
                if 0 <= t <= 2:
                    block = w_ref[t, u]
                else:
                    block = jnp.zeros((128, 128), bf16)
                target[base : base + 128, o * 128 : (o + 1) * 128] = block


def window(frame, pair):
    columns, images = frame.shape[1] - 2, frame.shape[2]
    parts = [
        frame[2 * pair + r, u : u + columns].reshape(columns * images, 128)
        for r in range(4)
        for u in range(3)
    ]
    return jnp.concatenate(parts, axis=1)


def clear_frame(frame):
    tall, wide_columns = frame.shape[:2]
    zero = jnp.zeros(frame.shape[2:], frame.dtype)
    for e in range(tall):
        frame[e, 0] = zero
        frame[e, wide_columns - 1] = zero
    for c in range(wide_columns):
        frame[0, c] = zero
        frame[tall - 1, c] = zero


def middle_body(
    info, st1, ga, sa, z_ref, edge_ref, w_ref, xz_ref,
    z2_ref, a_ref, stat_ref, frame, wide_w, coef, zacc,
):
    step = pl.program_id(0)
    last = pl.num_programs(0) - 1
    columns, images = z_ref.shape[1:3]
    area = columns * images

    def activated(z):
        return gelu_value(z * coef[0:1, :] + coef[1:2, :]).astype(bf16)

    @pl.when(step == 0)
    def _():
        mean, inv = moments(st1[0:1, :], st1[1:2, :], st1[2:3, :])
        scale = ga[...] * inv
        coef[0:1, :] = scale
        coef[1:2, :] = sa[...] - mean * scale
        paired_weights(w_ref, wide_w)
        zacc[...] = jnp.zeros_like(zacc)
        clear_frame(frame)
        place = (1 - info[1]) * (frame.shape[0] - 1)
        for c, n in groups(columns):
            frame[place, 1 + c : 1 + c + n] = activated(edge_ref[c : c + n])

    @pl.when(step < last)
    def _():
        for r in range(2):
            for c, n in groups(columns):
                value = activated(z_ref[r, c : c + n])
                frame[2 * step + 1 + r, 1 + c : 1 + c + n] = value
                a_ref[r, c : c + n] = value

    @pl.when(step > 0)
    def _():
        mask = live(info, images, 128)
        y = dot(window(frame, step - 1), wide_w[...])
        for r in range(2):
            z = y[:, r * 128 : (r + 1) * 128].reshape(columns, images, 128)
            z2_ref[r] = z
            z = jnp.where(mask, z, 0.0)
            zacc[0] += fold8(z)
            zacc[1] += fold8(z * z)

    @pl.when(step == last)
    def _():
        stat_ref[...] = jnp.zeros_like(stat_ref)
        for k in range(2):
            stat_ref[k : k + 1, :] = total_row(zacc[k])


def second_coef(st1, st2, gb, sb, coef):
    mean, inv = moments(st2[0:1, :], st2[1:2, :], st1[2:3, :])
    scale = gb[...] * inv
    coef[0:1, :] = scale
    coef[1:2, :] = sb[...] - mean * scale
    coef[2:3, :] = inv
    coef[3:4, :] = -mean * inv


def second_body(
    info, st1, st2, gb, sb, z_ref, wo_ref,
    act_ref, g_ref, gx_ref, ye_ref, ze_ref, st_ref, keep_ref, gram_ref, coef, cross, sums,
):
    step = pl.program_id(0)
    tall, columns, images = z_ref.shape[:3]
    area = columns * images

    @pl.when(step == 0)
    def _():
        second_coef(st1, st2, gb, sb, coef)
        cross[...] = jnp.zeros_like(cross)
        sums[...] = jnp.zeros_like(sums)

    mask = live(info, images, 128)
    scale, bias, inv, shift = (coef[i : i + 1, :] for i in range(4))
    edge_row = (1 - info[1]) * (tall - 1)
    at_edge = step == (1 - info[1]) * (pl.num_programs(0) - 1)
    totals = [jnp.zeros((8, 128), f32) for _ in range(3)]
    for r in range(tall):
        acts, others = [], []
        for c, n in groups(columns):
            z = z_ref[r, c : c + n]
            value, slope = gelu_terms(z * scale + bias)
            dotted = jnp.where(mask, slope * (z * inv + shift), 0.0).astype(bf16)
            slope = jnp.where(mask, slope, 0.0).astype(bf16)
            g_ref[r, c : c + n] = slope
            gx_ref[r, c : c + n] = dotted
            value = value.astype(bf16)
            act_ref[r, c : c + n] = value
            value = jnp.where(mask, value, jnp.zeros((), bf16))
            acts.append(value.reshape(n * images, 128))
            for k, part in enumerate((slope, dotted, value)):
                totals[k] += fold8(part.astype(f32))
        acts = jnp.concatenate(acts, axis=0)
        cross[...] += dot_tn(
            acts,
            jnp.concatenate(
                [acts, g_ref[r].reshape(area, 128), gx_ref[r].reshape(area, 128)], axis=1
            ),
        )

        @pl.when(at_edge & (edge_row == r))
        def _():
            ye_ref[:, :, 0:128] = act_ref[r]
            ye_ref[:, :, 128:256] = g_ref[r]
            ze_ref[...] = z_ref[r]

    for k in range(3):
        sums[k] += totals[k]

    @pl.when(step == pl.num_programs(0) - 1)
    def _():
        gram = cross[:, 0:128]
        gram_ref[0:128, :] = gram
        st_ref[8:16, :] = jnp.zeros((8, 128), f32)
        st_ref[8:9, :] = total_row(sums[2])
        gram_ref[128:136, :] = st_ref[8:16, :]
        spread = dot_halves(gram_ref[...], wo_ref[...])
        put_wide(st_ref, 0, spread[128:129, :])
        put_wide(st_ref, 4, total_row(spread[0:128, :] * wo_ref[...].astype(f32)))
        st_ref[9:16, :] = jnp.zeros((7, 128), f32)
        for k in range(2):
            st_ref[9 + k : 10 + k, :] = total_row(sums[k])
        low = info[1] == 0
        keep_ref[...] = jnp.where(low, cross[:, 128:256], cross[:, 256:384])
        st_ref[16:144, :] = jnp.where(low, cross[:, 256:384], cross[:, 128:256])


def last_body(
    info, st1, st3, gc, sc, y_ref, g_ref, gx_ref, x_ref, cot_ref, wo_ref,
    out_ref, e_ref, t_ref, te_ref, st_ref, u_ref, ws_ref,
    coef, w_two, w_turn, z_buf, cross, sums, sums_b,
):
    step = pl.program_id(0)
    tall, columns, images = x_ref.shape[:3]
    area = columns * images

    @pl.when(step == 0)
    def _():
        mean, inv = moments(wide(st3, 0), wide(st3, 4), st1[2:3, 0:1])
        scale = gc[...] * inv
        coef[0:1, :] = sc[...] - mean * scale
        high, low = split_two(wo_ref[...].astype(f32) * scale)
        w_two[0:128, :] = high
        w_two[128:256, :] = low
        ws_ref[...] = w_two[...]
        w_turn[:, 0:128] = jnp.transpose(w_two[0:128, :])
        w_turn[:, 128:256] = jnp.transpose(w_two[128:256, :])
        cross[...] = jnp.zeros_like(cross)
        sums[...] = jnp.zeros_like(sums)
        sums_b[...] = jnp.zeros_like(sums_b)

    mask = live(info, images, 512)
    bias = coef[0:1, :]
    zero = jnp.zeros((), bf16)
    piece = columns // 4
    parts = [(r, c) for r in range(tall) for c in range(0, columns, piece)]
    n = piece * images

    def product(r, c):
        act = y_ref[r, c : c + piece].reshape(n, 128)
        z = dot(jnp.concatenate([act, act], axis=1), w_two[...])
        z_buf[r, c : c + piece] = z.reshape(piece, images, 512)

    def pointwise(r, c):
        x = jnp.where(mask, x_ref[r, c], zero).astype(f32)
        value, slope = gelu_terms(z_buf[r, c] + (bias + x))
        out_ref[r, c] = value.astype(bf16)
        cot = jnp.where(mask, cot_ref[r, c], zero).astype(f32)
        e = slope * cot
        e_ref[r, c] = e.astype(bf16)
        return fold8(e), fold8(x)

    def collect(r, c):
        e = e_ref[r, c : c + piece].reshape(n, 512)
        cross[...] += dot_tn(y_ref[r, c : c + piece].reshape(n, 128), e)

    def through(r, c):
        y = dot(e_ref[r, c : c + piece].reshape(n, 512), w_turn[...])
        t = (y[:, 0:128] + y[:, 128:256]).reshape(piece, images, 128)
        t_ref[r, c : c + piece] = t
        sums_b[0] += fold8(t * g_ref[r, c : c + piece].astype(f32))
        sums_b[1] += fold8(t * gx_ref[r, c : c + piece].astype(f32))

    product(*parts[0])
    for k in range(len(parts) + 1):
        work = []
        if k + 1 < len(parts):
            work.append(functools.partial(product, *parts[k + 1]))
        if k > 0:
            work.append(functools.partial(through, *parts[k - 1]))
            work.append(functools.partial(collect, *parts[k - 1]))
        if k < len(parts):
            r, first = parts[k]
            total_e = jnp.zeros((8, 512), f32)
            total_x = jnp.zeros((8, 512), f32)
            for c in range(piece):
                if c % 2 == 0 and work:
                    work.pop(0)()
                add_e, add_x = pointwise(r, first + c)
                total_e += add_e
                total_x += add_x
            sums[0] += total_e
            sums[1] += total_x
        for rest in work:
            rest()
    take_edge(info, te_ref, t_ref)

    @pl.when(step == pl.num_programs(0) - 1)
    def _():
        u_ref[...] = cross[...]
        put_wide(st_ref, 0, total_row(sums[0]))
        put_wide(st_ref, 4, total_row(wo_ref[...].astype(f32) * cross[...]))
        put_wide(st_ref, 10, total_row(sums[1]))
        for k in range(2):
            st_ref[8 + k : 9 + k, :] = total_row(sums_b[k])
            st_ref[14 + k : 15 + k, :] = jnp.zeros((1, 128), f32)


def back_body(
    info, st1, st2, st3, st4, kept_ref, other_ref, own4, xz_ref, gram_ref, u_ref, ga, sa, gb, gc, wo_ref, ws_ref, wt_ref,
    y_ref, s_ref, ye_ref, z2_ref, ze_ref, t_ref, te_ref, a_ref, z1_ref, x_ref,
    h_ref, mine_ref, sent_ref, small_ref,
    coef, mm, wide_w, frame, dacc, vacc, sums, packed,
):
    step = pl.program_id(0)
    last = pl.num_programs(0) - 1
    columns, images = z1_ref.shape[1:3]
    area = columns * images
    mask = live(info, images, 128)

    def second_back(t, product, slope, z):
        kappa, scale_b, beta, alpha = (coef[i : i + 1, :] for i in range(4))
        through = t - kappa - product[..., 0:128] - product[..., 128:256]
        grad = scale_b * (slope.astype(f32) * through) - (alpha + beta * z)
        return jnp.where(mask, grad, 0.0).astype(bf16)

    @pl.when(step == 0)
    def _():
        pixels = st1[2:3, :]
        pixel = st1[2:3, 0:1]
        mean_a, inv_a = moments(st1[0:1, :], st1[1:2, :], pixels)
        mean_b, inv_b = moments(st2[0:1, :], st2[1:2, :], pixels)
        mean_c, inv_c = moments(wide(st3, 0), wide(st3, 4), pixel)
        total_c = wide(st4, 0)
        dot_c = inv_c * (wide(st4, 4) - mean_c * total_c)
        weights = wo_ref[...].astype(f32)
        scaled = ws_ref[0:128, :].astype(f32) + ws_ref[128:256, :].astype(f32)
        near, far = split_two(weights * (inv_c * dot_c / pixel))
        mat = dot_nt(near, ws_ref[0:128, :]) + dot_nt(near, ws_ref[128:256, :])
        mat = mat + dot_nt(far, ws_ref[0:128, :])
        high, low = split_two(mat)
        mm[:, 0:128] = high
        mm[:, 128:256] = low
        kappa = row_of_sums(scaled * (total_c / pixel))[0:1, :]
        mean_act = jnp.transpose(jnp.broadcast_to(st3[8:9, :] / pixels, (8, 128)))[:, 0:1]
        kappa = kappa - total_row(mean_act * mat)
        p_sum = jnp.where(info[1] == 0, kept_ref[...], other_ref[16:144, :])
        q_sum = jnp.where(info[1] == 0, other_ref[16:144, :], kept_ref[...])
        total_b = st4[8:9, :] - kappa * st3[9:10, :] - total_row(mat * p_sum)
        dot_b = st4[9:10, :] - kappa * st3[10:11, :] - total_row(mat * q_sum)
        scale_b = gb[...] * inv_b
        scale_a = ga[...] * inv_a
        coef[0:1, :] = kappa
        coef[1:2, :] = scale_b
        coef[2:3, :] = scale_b * inv_b * dot_b / pixels
        coef[3:4, :] = scale_b * (total_b - mean_b * inv_b * dot_b) / pixels
        coef[4:5, :] = scale_a
        coef[5:6, :] = sa[...] - mean_a * scale_a
        small_ref[...] = jnp.zeros_like(small_ref)
        put_wide(small_ref, 0, total_c)
        put_wide(small_ref, 4, dot_c)
        small_ref[8:9, :] = total_b
        small_ref[9:10, :] = dot_b
        column = jnp.transpose(gram_ref[128:136, :])[:, 0:1]
        product = dot_halves(gram_ref[0:128, :], wo_ref[...])
        grad = u_ref[...] - column * (total_c / pixel) - (product - column * mean_c) * (
            inv_c * dot_c / pixel
        )
        grad = grad * (gc[...] * inv_c)
        for i in range(4):
            packed[1152 + i * 128 : 1280 + i * 128, :] = grad[:, i * 128 : (i + 1) * 128]
        paired_weights(wt_ref, wide_w)
        dacc[...] = jnp.zeros_like(dacc)
        vacc[...] = jnp.zeros_like(vacc)
        sums[...] = jnp.zeros_like(sums)
        clear_frame(frame)
        place = (1 - info[1]) * (frame.shape[0] - 1)
        for c, n in groups(columns):
            act = ye_ref[c : c + n, :, 0:128].reshape(n * images, 128)
            extra = dot(act, mm[...]).reshape(n, images, 256)
            frame[place, 1 + c : 1 + c + n] = second_back(
                te_ref[c : c + n], extra, ye_ref[c : c + n, :, 128:256], ze_ref[c : c + n]
            )

    @pl.when(step < last)
    def _():
        for r in range(2):
            act = y_ref[r].reshape(area, 128)
            extra = dot(act, mm[...]).reshape(columns, images, 256)
            for c, n in groups(columns):
                frame[2 * step + 1 + r, 1 + c : 1 + c + n] = second_back(
                    t_ref[r, c : c + n],
                    extra[c : c + n],
                    s_ref[r, c : c + n],
                    z2_ref[r, c : c + n],
                )

    @pl.when(step > 0)
    def _():
        scale_a, bias_a = coef[4:5, :], coef[5:6, :]
        near = window(frame, step - 1)
        through = dot(near, wide_w[...])
        act = jnp.concatenate([a_ref[r].reshape(area, 128) for r in range(2)], axis=1)
        dacc[...] += dot_tn(act, near)
        total = jnp.zeros((8, 128), f32)
        dots = jnp.zeros((8, 128), f32)
        for r in range(2):
            part = through[:, r * 128 : (r + 1) * 128].reshape(columns, images, 128)
            for c, n in groups(columns):
                z = z1_ref[r, c : c + n]
                slope = gelu_terms(z * scale_a + bias_a)[1]
                grad = jnp.where(mask, part[c : c + n] * slope, 0.0)
                total += fold8(grad)
                dots += fold8(grad * z)
                h_ref[r, c : c + n] = grad.astype(bf16)
        sums[0] += total
        sums[1] += dots
        vacc[...] += dot_tn(h_ref[...].reshape(2 * area, 128), x_ref[...].reshape(2 * area, 512))

    @pl.when(step == last)
    def _():
        pixels = st1[2:3, :]
        total_h, dot_h = total_row(sums[0]), total_row(sums[1])
        tail = jnp.concatenate(
            [total_h, dot_h, st1[0:1, :] / pixels, jnp.zeros((5, 128), f32)], axis=0
        )
        columns2 = jnp.transpose(tail)
        column_h, mean_a = columns2[:, 0:1], columns2[:, 2:3]
        for i in range(4):
            lanes = slice(i * 128, (i + 1) * 128)
            center = st4[10 + i : 11 + i, :] / pixels
            packed[1664 + i * 128 : 1792 + i * 128, :] = vacc[:, lanes] - column_h * center
            packed[2176 + i * 128 : 2304 + i * 128, :] = (
                xz_ref[lanes, :] - mean_a * own4[10 + i : 11 + i, :]
            )
        for t in range(3):
            for u in range(3):
                parts = []
                for o in range(2):
                    base = ((o + 2 - t) * 3 + 2 - u) * 128
                    parts.append(dacc[o * 128 : (o + 1) * 128, base : base + 128])
                packed[(t * 3 + u) * 128 : (t * 3 + u + 1) * 128, :] = parts[0] + parts[1]
        if packed.shape[0] > 2688:
            packed[2688:, :] = jnp.zeros((packed.shape[0] - 2688, 128), f32)
        half = packed.shape[0] // 2
        low = info[1] == 0
        mine_ref[0:half, :] = jnp.where(low, packed[0:half, :], packed[half:, :])
        sent_ref[0:half, :] = jnp.where(low, packed[half:, :], packed[0:half, :])
        mine_ref[half : half + 8, :] = tail
        sent_ref[half : half + 8, :] = tail


def pack_body(mine_ref, arrived_ref, out_ref):
    shares, block = out_ref.shape[:2]
    share = (mine_ref.shape[0] - 8) // shares
    small = mine_ref[shares * share :, :] + arrived_ref[shares * share :, :]
    high = small.astype(bf16).astype(f32)
    middle = (small - high).astype(bf16).astype(f32)
    low = small - high - middle
    tail = jnp.concatenate(
        [high[0:2], middle[0:2], low[0:2], jnp.zeros((block - share - 6, 128), f32)], axis=0
    )
    for k in range(shares):
        rows = slice(k * share, (k + 1) * share)
        total = mine_ref[rows, :] + arrived_ref[rows, :]
        out_ref[k] = jnp.concatenate([total, tail], axis=0).astype(bf16)


def share_body(share, in_ref, small_ref, out_ref):
    total = in_ref[0].astype(f32)
    for k in range(1, in_ref.shape[0]):
        total = total + in_ref[k].astype(f32)
    sums = total[share : share + 2] + total[share + 2 : share + 4] + total[share + 4 : share + 6]
    small_ref[...] = jnp.concatenate([sums, jnp.zeros((6, 128), f32)], axis=0)
    for k in range(out_ref.shape[0]):
        out_ref[k] = total.astype(bf16)


def input_body(info, st1, st5, ga, wi_ref, h_ref, z_ref, e_ref, g_ref, coef, w_turn):
    step = pl.program_id(0)
    tall, columns, images = z_ref.shape[:3]
    area = columns * images

    @pl.when(step == 0)
    def _():
        pixels = st1[2:3, :]
        mean, inv = moments(st1[0:1, :], st1[1:2, :], pixels)
        scale = ga[...] * inv
        w_turn[...] = jnp.transpose(wi_ref[...])
        total = st5[0:1, :]
        dot_a = inv * (st5[1:2, :] - mean * total)
        coef[0:1, :] = scale
        coef[1:2, :] = scale * inv * dot_a / pixels
        coef[2:3, :] = scale * (total - mean * inv * dot_a) / pixels

    mask = live(info, images, 128)
    scale, beta, alpha = (coef[i : i + 1, :] for i in range(3))
    for r in range(tall):
        parts = []
        for c, n in groups(columns):
            grad = scale * h_ref[r, c : c + n].astype(f32) - (alpha + beta * z_ref[r, c : c + n])
            parts.append(jnp.where(mask, grad, 0.0).astype(bf16).reshape(n * images, 128))
        through = dot(jnp.concatenate(parts, axis=0), w_turn[...])
        through = through.reshape(columns, images, 512)
        for c in range(columns):
            g_ref[r, c] = (through[c] + e_ref[r, c].astype(f32)).astype(bf16)


def final_body(
    share, info, st1, st5, ga, small_ref, mine_ref, other_ref,
    gwi_ref, gga_ref, gsa_ref, gwm_ref, ggb_ref, gsb_ref, gwo_ref, ggc_ref, gsc_ref, total_ref,
):
    shares = mine_ref.shape[0]
    for k in range(shares):
        mine, other = mine_ref[k].astype(f32), other_ref[k].astype(f32)
        low = jnp.where(info[1] == 0, mine, other)
        high = jnp.where(info[1] == 0, other, mine)
        total_ref[k * share : (k + 1) * share, :] = low[0:share]
        total_ref[(shares + k) * share : (shares + k + 1) * share, :] = high[0:share]
    pixels = st1[2:3, :]
    mean, inv = moments(st1[0:1, :], st1[1:2, :], pixels)
    total = st5[0:1, :]
    dot = inv * (st5[1:2, :] - mean * total)
    gsa_ref[...] = total
    gga_ref[...] = dot
    gsb_ref[...] = small_ref[8:9, :]
    ggb_ref[...] = small_ref[9:10, :]
    gsc_ref[...] = wide(small_ref, 0)
    ggc_ref[...] = wide(small_ref, 4)
    gwm_ref[...] = total_ref[0:1152, :]
    for i in range(4):
        gwo_ref[:, i * 128 : (i + 1) * 128] = total_ref[1152 + i * 128 : 1280 + i * 128, :]
        v = jnp.transpose(total_ref[1664 + i * 128 : 1792 + i * 128, :])
        xz = jnp.transpose(total_ref[2176 + i * 128 : 2304 + i * 128, :])
        gwi_ref[i * 128 : (i + 1) * 128, :] = (ga[...] * inv) * (v - xz * (inv * dot / pixels))


def local(
    images, counts, w_in, gain_a, shift_a, w_mid, gain_b, shift_b, w_out, gain_c, shift_c, cotangent
):
    count, rows, columns, channels = images.shape
    steps = rows // 2
    info = jnp.stack([counts[0], lax.axis_index("rows").astype(jnp.int32)])
    images = jnp.transpose(images, (1, 2, 0, 3))
    cotangent = jnp.transpose(cotangent, (1, 2, 0, 3))
    ga, sa, gb, sb = (v.reshape(1, 128) for v in (gain_a, shift_a, gain_b, shift_b))
    gc, sc = gain_c.reshape(1, 512), shift_c.reshape(1, 512)
    small = whole_spec((1, 128))
    large = whole_spec((1, 512))
    eight = whole_spec((8, 128))
    taps = whole_spec((3, 3, 128, 128))

    def tile(lanes):
        return (2, columns, count, lanes)

    def edge(lanes):
        return (columns, count, lanes)

    def ahead(i):
        return jnp.minimum(i, steps - 1)

    def behind(i):
        return jnp.maximum(i - 1, 0)

    def frame_like():
        return pltpu.VMEM((rows + 2, columns + 2, count, 128), bf16)

    pixels = count * rows * columns

    z1, z1_edge, st1 = call(
        first_body,
        steps,
        [SMEM, step_spec(tile(512)), whole_spec((512, 128))],
        [
            step_out(rows, tile(128), f32),
            whole_out(edge(128)),
            whole_out((8, 128)),
        ],
        [pltpu.VMEM((2, 8, 128), f32)],
        "first_norm_sums",
        pixels * 512 * 128 * 2,
        pixels * 1536,
    )(info, images, w_in)
    z1_edge = partner(z1_edge, 1)
    st1 = summed_at_once(st1)
    xz = call(
        cross_body,
        steps,
        [step_spec(tile(512)), step_spec(tile(128))],
        [whole_out((512, 128))],
        [pltpu.VMEM((128, 512), f32)],
        "input_cross",
        pixels * 512 * 128 * 2,
        pixels * 1536,
    )(images, z1)[0]
    w_back = jnp.swapaxes(w_mid[::-1, ::-1], 2, 3)
    xz, w_back = lax.optimization_barrier((xz, w_back))

    everyone = [list(range(lax.axis_size("batch")))]
    z2, act_a, st2 = call(
        middle_body,
        steps + 1,
        [
            SMEM, eight, small, small, step_spec(tile(128), ahead), whole_spec(edge(128)), taps,
            whole_spec((512, 128)),
        ],
        [
            step_out(rows, tile(128), f32, behind),
            step_out(rows, tile(128), bf16, ahead),
            whole_out((8, 128)),
        ],
        [
            frame_like(),
            pltpu.VMEM((1536, 256), bf16),
            pltpu.VMEM((8, 128), f32),
            pltpu.VMEM((2, 8, 128), f32),
        ],
        "middle_conv",
        pixels * 12 * 128 * 128 * 2,
        pixels * 1280,
    )(info, st1, ga, sa, z1, z1_edge, w_mid, xz)
    st2 = summed_by_swap(st2)

    act_b, slope_b, dotted_b, y_edge, z2_edge, head, kept, gram = call(
        second_body,
        steps,
        [SMEM, eight, eight, small, small, step_spec(tile(128)), whole_spec((128, 512))],
        [
            step_out(rows, tile(128), bf16),
            step_out(rows, tile(128), bf16),
            step_out(rows, tile(128), bf16),
            whole_out(edge(256), bf16),
            whole_out(edge(128)),
            whole_out((144, 128)),
            whole_out((128, 128)),
            whole_out((136, 128)),
        ],
        [pltpu.VMEM((8, 128), f32), pltpu.VMEM((128, 384), f32), pltpu.VMEM((3, 8, 128), f32)],
        "second_norm",
        pixels * 384 * 128 * 2,
        pixels * 1280,
    )(info, st1, st2, gb, sb, z2, w_out)
    arrived = partner(head, 1)
    st3 = swapped_sum(head[:16] + arrived[:16], everyone)
    st3, kept, arrived = lax.optimization_barrier((st3, kept, arrived))
    kept = swapped_sum(kept + arrived[16:], everyone)
    y_edge = partner(y_edge, 1)
    z2_edge = partner(z2_edge, 1)

    block_out, e, t, t_edge, own4, u_local, w_scaled = call(
        last_body,
        steps,
        [
            SMEM, eight, whole_spec((16, 128)), large, large, step_spec(tile(128)),
            step_spec(tile(128)), step_spec(tile(128)), step_spec(tile(512)),
            step_spec(tile(512)), whole_spec((128, 512)),
        ],
        [
            step_out(rows, tile(512), bf16),
            step_out(rows, tile(512), bf16),
            step_out(rows, tile(128), f32),
            whole_out(edge(128)),
            whole_out((16, 128)),
            whole_out((128, 512)),
            whole_out((256, 512), bf16),
        ],
        [
            pltpu.VMEM((8, 512), f32),
            pltpu.VMEM((256, 512), bf16),
            pltpu.VMEM((512, 256), bf16),
            pltpu.VMEM(tile(512), f32),
            pltpu.VMEM((128, 512), f32),
            pltpu.VMEM((2, 8, 512), f32),
            pltpu.VMEM((2, 8, 128), f32),
        ],
        "last_norm",
        pixels * 512 * 128 * 10,
        pixels * 4864,
    )(info, st1, st3, gc, sc, act_b, slope_b, dotted_b, images, cotangent, w_out)

    arrived = partner(jnp.concatenate([own4, kept]), 1)
    st4 = swapped_sum(own4 + arrived[:16], everyone)
    other = arrived
    t_edge = partner(t_edge, 1)

    shares = lax.axis_size("batch")
    share = -(-1344 // (8 * shares)) * 8
    half = share * shares
    block = -(-(share + 6) // 16) * 16
    h, mine, sent, small_sums = call(
        back_body,
        steps + 1,
        [
            SMEM, eight, eight, whole_spec((16, 128)), whole_spec((16, 128)),
            whole_spec((128, 128)), whole_spec((144, 128)), whole_spec((16, 128)),
            whole_spec((512, 128)), whole_spec((136, 128)),
            whole_spec((128, 512)), small, small, small, large, whole_spec((128, 512)),
            whole_spec((256, 512)), taps,
            step_spec(tile(128), ahead), step_spec(tile(128), ahead), whole_spec(edge(256)),
            step_spec(tile(128), ahead), whole_spec(edge(128)),
            step_spec(tile(128), ahead), whole_spec(edge(128)),
            step_spec(tile(128), behind), step_spec(tile(128), behind),
            step_spec(tile(512), behind),
        ],
        [
            step_out(rows, tile(128), bf16, behind),
            whole_out((half + 8, 128)),
            whole_out((half + 8, 128)),
            whole_out((16, 128)),
        ],
        [
            pltpu.VMEM((8, 128), f32),
            pltpu.VMEM((128, 256), bf16),
            pltpu.VMEM((1536, 256), bf16),
            frame_like(),
            pltpu.VMEM((256, 1536), f32),
            pltpu.VMEM((128, 512), f32),
            pltpu.VMEM((2, 8, 128), f32),
            pltpu.VMEM((2 * half, 128), f32),
        ],
        "middle_back",
        pixels * 32 * 128 * 128 * 2,
        pixels * 4000,
    )(
        info, st1, st2, st3, st4, kept, other, own4, xz, gram, u_local, ga, sa, gb, gc,
        w_out, w_scaled, w_back,
        act_b, slope_b, y_edge, z2, z2_edge, t, t_edge, act_a, z1, images,
    )
    arrived = partner(sent, 1)
    spread = call(
        pack_body,
        1,
        [whole_spec((half + 8, 128)), whole_spec((half + 8, 128))],
        [whole_out((shares, block, 128), bf16)],
        [],
        "pack_shares",
        1e6,
        2e6,
    )(mine, arrived)[0]
    spread = lax.all_to_all(spread, "batch", 0, 0, tiled=True)
    st5, spread = call(
        functools.partial(share_body, share),
        1,
        [whole_spec((shares, block, 128))],
        [whole_out((8, 128)), whole_out((shares, block, 128), bf16)],
        [],
        "sum_shares",
        1e6,
        1e6,
    )(spread)
    gathered = lax.all_to_all(spread, "batch", 0, 0, tiled=True)

    grad_images = call(
        input_body,
        steps,
        [
            SMEM, eight, eight, small, whole_spec((512, 128)),
            step_spec(tile(128)), step_spec(tile(128)), step_spec(tile(512)),
        ],
        [step_out(rows, tile(512), bf16)],
        [pltpu.VMEM((8, 128), f32), pltpu.VMEM((128, 512), bf16)],
        "input_grad",
        pixels * 512 * 128 * 2,
        pixels * 2816,
    )(info, st1, st5, ga, w_in, h, z1, e)[0]

    gathered, grad_images = lax.optimization_barrier((gathered, grad_images))
    shared = whole_spec((shares, block, 128))
    gwi, gga, gsa, gwm, ggb, gsb, gwo, ggc, gsc = call(
        functools.partial(final_body, share),
        1,
        [SMEM, eight, eight, small, whole_spec((16, 128)), shared, shared],
        [
            whole_out((512, 128)), whole_out((1, 128)), whole_out((1, 128)),
            whole_out((1152, 128)), whole_out((1, 128)), whole_out((1, 128)),
            whole_out((128, 512)), whole_out((1, 512)), whole_out((1, 512)),
        ],
        [pltpu.VMEM((2 * half, 128), f32)],
        "replicated_grads",
        1e6,
        3e6,
    )(info, st1, st5, ga, small_sums, gathered, partner(gathered, 1))
    return (
        jnp.transpose(block_out, (2, 0, 1, 3)),
        jnp.transpose(grad_images, (2, 0, 1, 3)),
        gwi,
        gga.reshape(128),
        gsa.reshape(128),
        gwm.reshape(3, 3, 128, 128),
        ggb.reshape(128),
        gsb.reshape(128),
        gwo,
        ggc.reshape(512),
        gsc.reshape(512),
    )


def solution(mesh):
    split = P("batch", "rows", None, None)
    placed = (split, P("batch"), P(), P(), P(), P(), P(), P(), P(), P(), P(), split)
    return jax.shard_map(
        local,
        mesh=mesh,
        in_specs=placed,
        out_specs=(split, split) + (P(),) * 9,
        check_vma=False,
    )
```

```python
import functools
import math

import jax
import jax.numpy as jnp
from jax import lax
from jax.experimental import pallas as pl
from jax.experimental.pallas import tpu as pltpu
from jax.sharding import PartitionSpec as P

epsilon = 1e-05
axes = ("batch", "rows")
f32 = jnp.float32
bf16 = jnp.bfloat16
C0 = math.sqrt(2.0 / math.pi)
C1 = C0 * 0.044715
K0 = -2.0 * C0 / math.log(2.0)
K1 = -2.0 * C1 / math.log(2.0)
K2 = -3.0 * math.log(2.0)
HIGH = lax.Precision.HIGHEST


def partner(block, mask):
    total = lax.axis_size("batch") * lax.axis_size("rows")
    return lax.ppermute(block, axes, [(i, i ^ mask) for i in range(total)])


def swapped_sum(block, groups):
    size = len(groups[0])
    spread = jnp.broadcast_to(block[None], (size,) + block.shape)
    arrived = lax.all_to_all(spread, "batch", 0, 0, axis_index_groups=groups, tiled=True)
    return jnp.sum(arrived, axis=0)


def swapped(spread):
    return lax.all_to_all(spread, "batch", 0, 0, tiled=True)


def summed_at_once(block):
    total = lax.axis_size("batch") * lax.axis_size("rows")
    spread = jnp.broadcast_to(block[None], (total,) + block.shape)
    return jnp.sum(lax.all_to_all(spread, axes, 0, 0, tiled=True), axis=0)


def summed_by_swap(block, near=None):
    block = block + partner(block, 1)
    count = lax.axis_size("batch")
    if near is None or count % near:
        return swapped_sum(block, [list(range(count))])
    block = swapped_sum(block, [list(range(i, i + near)) for i in range(0, count, near)])
    return swapped_sum(block, [list(range(i, count, near)) for i in range(near)])


def gate(u):
    inner = K0 + K1 * (u * u)
    return pltpu.reciprocal(1.0 + jnp.exp2(u * inner), approx=True), inner


def gelu_terms(u):
    half, inner = gate(u)
    value = u * half
    slope = half + value * (1.0 - half) * (K2 * inner - 4.0 * C0)
    return value, slope


def gelu_value(u):
    return u * gate(u)[0]


def moments(total, squares, pixels):
    mean = total / pixels
    return mean, lax.rsqrt(squares / pixels - mean * mean + epsilon)


def fold8(values):
    lanes = values.shape[-1]
    return jnp.sum(values.reshape(values.size // (8 * lanes), 8, lanes), axis=0)


def total_row(values):
    return jnp.sum(values, axis=0, keepdims=True)


def wide(ref, start):
    return jnp.concatenate([ref[start + i : start + i + 1, :] for i in range(4)], axis=1)


def put_wide(ref, start, row):
    for i in range(4):
        ref[start + i : start + i + 1, :] = row[:, i * 128 : (i + 1) * 128]


def dot_tn(a, b):
    return lax.dot_general(a, b, (((0,), (0,)), ((), ())), preferred_element_type=f32)


def dot_nt(a, b, precision=None):
    return lax.dot_general(
        a, b, (((1,), (1,)), ((), ())), preferred_element_type=f32, precision=precision
    )


def dot(a, b, precision=None):
    return jnp.dot(a, b, preferred_element_type=f32, precision=precision)


def split_two(values):
    high = values.astype(bf16)
    return high, (values - high.astype(f32)).astype(bf16)


def dot_halves(a, b):
    high, low = split_two(a)
    return dot(high, b) + dot(low, b)


def row_of_sums(values):
    high, low = split_two(values)
    one = jnp.ones((16, values.shape[1]), bf16)
    return (dot_nt(one, high) + dot_nt(one, low))[0:8, :]


def call(body, grid, ins, outs, scratch, name, flops, bytes_moved):
    return pl.pallas_call(
        body,
        grid=(grid,),
        in_specs=ins,
        out_specs=[spec for spec, _ in outs],
        out_shape=[shape for _, shape in outs],
        scratch_shapes=scratch,
        name=name,
        compiler_params=pltpu.CompilerParams(
            dimension_semantics=("arbitrary",), vmem_limit_bytes=52 << 20
        ),
        cost_estimate=pl.CostEstimate(
            flops=int(flops), bytes_accessed=int(bytes_moved), transcendentals=0
        ),
    )


SMEM = pl.BlockSpec(memory_space=pltpu.SMEM)
ANY = pl.BlockSpec(memory_space=pl.ANY)


def whole_spec(shape):
    return pl.BlockSpec(tuple(shape), lambda i: (0,) * len(shape))


def step_spec(shape, place=lambda i: i):
    return pl.BlockSpec(tuple(shape), lambda i: (place(i),) + (0,) * (len(shape) - 1))


def whole_out(shape, dtype=f32):
    return (whole_spec(shape), jax.ShapeDtypeStruct(shape, dtype))


def step_out(count, shape, dtype, place=lambda i: i):
    return (
        step_spec(shape, place),
        jax.ShapeDtypeStruct((count,) + tuple(shape[1:]), dtype),
    )


def live(info, images, lanes):
    return lax.broadcasted_iota(jnp.int32, (images, lanes), 0) < info[0]


def groups(columns):
    return [(c, min(4, columns - c)) for c in range(0, columns, 4)]


def take_edge(info, edge_ref, ref):
    step = pl.program_id(0)

    @pl.when((step == 0) & (info[1] == 1))
    def _():
        edge_ref[...] = ref[0].astype(edge_ref.dtype)

    @pl.when((step == pl.num_programs(0) - 1) & (info[1] == 0))
    def _():
        edge_ref[...] = ref[ref.shape[0] - 1].astype(edge_ref.dtype)


def first_body(info, x_ref, w_ref, z_ref, edge_ref, stat_ref, zacc):
    step = pl.program_id(0)
    tall, columns, images = x_ref.shape[:3]
    area = columns * images

    @pl.when(step == 0)
    def _():
        zacc[...] = jnp.zeros_like(zacc)

    mask = live(info, images, 128)
    for r in range(tall):
        x = x_ref[r].reshape(area, 512)
        z = dot(x, w_ref[...]).reshape(columns, images, 128)
        z = jnp.where(mask, z, 0.0)
        z_ref[r] = z
        zacc[0] += fold8(z)
        zacc[1] += fold8(z * z)
    take_edge(info, edge_ref, z_ref)

    @pl.when(step == pl.num_programs(0) - 1)
    def _():
        pixels = (info[0] * (pl.num_programs(0) * tall * columns)).astype(f32)
        stat_ref[...] = jnp.zeros_like(stat_ref)
        stat_ref[0:1, :] = total_row(zacc[0])
        stat_ref[1:2, :] = total_row(zacc[1])
        stat_ref[2:3, :] = jnp.full((1, 128), pixels, f32)


def cross_body(x_ref, z_ref, xz_ref, acc):
    step = pl.program_id(0)
    tall, columns, images = x_ref.shape[:3]
    area = columns * images

    @pl.when(step == 0)
    def _():
        acc[...] = jnp.zeros_like(acc)

    for r in range(tall):
        z = z_ref[r].astype(bf16).reshape(area, 128)
        acc[...] += dot_tn(z, x_ref[r].reshape(area, 512))

    @pl.when(step == pl.num_programs(0) - 1)
    def _():
        for i in range(4):
            xz_ref[i * 128 : (i + 1) * 128, :] = acc[:, i * 128 : (i + 1) * 128]


def paired_weights(w_ref, target):
    for r in range(4):
        for u in range(3):
            for o in range(2):
                t = r - o
                base = (r * 3 + u) * 128
                if 0 <= t <= 2:
                    block = w_ref[t, u]
                else:
                    block = jnp.zeros((128, 128), bf16)
                target[base : base + 128, o * 128 : (o + 1) * 128] = block


def window(frame, pair):
    columns, images = frame.shape[1] - 2, frame.shape[2]
    parts = [
        frame[2 * pair + r, u : u + columns].reshape(columns * images, 128)
        for r in range(4)
        for u in range(3)
    ]
    return jnp.concatenate(parts, axis=1)


def clear_frame(frame):
    tall, wide_columns = frame.shape[:2]
    zero = jnp.zeros(frame.shape[2:], frame.dtype)
    for e in range(tall):
        frame[e, 0] = zero
        frame[e, wide_columns - 1] = zero
    for c in range(wide_columns):
        frame[0, c] = zero
        frame[tall - 1, c] = zero


def middle_body(
    info, st1, ga, sa, z_ref, edge_ref, w_ref, xz_ref,
    z2_ref, a_ref, stat_ref, frame, wide_w, coef, zacc,
):
    step = pl.program_id(0)
    last = pl.num_programs(0) - 1
    columns, images = z_ref.shape[1:3]
    area = columns * images

    def activated(z):
        return gelu_value(z * coef[0:1, :] + coef[1:2, :]).astype(bf16)

    @pl.when(step == 0)
    def _():
        mean, inv = moments(st1[0:1, :], st1[1:2, :], st1[2:3, :])
        scale = ga[...] * inv
        coef[0:1, :] = scale
        coef[1:2, :] = sa[...] - mean * scale
        paired_weights(w_ref, wide_w)
        zacc[...] = jnp.zeros_like(zacc)
        clear_frame(frame)
        place = (1 - info[1]) * (frame.shape[0] - 1)
        for c, n in groups(columns):
            frame[place, 1 + c : 1 + c + n] = activated(edge_ref[c : c + n])

    @pl.when(step < last)
    def _():
        for r in range(2):
            for c, n in groups(columns):
                value = activated(z_ref[r, c : c + n])
                frame[2 * step + 1 + r, 1 + c : 1 + c + n] = value
                a_ref[r, c : c + n] = value

    @pl.when(step > 0)
    def _():
        mask = live(info, images, 128)
        y = dot(window(frame, step - 1), wide_w[...])
        for r in range(2):
            z = y[:, r * 128 : (r + 1) * 128].reshape(columns, images, 128)
            z2_ref[r] = z
            zacc[0] += fold8(jnp.where(mask, jnp.sum(z, axis=0), 0.0))
            zacc[1] += fold8(jnp.where(mask, jnp.sum(z * z, axis=0), 0.0))

    @pl.when(step == last)
    def _():
        stat_ref[...] = jnp.zeros_like(stat_ref)
        for k in range(2):
            stat_ref[k : k + 1, :] = total_row(zacc[k])


def second_coef(st1, st2, gb, sb, coef):
    mean, inv = moments(st2[0:1, :], st2[1:2, :], st1[2:3, :])
    scale = gb[...] * inv
    coef[0:1, :] = scale
    coef[1:2, :] = sb[...] - mean * scale
    coef[2:3, :] = inv
    coef[3:4, :] = -mean * inv


def second_body(
    info, st1, st2, gb, sb, z_ref, wo_ref,
    act_ref, g_ref, gx_ref, ye_ref, ze_ref, st_ref, keep_ref, gram_ref, coef, cross, sums,
):
    step = pl.program_id(0)
    tall, columns, images = z_ref.shape[:3]
    area = columns * images

    @pl.when(step == 0)
    def _():
        second_coef(st1, st2, gb, sb, coef)
        cross[...] = jnp.zeros_like(cross)
        sums[...] = jnp.zeros_like(sums)

    mask = live(info, images, 128)
    scale, bias, inv, shift = (coef[i : i + 1, :] for i in range(4))
    edge_row = (1 - info[1]) * (tall - 1)
    at_edge = step == (1 - info[1]) * (pl.num_programs(0) - 1)
    totals = [jnp.zeros((images, 128), f32) for _ in range(3)]
    for r in range(tall):
        acts, others = [], []
        for c, n in groups(columns):
            z = z_ref[r, c : c + n]
            value, slope = gelu_terms(z * scale + bias)
            dotted = slope * (z * inv + shift)
            slope, dotted, value = (v.astype(bf16) for v in (slope, dotted, value))
            for k, part in enumerate((slope, dotted, value)):
                totals[k] += jnp.sum(part.astype(f32), axis=0)
            g_ref[r, c : c + n] = slope
            gx_ref[r, c : c + n] = dotted
            act_ref[r, c : c + n] = value
            value = jnp.where(mask, value, jnp.zeros((), bf16))
            acts.append(value.reshape(n * images, 128))
        acts = jnp.concatenate(acts, axis=0)
        cross[...] += dot_tn(
            acts,
            jnp.concatenate(
                [acts, g_ref[r].reshape(area, 128), gx_ref[r].reshape(area, 128)], axis=1
            ),
        )

        @pl.when(at_edge & (edge_row == r))
        def _():
            ye_ref[:, :, 0:128] = act_ref[r]
            ye_ref[:, :, 128:256] = g_ref[r]
            ze_ref[...] = z_ref[r]

    for k in range(3):
        sums[k] += fold8(jnp.where(mask, totals[k], 0.0))

    @pl.when(step == pl.num_programs(0) - 1)
    def _():
        gram = cross[:, 0:128]
        gram_ref[0:128, :] = gram
        st_ref[8:16, :] = jnp.zeros((8, 128), f32)
        st_ref[8:9, :] = total_row(sums[2])
        gram_ref[128:136, :] = st_ref[8:16, :]
        spread = dot_halves(gram_ref[...], wo_ref[...])
        put_wide(st_ref, 0, spread[128:129, :])
        put_wide(st_ref, 4, total_row(spread[0:128, :] * wo_ref[...].astype(f32)))
        st_ref[9:16, :] = jnp.zeros((7, 128), f32)
        for k in range(2):
            st_ref[9 + k : 10 + k, :] = total_row(sums[k])
        low = info[1] == 0
        keep_ref[...] = jnp.where(low, cross[:, 128:256], cross[:, 256:384])
        st_ref[16:144, :] = jnp.where(low, cross[:, 256:384], cross[:, 128:256])


def spread_body(head_ref, arrived_ref, keep_ref, out_ref):
    sums = head_ref[0:16, :] + arrived_ref[0:16, :]
    share = 128 // out_ref.shape[0]
    for k in range(out_ref.shape[0]):
        rows = slice(k * share, (k + 1) * share)
        out_ref[k, 0:16] = sums
        out_ref[k, 16 : 16 + share] = keep_ref[rows, :] + arrived_ref[16 + k * share : 16 + (k + 1) * share, :]
        if share < 8:
            out_ref[k, 16 + share :] = jnp.zeros((8 - share, 128), f32)


def both_body(info, own_ref, arrived_ref, out_ref):
    sums = own_ref[0:16, :] + arrived_ref[0:16, :]
    mine, other = own_ref[16:, :], arrived_ref[16:, :]
    low = info[1] == 0
    block = jnp.concatenate(
        [sums, jnp.where(low, mine, other), jnp.where(low, other, mine)], axis=0
    )
    for k in range(out_ref.shape[0]):
        out_ref[k] = block


def last_body(
    info, st1, in3, gc, sc, y_ref, g_ref, gx_ref, x_ref, cot_ref, wo_ref,
    out_ref, e_ref, t_ref, te_ref, st_ref, st3, u_ref, ws_ref,
    coef, w_two, w_turn, z_buf, cross, sums, sums_b,
):
    step = pl.program_id(0)
    tall, columns, images = x_ref.shape[:3]
    area = columns * images

    @pl.when(step == 0)
    def _():
        total = in3[0]
        for k in range(1, in3.shape[0]):
            total = total + in3[k]
        st3[...] = total[0:16]
        st_ref[16:, :] = total[16:]
        mean, inv = moments(wide(st3, 0), wide(st3, 4), st1[2:3, 0:1])
        scale = gc[...] * inv
        coef[0:1, :] = sc[...] - mean * scale
        high, low = split_two(wo_ref[...].astype(f32) * scale)
        w_two[0:128, :] = high
        w_two[128:256, :] = low
        ws_ref[...] = w_two[...]
        w_turn[:, 0:128] = jnp.transpose(w_two[0:128, :])
        w_turn[:, 128:256] = jnp.transpose(w_two[128:256, :])
        cross[...] = jnp.zeros_like(cross)
        sums[...] = jnp.zeros_like(sums)
        sums_b[...] = jnp.zeros_like(sums_b)

    mask = live(info, images, 512)
    bias = coef[0:1, :]
    zero = jnp.zeros((), bf16)
    piece = columns // 4
    parts = [(r, c) for r in range(tall) for c in range(0, columns, piece)]
    n = piece * images

    def product(r, c):
        act = y_ref[r, c : c + piece].reshape(n, 128)
        z = dot(jnp.concatenate([act, act], axis=1), w_two[...])
        z_buf[r, c : c + piece] = z.reshape(piece, images, 512)

    def pointwise(r, c):
        x = jnp.where(mask, x_ref[r, c], zero).astype(f32)
        value, slope = gelu_terms(z_buf[r, c] + (bias + x))
        out_ref[r, c] = value.astype(bf16)
        cot = jnp.where(mask, cot_ref[r, c], zero).astype(f32)
        e = slope * cot
        e_ref[r, c] = e.astype(bf16)
        return fold8(e), fold8(x)

    def collect(r, c):
        e = e_ref[r, c : c + piece].reshape(n, 512)
        cross[...] += dot_tn(y_ref[r, c : c + piece].reshape(n, 128), e)

    def through(r, c):
        y = dot(e_ref[r, c : c + piece].reshape(n, 512), w_turn[...])
        t = (y[:, 0:128] + y[:, 128:256]).reshape(piece, images, 128)
        t_ref[r, c : c + piece] = t
        sums_b[0] += fold8(t * g_ref[r, c : c + piece].astype(f32))
        sums_b[1] += fold8(t * gx_ref[r, c : c + piece].astype(f32))

    product(*parts[0])
    for k in range(len(parts) + 1):
        work = []
        if k + 1 < len(parts):
            work.append(functools.partial(product, *parts[k + 1]))
        if k > 0:
            work.append(functools.partial(through, *parts[k - 1]))
            work.append(functools.partial(collect, *parts[k - 1]))
        if k < len(parts):
            r, first = parts[k]
            total_e = jnp.zeros((8, 512), f32)
            total_x = jnp.zeros((8, 512), f32)
            for c in range(piece):
                if c % 2 == 0 and work:
                    work.pop(0)()
                add_e, add_x = pointwise(r, first + c)
                total_e += add_e
                total_x += add_x
            sums[0] += total_e
            sums[1] += total_x
        for rest in work:
            rest()
    take_edge(info, te_ref, t_ref)

    @pl.when(step == pl.num_programs(0) - 1)
    def _():
        u_ref[...] = cross[...]
        put_wide(st_ref, 0, total_row(sums[0]))
        put_wide(st_ref, 4, total_row(wo_ref[...].astype(f32) * cross[...]))
        put_wide(st_ref, 10, total_row(sums[1]))
        for k in range(2):
            st_ref[8 + k : 9 + k, :] = total_row(sums_b[k])
            st_ref[14 + k : 15 + k, :] = jnp.zeros((1, 128), f32)


def back_body(
    info, st1, st2, st3, in4, own4, xz_ref, gram_ref, u_ref, ga, sa, gb, gc, wo_ref, ws_ref, wt_ref,
    y_ref, s_ref, ye_ref, z2_ref, ze_ref, t_ref, te_ref, a_ref, z1_ref, x_ref,
    h_ref, mine_ref, sent_ref, small_ref,
    coef, mm, wide_w, frame, dacc, vacc, sums, packed, st4, pq,
):
    step = pl.program_id(0)
    last = pl.num_programs(0) - 1
    columns, images = z1_ref.shape[1:3]
    area = columns * images
    mask = live(info, images, 128)

    def second_back(t, product, slope, z):
        kappa, scale_b, beta, alpha = (coef[i : i + 1, :] for i in range(4))
        through = t - kappa - product[..., 0:128] - product[..., 128:256]
        grad = scale_b * (slope.astype(f32) * through) - (alpha + beta * z)
        return jnp.where(mask, grad, 0.0).astype(bf16)

    @pl.when(step == 0)
    def _():
        pixels = st1[2:3, :]
        pixel = st1[2:3, 0:1]
        mean_a, inv_a = moments(st1[0:1, :], st1[1:2, :], pixels)
        mean_b, inv_b = moments(st2[0:1, :], st2[1:2, :], pixels)
        mean_c, inv_c = moments(wide(st3, 0), wide(st3, 4), pixel)
        total = in4[0, 0:16]
        share = 128 // in4.shape[0]
        span = (in4.shape[1] - 16) // 2
        for k in range(in4.shape[0]):
            if k > 0:
                total = total + in4[k, 0:16]
            rows = slice(k * share, (k + 1) * share)
            pq[0, rows] = in4[k, 16 : 16 + share]
            pq[1, rows] = in4[k, 16 + span : 16 + span + share]
        st4[...] = total
        total_c = wide(st4, 0)
        dot_c = inv_c * (wide(st4, 4) - mean_c * total_c)
        weights = wo_ref[...].astype(f32)
        scaled = ws_ref[0:128, :].astype(f32) + ws_ref[128:256, :].astype(f32)
        near, far = split_two(weights * (inv_c * dot_c / pixel))
        mat = dot_nt(near, ws_ref[0:128, :]) + dot_nt(near, ws_ref[128:256, :])
        mat = mat + dot_nt(far, ws_ref[0:128, :])
        high, low = split_two(mat)
        mm[:, 0:128] = high
        mm[:, 128:256] = low
        kappa = row_of_sums(scaled * (total_c / pixel))[0:1, :]
        mean_act = jnp.transpose(jnp.broadcast_to(st3[8:9, :] / pixels, (8, 128)))[:, 0:1]
        kappa = kappa - total_row(mean_act * mat)
        total_b = st4[8:9, :] - kappa * st3[9:10, :] - total_row(mat * pq[0])
        dot_b = st4[9:10, :] - kappa * st3[10:11, :] - total_row(mat * pq[1])
        scale_b = gb[...] * inv_b
        scale_a = ga[...] * inv_a
        coef[0:1, :] = kappa
        coef[1:2, :] = scale_b
        coef[2:3, :] = scale_b * inv_b * dot_b / pixels
        coef[3:4, :] = scale_b * (total_b - mean_b * inv_b * dot_b) / pixels
        coef[4:5, :] = scale_a
        coef[5:6, :] = sa[...] - mean_a * scale_a
        small_ref[...] = jnp.zeros_like(small_ref)
        put_wide(small_ref, 0, total_c)
        put_wide(small_ref, 4, dot_c)
        small_ref[8:9, :] = total_b
        small_ref[9:10, :] = dot_b
        column = jnp.transpose(gram_ref[128:136, :])[:, 0:1]
        product = dot_halves(gram_ref[0:128, :], wo_ref[...])
        grad = u_ref[...] - column * (total_c / pixel) - (product - column * mean_c) * (
            inv_c * dot_c / pixel
        )
        grad = grad * (gc[...] * inv_c)
        for i in range(4):
            packed[1152 + i * 128 : 1280 + i * 128, :] = grad[:, i * 128 : (i + 1) * 128]
        paired_weights(wt_ref, wide_w)
        dacc[...] = jnp.zeros_like(dacc)
        vacc[...] = jnp.zeros_like(vacc)
        sums[...] = jnp.zeros_like(sums)
        clear_frame(frame)
        place = (1 - info[1]) * (frame.shape[0] - 1)
        for c, n in groups(columns):
            act = ye_ref[c : c + n, :, 0:128].reshape(n * images, 128)
            extra = dot(act, mm[...]).reshape(n, images, 256)
            frame[place, 1 + c : 1 + c + n] = second_back(
                te_ref[c : c + n], extra, ye_ref[c : c + n, :, 128:256], ze_ref[c : c + n]
            )

    @pl.when(step < last)
    def _():
        for r in range(2):
            act = y_ref[r].reshape(area, 128)
            extra = dot(act, mm[...]).reshape(columns, images, 256)
            for c, n in groups(columns):
                frame[2 * step + 1 + r, 1 + c : 1 + c + n] = second_back(
                    t_ref[r, c : c + n],
                    extra[c : c + n],
                    s_ref[r, c : c + n],
                    z2_ref[r, c : c + n],
                )

    @pl.when(step > 0)
    def _():
        scale_a, bias_a = coef[4:5, :], coef[5:6, :]
        near = window(frame, step - 1)
        through = dot(near, wide_w[...])
        act = jnp.concatenate([a_ref[r].reshape(area, 128) for r in range(2)], axis=1)
        dacc[...] += dot_tn(act, near)
        total = jnp.zeros((8, 128), f32)
        dots = jnp.zeros((8, 128), f32)
        for r in range(2):
            part = through[:, r * 128 : (r + 1) * 128].reshape(columns, images, 128)
            for c, n in groups(columns):
                z = z1_ref[r, c : c + n]
                slope = gelu_terms(z * scale_a + bias_a)[1]
                grad = part[c : c + n] * slope
                total += fold8(grad)
                dots += fold8(grad * z)
                h_ref[r, c : c + n] = grad.astype(bf16)
        sums[0] += total
        sums[1] += dots
        vacc[...] += dot_tn(h_ref[...].reshape(2 * area, 128), x_ref[...].reshape(2 * area, 512))

    @pl.when(step == last)
    def _():
        pixels = st1[2:3, :]
        total_h, dot_h = total_row(sums[0]), total_row(sums[1])
        tail = jnp.concatenate(
            [total_h, dot_h, st1[0:1, :] / pixels, jnp.zeros((5, 128), f32)], axis=0
        )
        columns2 = jnp.transpose(tail)
        column_h, mean_a = columns2[:, 0:1], columns2[:, 2:3]
        for i in range(4):
            lanes = slice(i * 128, (i + 1) * 128)
            center = st4[10 + i : 11 + i, :] / pixels
            packed[1664 + i * 128 : 1792 + i * 128, :] = vacc[:, lanes] - column_h * center
            packed[2176 + i * 128 : 2304 + i * 128, :] = (
                xz_ref[lanes, :] - mean_a * own4[10 + i : 11 + i, :]
            )
        for t in range(3):
            for u in range(3):
                parts = []
                for o in range(2):
                    base = ((o + 2 - t) * 3 + 2 - u) * 128
                    parts.append(dacc[o * 128 : (o + 1) * 128, base : base + 128])
                packed[(t * 3 + u) * 128 : (t * 3 + u + 1) * 128, :] = parts[0] + parts[1]
        if packed.shape[0] > 2688:
            packed[2688:, :] = jnp.zeros((packed.shape[0] - 2688, 128), f32)
        half = packed.shape[0] // 2
        low = info[1] == 0
        mine_ref[0:half, :] = jnp.where(low, packed[0:half, :], packed[half:, :])
        sent_ref[0:half, :] = jnp.where(low, packed[half:, :], packed[0:half, :])
        mine_ref[half : half + 8, :] = tail
        sent_ref[half : half + 8, :] = tail


def pack_body(mine_ref, arrived_ref, out_ref):
    shares, block = out_ref.shape[:2]
    share = (mine_ref.shape[0] - 8) // shares
    small = mine_ref[shares * share :, :] + arrived_ref[shares * share :, :]
    high = small.astype(bf16).astype(f32)
    middle = (small - high).astype(bf16).astype(f32)
    low = small - high - middle
    tail = jnp.concatenate(
        [high[0:2], middle[0:2], low[0:2], jnp.zeros((block - share - 6, 128), f32)], axis=0
    )
    for k in range(shares):
        rows = slice(k * share, (k + 1) * share)
        total = mine_ref[rows, :] + arrived_ref[rows, :]
        out_ref[k] = jnp.concatenate([total, tail], axis=0).astype(bf16)


def share_body(share, in_ref, small_ref, out_ref):
    total = in_ref[0].astype(f32)
    for k in range(1, in_ref.shape[0]):
        total = total + in_ref[k].astype(f32)
    sums = total[share : share + 2] + total[share + 2 : share + 4] + total[share + 4 : share + 6]
    small_ref[...] = jnp.concatenate([sums, jnp.zeros((6, 128), f32)], axis=0)
    for k in range(out_ref.shape[0]):
        out_ref[k] = total.astype(bf16)


def input_body(info, st1, st5, ga, wi_ref, h_ref, z_ref, e_ref, g_ref, coef, w_turn):
    step = pl.program_id(0)
    tall, columns, images = z_ref.shape[:3]
    area = columns * images

    @pl.when(step == 0)
    def _():
        pixels = st1[2:3, :]
        mean, inv = moments(st1[0:1, :], st1[1:2, :], pixels)
        scale = ga[...] * inv
        w_turn[...] = jnp.transpose(wi_ref[...])
        total = st5[0:1, :]
        dot_a = inv * (st5[1:2, :] - mean * total)
        coef[0:1, :] = scale
        coef[1:2, :] = scale * inv * dot_a / pixels
        coef[2:3, :] = scale * (total - mean * inv * dot_a) / pixels

    mask = live(info, images, 128)
    scale, beta, alpha = (coef[i : i + 1, :] for i in range(3))
    for r in range(tall):
        parts = []
        for c, n in groups(columns):
            grad = scale * h_ref[r, c : c + n].astype(f32) - (alpha + beta * z_ref[r, c : c + n])
            parts.append(jnp.where(mask, grad, 0.0).astype(bf16).reshape(n * images, 128))
        through = dot(jnp.concatenate(parts, axis=0), w_turn[...])
        through = through.reshape(columns, images, 512)
        for c in range(columns):
            g_ref[r, c] = (through[c] + e_ref[r, c].astype(f32)).astype(bf16)


def final_body(
    share, info, st1, st5, ga, small_ref, mine_ref, other_ref,
    gwi_ref, gga_ref, gsa_ref, gwm_ref, ggb_ref, gsb_ref, gwo_ref, ggc_ref, gsc_ref, total_ref,
):
    shares = mine_ref.shape[0]
    for k in range(shares):
        mine, other = mine_ref[k].astype(f32), other_ref[k].astype(f32)
        low = jnp.where(info[1] == 0, mine, other)
        high = jnp.where(info[1] == 0, other, mine)
        total_ref[k * share : (k + 1) * share, :] = low[0:share]
        total_ref[(shares + k) * share : (shares + k + 1) * share, :] = high[0:share]
    pixels = st1[2:3, :]
    mean, inv = moments(st1[0:1, :], st1[1:2, :], pixels)
    total = st5[0:1, :]
    dot = inv * (st5[1:2, :] - mean * total)
    gsa_ref[...] = total
    gga_ref[...] = dot
    gsb_ref[...] = small_ref[8:9, :]
    ggb_ref[...] = small_ref[9:10, :]
    gsc_ref[...] = wide(small_ref, 0)
    ggc_ref[...] = wide(small_ref, 4)
    gwm_ref[...] = total_ref[0:1152, :]
    for i in range(4):
        gwo_ref[:, i * 128 : (i + 1) * 128] = total_ref[1152 + i * 128 : 1280 + i * 128, :]
        v = jnp.transpose(total_ref[1664 + i * 128 : 1792 + i * 128, :])
        xz = jnp.transpose(total_ref[2176 + i * 128 : 2304 + i * 128, :])
        gwi_ref[i * 128 : (i + 1) * 128, :] = (ga[...] * inv) * (v - xz * (inv * dot / pixels))


def local(
    images, counts, w_in, gain_a, shift_a, w_mid, gain_b, shift_b, w_out, gain_c, shift_c, cotangent
):
    count, rows, columns, channels = images.shape
    steps = rows // 2
    info = jnp.stack([counts[0], lax.axis_index("rows").astype(jnp.int32)])
    images = jnp.transpose(images, (1, 2, 0, 3))
    cotangent = jnp.transpose(cotangent, (1, 2, 0, 3))
    ga, sa, gb, sb = (v.reshape(1, 128) for v in (gain_a, shift_a, gain_b, shift_b))
    gc, sc = gain_c.reshape(1, 512), shift_c.reshape(1, 512)
    small = whole_spec((1, 128))
    large = whole_spec((1, 512))
    eight = whole_spec((8, 128))
    taps = whole_spec((3, 3, 128, 128))

    def tile(lanes):
        return (2, columns, count, lanes)

    def edge(lanes):
        return (columns, count, lanes)

    def ahead(i):
        return jnp.minimum(i, steps - 1)

    def behind(i):
        return jnp.maximum(i - 1, 0)

    def frame_like():
        return pltpu.VMEM((rows + 2, columns + 2, count, 128), bf16)

    pixels = count * rows * columns

    z1, z1_edge, st1 = call(
        first_body,
        steps,
        [SMEM, step_spec(tile(512)), whole_spec((512, 128))],
        [
            step_out(rows, tile(128), f32),
            whole_out(edge(128)),
            whole_out((8, 128)),
        ],
        [pltpu.VMEM((2, 8, 128), f32)],
        "first_norm_sums",
        pixels * 512 * 128 * 2,
        pixels * 1536,
    )(info, images, w_in)
    z1_edge = partner(z1_edge, 1)
    st1 = summed_at_once(st1)
    xz = call(
        cross_body,
        steps,
        [step_spec(tile(512)), step_spec(tile(128))],
        [whole_out((512, 128))],
        [pltpu.VMEM((128, 512), f32)],
        "input_cross",
        pixels * 512 * 128 * 2,
        pixels * 1536,
    )(images, z1)[0]
    w_back = jnp.swapaxes(w_mid[::-1, ::-1], 2, 3)
    xz, w_back = lax.optimization_barrier((xz, w_back))

    shares = lax.axis_size("batch")
    span = max(8, 128 // shares)
    everyone = [list(range(lax.axis_size("batch")))]
    z2, act_a, st2 = call(
        middle_body,
        steps + 1,
        [
            SMEM, eight, small, small, step_spec(tile(128), ahead), whole_spec(edge(128)), taps,
            whole_spec((512, 128)),
        ],
        [
            step_out(rows, tile(128), f32, behind),
            step_out(rows, tile(128), bf16, ahead),
            whole_out((8, 128)),
        ],
        [
            frame_like(),
            pltpu.VMEM((1536, 256), bf16),
            pltpu.VMEM((8, 128), f32),
            pltpu.VMEM((2, 8, 128), f32),
        ],
        "middle_conv",
        pixels * 12 * 128 * 128 * 2,
        pixels * 1280,
    )(info, st1, ga, sa, z1, z1_edge, w_mid, xz)
    st2 = summed_by_swap(st2)

    act_b, slope_b, dotted_b, y_edge, z2_edge, head, kept, gram = call(
        second_body,
        steps,
        [SMEM, eight, eight, small, small, step_spec(tile(128)), whole_spec((128, 512))],
        [
            step_out(rows, tile(128), bf16),
            step_out(rows, tile(128), bf16),
            step_out(rows, tile(128), bf16),
            whole_out(edge(256), bf16),
            whole_out(edge(128)),
            whole_out((144, 128)),
            whole_out((128, 128)),
            whole_out((136, 128)),
        ],
        [pltpu.VMEM((8, 128), f32), pltpu.VMEM((128, 384), f32), pltpu.VMEM((3, 8, 128), f32)],
        "second_norm",
        pixels * 384 * 128 * 2,
        pixels * 1280,
    )(info, st1, st2, gb, sb, z2, w_out)
    arrived3 = swapped(
        call(
            spread_body,
            1,
            [whole_spec((144, 128)), whole_spec((144, 128)), whole_spec((128, 128))],
            [whole_out((shares, 16 + span, 128))],
            [],
            "spread_third",
            1e5,
            1e6,
        )(head, partner(head, 1), kept)[0]
    )

    block_out, e, t, t_edge, own4, st3, u_local, w_scaled = call(
        last_body,
        steps,
        [
            SMEM, eight, whole_spec((shares, 16 + span, 128)), large, large, step_spec(tile(128)),
            step_spec(tile(128)), step_spec(tile(128)), step_spec(tile(512)),
            step_spec(tile(512)), whole_spec((128, 512)),
        ],
        [
            step_out(rows, tile(512), bf16),
            step_out(rows, tile(512), bf16),
            step_out(rows, tile(128), f32),
            whole_out(edge(128)),
            whole_out((16 + span, 128)),
            whole_out((16, 128)),
            whole_out((128, 512)),
            whole_out((256, 512), bf16),
        ],
        [
            pltpu.VMEM((8, 512), f32),
            pltpu.VMEM((256, 512), bf16),
            pltpu.VMEM((512, 256), bf16),
            pltpu.VMEM(tile(512), f32),
            pltpu.VMEM((128, 512), f32),
            pltpu.VMEM((2, 8, 512), f32),
            pltpu.VMEM((2, 8, 128), f32),
        ],
        "last_norm",
        pixels * 512 * 128 * 10,
        pixels * 4864,
    )(info, st1, arrived3, gc, sc, act_b, slope_b, dotted_b, images, cotangent, w_out)

    other4, y_edge, z2_edge, t_edge = lax.optimization_barrier(
        tuple(
            partner(v, 1)
            for v in lax.optimization_barrier((own4, y_edge, z2_edge, t_edge))
        )
    )
    arrived4 = swapped(
        call(
            both_body,
            1,
            [SMEM, whole_spec((16 + span, 128)), whole_spec((16 + span, 128))],
            [whole_out((shares, 16 + 2 * span, 128))],
            [],
            "spread_fourth",
            1e5,
            1e6,
        )(info, own4, other4)[0]
    )

    share = -(-1344 // (8 * shares)) * 8
    half = share * shares
    block = -(-(share + 6) // 16) * 16
    h, mine, sent, small_sums = call(
        back_body,
        steps + 1,
        [
            SMEM, eight, eight, whole_spec((16, 128)), whole_spec((shares, 16 + 2 * span, 128)),
            whole_spec((16 + span, 128)),
            whole_spec((512, 128)), whole_spec((136, 128)),
            whole_spec((128, 512)), small, small, small, large, whole_spec((128, 512)),
            whole_spec((256, 512)), taps,
            step_spec(tile(128), ahead), step_spec(tile(128), ahead), whole_spec(edge(256)),
            step_spec(tile(128), ahead), whole_spec(edge(128)),
            step_spec(tile(128), ahead), whole_spec(edge(128)),
            step_spec(tile(128), behind), step_spec(tile(128), behind),
            step_spec(tile(512), behind),
        ],
        [
            step_out(rows, tile(128), bf16, behind),
            whole_out((half + 8, 128)),
            whole_out((half + 8, 128)),
            whole_out((16, 128)),
        ],
        [
            pltpu.VMEM((8, 128), f32),
            pltpu.VMEM((128, 256), bf16),
            pltpu.VMEM((1536, 256), bf16),
            frame_like(),
            pltpu.VMEM((256, 1536), f32),
            pltpu.VMEM((128, 512), f32),
            pltpu.VMEM((2, 8, 128), f32),
            pltpu.VMEM((2 * half, 128), f32),
            pltpu.VMEM((16, 128), f32),
            pltpu.VMEM((2, 128, 128), f32),
        ],
        "middle_back",
        pixels * 32 * 128 * 128 * 2,
        pixels * 4000,
    )(
        info, st1, st2, st3, arrived4, own4, xz, gram, u_local, ga, sa, gb, gc,
        w_out, w_scaled, w_back,
        act_b, slope_b, y_edge, z2, z2_edge, t, t_edge, act_a, z1, images,
    )
    arrived = partner(sent, 1)
    spread = call(
        pack_body,
        1,
        [whole_spec((half + 8, 128)), whole_spec((half + 8, 128))],
        [whole_out((shares, block, 128), bf16)],
        [],
        "pack_shares",
        1e6,
        2e6,
    )(mine, arrived)[0]
    spread = swapped(spread)
    st5, spread = call(
        functools.partial(share_body, share),
        1,
        [whole_spec((shares, block, 128))],
        [whole_out((8, 128)), whole_out((shares, block, 128), bf16)],
        [],
        "sum_shares",
        1e6,
        1e6,
    )(spread)
    gathered = swapped(spread)

    grad_images = call(
        input_body,
        steps,
        [
            SMEM, eight, eight, small, whole_spec((512, 128)),
            step_spec(tile(128)), step_spec(tile(128)), step_spec(tile(512)),
        ],
        [step_out(rows, tile(512), bf16)],
        [pltpu.VMEM((8, 128), f32), pltpu.VMEM((128, 512), bf16)],
        "input_grad",
        pixels * 512 * 128 * 2,
        pixels * 2816,
    )(info, st1, st5, ga, w_in, h, z1, e)[0]

    gathered, grad_images = lax.optimization_barrier((gathered, grad_images))
    shared = whole_spec((shares, block, 128))
    gwi, gga, gsa, gwm, ggb, gsb, gwo, ggc, gsc = call(
        functools.partial(final_body, share),
        1,
        [SMEM, eight, eight, small, whole_spec((16, 128)), shared, shared],
        [
            whole_out((512, 128)), whole_out((1, 128)), whole_out((1, 128)),
            whole_out((1152, 128)), whole_out((1, 128)), whole_out((1, 128)),
            whole_out((128, 512)), whole_out((1, 512)), whole_out((1, 512)),
        ],
        [pltpu.VMEM((2 * half, 128), f32)],
        "replicated_grads",
        1e6,
        3e6,
    )(info, st1, st5, ga, small_sums, gathered, partner(gathered, 1))
    return (
        jnp.transpose(block_out, (2, 0, 1, 3)),
        jnp.transpose(grad_images, (2, 0, 1, 3)),
        gwi,
        gga.reshape(128),
        gsa.reshape(128),
        gwm.reshape(3, 3, 128, 128),
        ggb.reshape(128),
        gsb.reshape(128),
        gwo,
        ggc.reshape(512),
        gsc.reshape(512),
    )


def solution(mesh):
    split = P("batch", "rows", None, None)
    placed = (split, P("batch"), P(), P(), P(), P(), P(), P(), P(), P(), P(), split)
    return jax.shard_map(
        local,
        mesh=mesh,
        in_specs=placed,
        out_specs=(split, split) + (P(),) * 9,
        check_vma=False,
    )
```

```python
import functools
import math

import jax
import jax.numpy as jnp
from jax import lax
from jax.experimental import pallas as pl
from jax.experimental.pallas import tpu as pltpu
from jax.sharding import PartitionSpec as P

epsilon = 1e-05
axes = ("batch", "rows")
f32 = jnp.float32
bf16 = jnp.bfloat16
C0 = math.sqrt(2.0 / math.pi)
C1 = C0 * 0.044715
K0 = -2.0 * C0 / math.log(2.0)
K1 = -2.0 * C1 / math.log(2.0)
K2 = -3.0 * math.log(2.0)
HIGH = lax.Precision.HIGHEST


def partner(block, mask):
    total = lax.axis_size("batch") * lax.axis_size("rows")
    return lax.ppermute(block, axes, [(i, i ^ mask) for i in range(total)])


def swapped_sum(block, groups):
    size = len(groups[0])
    spread = jnp.broadcast_to(block[None], (size,) + block.shape)
    arrived = lax.all_to_all(spread, "batch", 0, 0, axis_index_groups=groups, tiled=True)
    return jnp.sum(arrived, axis=0)


def swapped(spread):
    return lax.all_to_all(spread, "batch", 0, 0, tiled=True)


def summed_at_once(block):
    total = lax.axis_size("batch") * lax.axis_size("rows")
    spread = jnp.broadcast_to(block[None], (total,) + block.shape)
    return jnp.sum(lax.all_to_all(spread, axes, 0, 0, tiled=True), axis=0)


def summed_by_swap(block, near=None):
    block = block + partner(block, 1)
    count = lax.axis_size("batch")
    if near is None or count % near:
        return swapped_sum(block, [list(range(count))])
    block = swapped_sum(block, [list(range(i, i + near)) for i in range(0, count, near)])
    return swapped_sum(block, [list(range(i, count, near)) for i in range(near)])


def gate(u):
    inner = K0 + K1 * (u * u)
    return pltpu.reciprocal(1.0 + jnp.exp2(u * inner), approx=True), inner


def gelu_terms(u):
    half, inner = gate(u)
    value = u * half
    slope = half + value * (1.0 - half) * (K2 * inner - 4.0 * C0)
    return value, slope


def gelu_value(u):
    return u * gate(u)[0]


def moments(total, squares, pixels):
    mean = total / pixels
    return mean, lax.rsqrt(squares / pixels - mean * mean + epsilon)


def fold8(values):
    lanes = values.shape[-1]
    return jnp.sum(values.reshape(values.size // (8 * lanes), 8, lanes), axis=0)


def total_row(values):
    return jnp.sum(values, axis=0, keepdims=True)


def wide(ref, start):
    return jnp.concatenate([ref[start + i : start + i + 1, :] for i in range(4)], axis=1)


def put_wide(ref, start, row):
    for i in range(4):
        ref[start + i : start + i + 1, :] = row[:, i * 128 : (i + 1) * 128]


def dot_tn(a, b):
    return lax.dot_general(a, b, (((0,), (0,)), ((), ())), preferred_element_type=f32)


def dot_nt(a, b, precision=None):
    return lax.dot_general(
        a, b, (((1,), (1,)), ((), ())), preferred_element_type=f32, precision=precision
    )


def dot(a, b, precision=None):
    return jnp.dot(a, b, preferred_element_type=f32, precision=precision)


def split_two(values):
    high = values.astype(bf16)
    return high, (values - high.astype(f32)).astype(bf16)


def dot_halves(a, b):
    high, low = split_two(a)
    return dot(high, b) + dot(low, b)


def row_of_sums(values):
    high, low = split_two(values)
    one = jnp.ones((16, values.shape[1]), bf16)
    return (dot_nt(one, high) + dot_nt(one, low))[0:8, :]


def call(body, grid, ins, outs, scratch, name, flops, bytes_moved, vmem=52):
    return pl.pallas_call(
        body,
        grid=(grid,),
        in_specs=ins,
        out_specs=[spec for spec, _ in outs],
        out_shape=[shape for _, shape in outs],
        scratch_shapes=scratch,
        name=name,
        compiler_params=pltpu.CompilerParams(
            dimension_semantics=("arbitrary",), vmem_limit_bytes=vmem << 20
        ),
        cost_estimate=pl.CostEstimate(
            flops=int(flops), bytes_accessed=int(bytes_moved), transcendentals=0
        ),
    )


SMEM = pl.BlockSpec(memory_space=pltpu.SMEM)
ANY = pl.BlockSpec(memory_space=pl.ANY)


def whole_spec(shape):
    return pl.BlockSpec(tuple(shape), lambda i: (0,) * len(shape))


def step_spec(shape, place=lambda i: i):
    return pl.BlockSpec(tuple(shape), lambda i: (place(i),) + (0,) * (len(shape) - 1))


def whole_out(shape, dtype=f32):
    return (whole_spec(shape), jax.ShapeDtypeStruct(shape, dtype))


def step_out(count, shape, dtype, place=lambda i: i):
    return (
        step_spec(shape, place),
        jax.ShapeDtypeStruct((count,) + tuple(shape[1:]), dtype),
    )


def live(info, images, lanes):
    return lax.broadcasted_iota(jnp.int32, (images, lanes), 0) < info[0]


def groups(columns):
    return [(c, min(4, columns - c)) for c in range(0, columns, 4)]


def take_edge(info, edge_ref, ref):
    step = pl.program_id(0)

    @pl.when((step == 0) & (info[1] == 1))
    def _():
        edge_ref[...] = ref[0].astype(edge_ref.dtype)

    @pl.when((step == pl.num_programs(0) - 1) & (info[1] == 0))
    def _():
        edge_ref[...] = ref[ref.shape[0] - 1].astype(edge_ref.dtype)


def first_body(info, x_ref, w_ref, z_ref, edge_ref, stat_ref, zacc):
    step = pl.program_id(0)
    tall, columns, images = x_ref.shape[:3]
    area = columns * images

    @pl.when(step == 0)
    def _():
        zacc[...] = jnp.zeros_like(zacc)

    mask = live(info, images, 128)
    for r in range(tall):
        x = x_ref[r].reshape(area, 512)
        z = dot(x, w_ref[...]).reshape(columns, images, 128)
        z = jnp.where(mask, z, 0.0)
        z_ref[r] = z
        zacc[0] += fold8(z)
        zacc[1] += fold8(z * z)
    take_edge(info, edge_ref, z_ref)

    @pl.when(step == pl.num_programs(0) - 1)
    def _():
        pixels = (info[0] * (pl.num_programs(0) * tall * columns)).astype(f32)
        stat_ref[...] = jnp.zeros_like(stat_ref)
        stat_ref[0:1, :] = total_row(zacc[0])
        stat_ref[1:2, :] = total_row(zacc[1])
        stat_ref[2:3, :] = jnp.full((1, 128), pixels, f32)


def cross_body(x_ref, z_ref, xz_ref, acc):
    step = pl.program_id(0)
    tall, columns, images = x_ref.shape[:3]
    area = columns * images

    @pl.when(step == 0)
    def _():
        acc[...] = jnp.zeros_like(acc)

    for r in range(tall):
        z = z_ref[r].astype(bf16).reshape(area, 128)
        acc[...] += dot_tn(z, x_ref[r].reshape(area, 512))

    @pl.when(step == pl.num_programs(0) - 1)
    def _():
        for i in range(4):
            xz_ref[i * 128 : (i + 1) * 128, :] = acc[:, i * 128 : (i + 1) * 128]


def paired_weights(w_ref, target):
    for r in range(4):
        for u in range(3):
            for o in range(2):
                t = r - o
                base = (r * 3 + u) * 128
                if 0 <= t <= 2:
                    block = w_ref[t, u]
                else:
                    block = jnp.zeros((128, 128), bf16)
                target[base : base + 128, o * 128 : (o + 1) * 128] = block


def window(frame, pair):
    columns, images = frame.shape[1] - 2, frame.shape[2]
    parts = [
        frame[2 * pair + r, u : u + columns].reshape(columns * images, 128)
        for r in range(4)
        for u in range(3)
    ]
    return jnp.concatenate(parts, axis=1)


def clear_frame(frame):
    tall, wide_columns = frame.shape[:2]
    zero = jnp.zeros(frame.shape[2:], frame.dtype)
    for e in range(tall):
        frame[e, 0] = zero
        frame[e, wide_columns - 1] = zero
    for c in range(wide_columns):
        frame[0, c] = zero
        frame[tall - 1, c] = zero


def middle_body(
    info, st1, ga, sa, z_ref, edge_ref, w_ref, xz_ref,
    z2_ref, a_ref, stat_ref, frame, wide_w, coef, zacc,
):
    step = pl.program_id(0)
    last = pl.num_programs(0) - 1
    columns, images = z_ref.shape[1:3]
    area = columns * images

    def activated(z):
        return gelu_value(z * coef[0:1, :] + coef[1:2, :]).astype(bf16)

    @pl.when(step == 0)
    def _():
        mean, inv = moments(st1[0:1, :], st1[1:2, :], st1[2:3, :])
        scale = ga[...] * inv
        coef[0:1, :] = scale
        coef[1:2, :] = sa[...] - mean * scale
        paired_weights(w_ref, wide_w)
        zacc[...] = jnp.zeros_like(zacc)
        clear_frame(frame)
        place = (1 - info[1]) * (frame.shape[0] - 1)
        for c, n in groups(columns):
            frame[place, 1 + c : 1 + c + n] = activated(edge_ref[c : c + n])

    @pl.when(step < last)
    def _():
        for r in range(2):
            for c, n in groups(columns):
                value = activated(z_ref[r, c : c + n])
                frame[2 * step + 1 + r, 1 + c : 1 + c + n] = value
                a_ref[r, c : c + n] = value

    @pl.when(step > 0)
    def _():
        mask = live(info, images, 128)
        y = dot(window(frame, step - 1), wide_w[...])
        for r in range(2):
            z = y[:, r * 128 : (r + 1) * 128].reshape(columns, images, 128)
            z2_ref[r] = z
            zacc[0] += fold8(jnp.where(mask, jnp.sum(z, axis=0), 0.0))
            zacc[1] += fold8(jnp.where(mask, jnp.sum(z * z, axis=0), 0.0))

    @pl.when(step == last)
    def _():
        stat_ref[...] = jnp.zeros_like(stat_ref)
        for k in range(2):
            stat_ref[k : k + 1, :] = total_row(zacc[k])


def second_coef(st1, st2, gb, sb, coef):
    mean, inv = moments(st2[0:1, :], st2[1:2, :], st1[2:3, :])
    scale = gb[...] * inv
    coef[0:1, :] = scale
    coef[1:2, :] = sb[...] - mean * scale
    coef[2:3, :] = inv
    coef[3:4, :] = -mean * inv


def second_body(
    info, st1, st2, gb, sb, z_ref, wo_ref,
    act_ref, g_ref, gx_ref, ye_ref, ze_ref, st_ref, keep_ref, gram_ref, coef, cross, sums,
):
    step = pl.program_id(0)
    tall, columns, images = z_ref.shape[:3]
    area = columns * images

    @pl.when(step == 0)
    def _():
        second_coef(st1, st2, gb, sb, coef)
        cross[...] = jnp.zeros_like(cross)
        sums[...] = jnp.zeros_like(sums)

    mask = live(info, images, 128)
    scale, bias, inv, shift = (coef[i : i + 1, :] for i in range(4))
    edge_row = (1 - info[1]) * (tall - 1)
    at_edge = step == (1 - info[1]) * (pl.num_programs(0) - 1)
    totals = [jnp.zeros((images, 128), f32) for _ in range(3)]
    for r in range(tall):
        acts, others = [], []
        for c, n in groups(columns):
            z = z_ref[r, c : c + n]
            value, slope = gelu_terms(z * scale + bias)
            dotted = slope * (z * inv + shift)
            slope, dotted, value = (v.astype(bf16) for v in (slope, dotted, value))
            for k, part in enumerate((slope, dotted, value)):
                totals[k] += jnp.sum(part.astype(f32), axis=0)
            g_ref[r, c : c + n] = slope
            gx_ref[r, c : c + n] = dotted
            act_ref[r, c : c + n] = value
            value = jnp.where(mask, value, jnp.zeros((), bf16))
            acts.append(value.reshape(n * images, 128))
        acts = jnp.concatenate(acts, axis=0)
        cross[...] += dot_tn(
            acts,
            jnp.concatenate(
                [acts, g_ref[r].reshape(area, 128), gx_ref[r].reshape(area, 128)], axis=1
            ),
        )

        @pl.when(at_edge & (edge_row == r))
        def _():
            ye_ref[:, :, 0:128] = act_ref[r]
            ye_ref[:, :, 128:256] = g_ref[r]
            ze_ref[...] = z_ref[r]

    for k in range(3):
        sums[k] += fold8(jnp.where(mask, totals[k], 0.0))

    @pl.when(step == pl.num_programs(0) - 1)
    def _():
        gram = cross[:, 0:128]
        gram_ref[0:128, :] = gram
        st_ref[8:16, :] = jnp.zeros((8, 128), f32)
        st_ref[8:9, :] = total_row(sums[2])
        gram_ref[128:136, :] = st_ref[8:16, :]
        spread = dot_halves(gram_ref[...], wo_ref[...])
        put_wide(st_ref, 0, spread[128:129, :])
        put_wide(st_ref, 4, total_row(spread[0:128, :] * wo_ref[...].astype(f32)))
        st_ref[9:16, :] = jnp.zeros((7, 128), f32)
        for k in range(2):
            st_ref[9 + k : 10 + k, :] = total_row(sums[k])
        low = info[1] == 0
        keep_ref[...] = jnp.where(low, cross[:, 128:256], cross[:, 256:384])
        st_ref[16:144, :] = jnp.where(low, cross[:, 256:384], cross[:, 128:256])


def spread_body(head_ref, arrived_ref, keep_ref, out_ref):
    sums = head_ref[0:16, :] + arrived_ref[0:16, :]
    share = 128 // out_ref.shape[0]
    for k in range(out_ref.shape[0]):
        rows = slice(k * share, (k + 1) * share)
        out_ref[k, 0:16] = sums
        out_ref[k, 16 : 16 + share] = keep_ref[rows, :] + arrived_ref[16 + k * share : 16 + (k + 1) * share, :]
        if share < 8:
            out_ref[k, 16 + share :] = jnp.zeros((8 - share, 128), f32)


def both_body(info, own_ref, arrived_ref, out_ref):
    sums = own_ref[0:16, :] + arrived_ref[0:16, :]
    mine, other = own_ref[16:, :], arrived_ref[16:, :]
    low = info[1] == 0
    block = jnp.concatenate(
        [sums, jnp.where(low, mine, other), jnp.where(low, other, mine)], axis=0
    )
    for k in range(out_ref.shape[0]):
        out_ref[k] = block


def last_body(
    info, st1, in3, gc, sc, y_ref, g_ref, gx_ref, x_ref, cot_ref, wo_ref,
    out_ref, e_ref, t_ref, te_ref, st_ref, st3, u_ref, ws_ref,
    coef, w_two, w_turn, z_buf, cross, sums, sums_b,
):
    step = pl.program_id(0)
    tall, columns, images = x_ref.shape[:3]
    area = columns * images

    @pl.when(step == 0)
    def _():
        total = in3[0]
        for k in range(1, in3.shape[0]):
            total = total + in3[k]
        st3[...] = total[0:16]
        st_ref[16:, :] = total[16:]
        mean, inv = moments(wide(st3, 0), wide(st3, 4), st1[2:3, 0:1])
        scale = gc[...] * inv
        coef[0:1, :] = sc[...] - mean * scale
        high, low = split_two(wo_ref[...].astype(f32) * scale)
        w_two[0:128, :] = high
        w_two[128:256, :] = low
        ws_ref[...] = w_two[...]
        w_turn[:, 0:128] = jnp.transpose(w_two[0:128, :])
        w_turn[:, 128:256] = jnp.transpose(w_two[128:256, :])
        cross[...] = jnp.zeros_like(cross)
        sums[...] = jnp.zeros_like(sums)
        sums_b[...] = jnp.zeros_like(sums_b)

    mask = live(info, images, 512)
    bias = coef[0:1, :]
    zero = jnp.zeros((), bf16)
    piece = columns // 4
    parts = [(r, c) for r in range(tall) for c in range(0, columns, piece)]
    n = piece * images

    def product(r, c):
        act = y_ref[r, c : c + piece].reshape(n, 128)
        z = dot(jnp.concatenate([act, act], axis=1), w_two[...])
        z_buf[r, c : c + piece] = z.reshape(piece, images, 512)

    def pointwise(r, c):
        x = jnp.where(mask, x_ref[r, c], zero).astype(f32)
        value, slope = gelu_terms(z_buf[r, c] + (bias + x))
        out_ref[r, c] = value.astype(bf16)
        cot = jnp.where(mask, cot_ref[r, c], zero).astype(f32)
        e = slope * cot
        e_ref[r, c] = e.astype(bf16)
        return fold8(e), fold8(x)

    def collect(r, c):
        e = e_ref[r, c : c + piece].reshape(n, 512)
        cross[...] += dot_tn(y_ref[r, c : c + piece].reshape(n, 128), e)

    def through(r, c):
        y = dot(e_ref[r, c : c + piece].reshape(n, 512), w_turn[...])
        t = (y[:, 0:128] + y[:, 128:256]).reshape(piece, images, 128)
        t_ref[r, c : c + piece] = t.astype(bf16)
        sums_b[0] += fold8(t * g_ref[r, c : c + piece].astype(f32))
        sums_b[1] += fold8(t * gx_ref[r, c : c + piece].astype(f32))

    product(*parts[0])
    for k in range(len(parts) + 1):
        work = []
        if k + 1 < len(parts):
            work.append(functools.partial(product, *parts[k + 1]))
        if k > 0:
            work.append(functools.partial(through, *parts[k - 1]))
            work.append(functools.partial(collect, *parts[k - 1]))
        if k < len(parts):
            r, first = parts[k]
            total_e = jnp.zeros((8, 512), f32)
            total_x = jnp.zeros((8, 512), f32)
            for c in range(piece):
                if c % 2 == 0 and work:
                    work.pop(0)()
                add_e, add_x = pointwise(r, first + c)
                total_e += add_e
                total_x += add_x
            sums[0] += total_e
            sums[1] += total_x
        for rest in work:
            rest()
    take_edge(info, te_ref, t_ref)

    @pl.when(step == pl.num_programs(0) - 1)
    def _():
        u_ref[...] = cross[...]
        put_wide(st_ref, 0, total_row(sums[0]))
        put_wide(st_ref, 4, total_row(wo_ref[...].astype(f32) * cross[...]))
        put_wide(st_ref, 10, total_row(sums[1]))
        for k in range(2):
            st_ref[8 + k : 9 + k, :] = total_row(sums_b[k])
            st_ref[14 + k : 15 + k, :] = jnp.zeros((1, 128), f32)


def back_body(
    info, st1, st2, st3, in4, own4, xz_ref, gram_ref, u_ref, ga, sa, gb, gc, wo_ref, ws_ref, wt_ref,
    y_ref, s_ref, ye_ref, z2_ref, ze_ref, t_ref, te_ref, a_ref, z1_ref, x_ref,
    h_ref, mine_ref, sent_ref, small_ref,
    coef, mm, wide_w, frame, dacc, vacc, sums, packed, st4, pq,
):
    step = pl.program_id(0)
    last = pl.num_programs(0) - 1
    columns, images = z1_ref.shape[1:3]
    area = columns * images
    mask = live(info, images, 128)

    def second_back(t, product, slope, z):
        kappa, scale_b, beta, alpha = (coef[i : i + 1, :] for i in range(4))
        through = t.astype(f32) - kappa - product[..., 0:128] - product[..., 128:256]
        grad = scale_b * (slope.astype(f32) * through) - (alpha + beta * z)
        return jnp.where(mask, grad, 0.0).astype(bf16)

    @pl.when(step == 0)
    def _():
        pixels = st1[2:3, :]
        pixel = st1[2:3, 0:1]
        mean_a, inv_a = moments(st1[0:1, :], st1[1:2, :], pixels)
        mean_b, inv_b = moments(st2[0:1, :], st2[1:2, :], pixels)
        mean_c, inv_c = moments(wide(st3, 0), wide(st3, 4), pixel)
        total = in4[0, 0:16]
        share = 128 // in4.shape[0]
        span = (in4.shape[1] - 16) // 2
        for k in range(in4.shape[0]):
            if k > 0:
                total = total + in4[k, 0:16]
            rows = slice(k * share, (k + 1) * share)
            pq[0, rows] = in4[k, 16 : 16 + share]
            pq[1, rows] = in4[k, 16 + span : 16 + span + share]
        st4[...] = total
        total_c = wide(st4, 0)
        dot_c = inv_c * (wide(st4, 4) - mean_c * total_c)
        weights = wo_ref[...].astype(f32)
        scaled = ws_ref[0:128, :].astype(f32) + ws_ref[128:256, :].astype(f32)
        near, far = split_two(weights * (inv_c * dot_c / pixel))
        mat = dot_nt(near, ws_ref[0:128, :]) + dot_nt(near, ws_ref[128:256, :])
        mat = mat + dot_nt(far, ws_ref[0:128, :])
        high, low = split_two(mat)
        mm[:, 0:128] = high
        mm[:, 128:256] = low
        kappa = row_of_sums(scaled * (total_c / pixel))[0:1, :]
        mean_act = jnp.transpose(jnp.broadcast_to(st3[8:9, :] / pixels, (8, 128)))[:, 0:1]
        kappa = kappa - total_row(mean_act * mat)
        total_b = st4[8:9, :] - kappa * st3[9:10, :] - total_row(mat * pq[0])
        dot_b = st4[9:10, :] - kappa * st3[10:11, :] - total_row(mat * pq[1])
        scale_b = gb[...] * inv_b
        scale_a = ga[...] * inv_a
        coef[0:1, :] = kappa
        coef[1:2, :] = scale_b
        coef[2:3, :] = scale_b * inv_b * dot_b / pixels
        coef[3:4, :] = scale_b * (total_b - mean_b * inv_b * dot_b) / pixels
        coef[4:5, :] = scale_a
        coef[5:6, :] = sa[...] - mean_a * scale_a
        small_ref[...] = jnp.zeros_like(small_ref)
        put_wide(small_ref, 0, total_c)
        put_wide(small_ref, 4, dot_c)
        small_ref[8:9, :] = total_b
        small_ref[9:10, :] = dot_b
        column = jnp.transpose(gram_ref[128:136, :])[:, 0:1]
        product = dot_halves(gram_ref[0:128, :], wo_ref[...])
        grad = u_ref[...] - column * (total_c / pixel) - (product - column * mean_c) * (
            inv_c * dot_c / pixel
        )
        grad = grad * (gc[...] * inv_c)
        for i in range(4):
            packed[1152 + i * 128 : 1280 + i * 128, :] = grad[:, i * 128 : (i + 1) * 128]
        paired_weights(wt_ref, wide_w)
        dacc[...] = jnp.zeros_like(dacc)
        vacc[...] = jnp.zeros_like(vacc)
        sums[...] = jnp.zeros_like(sums)
        clear_frame(frame)
        place = (1 - info[1]) * (frame.shape[0] - 1)
        for c, n in groups(columns):
            act = ye_ref[c : c + n, :, 0:128].reshape(n * images, 128)
            extra = dot(act, mm[...]).reshape(n, images, 256)
            frame[place, 1 + c : 1 + c + n] = second_back(
                te_ref[c : c + n], extra, ye_ref[c : c + n, :, 128:256], ze_ref[c : c + n]
            )

    @pl.when(step < last)
    def _():
        for r in range(2):
            act = y_ref[r].reshape(area, 128)
            extra = dot(act, mm[...]).reshape(columns, images, 256)
            for c, n in groups(columns):
                frame[2 * step + 1 + r, 1 + c : 1 + c + n] = second_back(
                    t_ref[r, c : c + n],
                    extra[c : c + n],
                    s_ref[r, c : c + n],
                    z2_ref[r, c : c + n],
                )

    @pl.when(step > 0)
    def _():
        scale_a, bias_a = coef[4:5, :], coef[5:6, :]
        near = window(frame, step - 1)
        through = dot(near, wide_w[...])
        act = jnp.concatenate([a_ref[r].reshape(area, 128) for r in range(2)], axis=1)
        dacc[...] += dot_tn(act, near)
        total = jnp.zeros((8, 128), f32)
        dots = jnp.zeros((8, 128), f32)
        for r in range(2):
            part = through[:, r * 128 : (r + 1) * 128].reshape(columns, images, 128)
            for c, n in groups(columns):
                z = z1_ref[r, c : c + n]
                slope = gelu_terms(z * scale_a + bias_a)[1]
                grad = part[c : c + n] * slope
                total += fold8(grad)
                dots += fold8(grad * z)
                h_ref[r, c : c + n] = grad.astype(bf16)
        sums[0] += total
        sums[1] += dots
        vacc[...] += dot_tn(h_ref[...].reshape(2 * area, 128), x_ref[...].reshape(2 * area, 512))

    @pl.when(step == last)
    def _():
        pixels = st1[2:3, :]
        total_h, dot_h = total_row(sums[0]), total_row(sums[1])
        tail = jnp.concatenate(
            [total_h, dot_h, st1[0:1, :] / pixels, jnp.zeros((5, 128), f32)], axis=0
        )
        columns2 = jnp.transpose(tail)
        column_h, mean_a = columns2[:, 0:1], columns2[:, 2:3]
        for i in range(4):
            lanes = slice(i * 128, (i + 1) * 128)
            center = st4[10 + i : 11 + i, :] / pixels
            packed[1664 + i * 128 : 1792 + i * 128, :] = vacc[:, lanes] - column_h * center
            packed[2176 + i * 128 : 2304 + i * 128, :] = (
                xz_ref[lanes, :] - mean_a * own4[10 + i : 11 + i, :]
            )
        for t in range(3):
            for u in range(3):
                parts = []
                for o in range(2):
                    base = ((o + 2 - t) * 3 + 2 - u) * 128
                    parts.append(dacc[o * 128 : (o + 1) * 128, base : base + 128])
                packed[(t * 3 + u) * 128 : (t * 3 + u + 1) * 128, :] = parts[0] + parts[1]
        if packed.shape[0] > 2688:
            packed[2688:, :] = jnp.zeros((packed.shape[0] - 2688, 128), f32)
        half = packed.shape[0] // 2
        low = info[1] == 0
        mine_ref[0:half, :] = jnp.where(low, packed[0:half, :], packed[half:, :])
        sent_ref[0:half, :] = jnp.where(low, packed[half:, :], packed[0:half, :])
        mine_ref[half : half + 8, :] = tail
        sent_ref[half : half + 8, :] = tail


def pack_body(mine_ref, arrived_ref, out_ref):
    shares, block = out_ref.shape[:2]
    share = (mine_ref.shape[0] - 8) // shares
    small = mine_ref[shares * share :, :] + arrived_ref[shares * share :, :]
    high = small.astype(bf16).astype(f32)
    middle = (small - high).astype(bf16).astype(f32)
    low = small - high - middle
    tail = jnp.concatenate(
        [high[0:2], middle[0:2], low[0:2], jnp.zeros((block - share - 6, 128), f32)], axis=0
    )
    for k in range(shares):
        rows = slice(k * share, (k + 1) * share)
        total = mine_ref[rows, :] + arrived_ref[rows, :]
        out_ref[k] = jnp.concatenate([total, tail], axis=0).astype(bf16)


def share_body(share, in_ref, small_ref, out_ref):
    total = in_ref[0].astype(f32)
    for k in range(1, in_ref.shape[0]):
        total = total + in_ref[k].astype(f32)
    sums = total[share : share + 2] + total[share + 2 : share + 4] + total[share + 4 : share + 6]
    small_ref[...] = jnp.concatenate([sums, jnp.zeros((6, 128), f32)], axis=0)
    for k in range(out_ref.shape[0]):
        out_ref[k] = total.astype(bf16)


def input_body(info, st1, st5, ga, wi_ref, h_ref, z_ref, e_ref, g_ref, coef, w_turn):
    step = pl.program_id(0)
    tall, columns, images = z_ref.shape[:3]
    area = columns * images

    @pl.when(step == 0)
    def _():
        pixels = st1[2:3, :]
        mean, inv = moments(st1[0:1, :], st1[1:2, :], pixels)
        scale = ga[...] * inv
        w_turn[...] = jnp.transpose(wi_ref[...])
        total = st5[0:1, :]
        dot_a = inv * (st5[1:2, :] - mean * total)
        coef[0:1, :] = scale
        coef[1:2, :] = scale * inv * dot_a / pixels
        coef[2:3, :] = scale * (total - mean * inv * dot_a) / pixels

    mask = live(info, images, 128)
    scale, beta, alpha = (coef[i : i + 1, :] for i in range(3))
    for r in range(tall):
        parts = []
        for c, n in groups(columns):
            grad = scale * h_ref[r, c : c + n].astype(f32) - (alpha + beta * z_ref[r, c : c + n])
            parts.append(jnp.where(mask, grad, 0.0).astype(bf16).reshape(n * images, 128))
        through = dot(jnp.concatenate(parts, axis=0), w_turn[...])
        through = through.reshape(columns, images, 512)
        for c in range(columns):
            g_ref[r, c] = (through[c] + e_ref[r, c].astype(f32)).astype(bf16)


def final_body(
    share, info, st1, st5, ga, small_ref, mine_ref, other_ref,
    gwi_ref, gga_ref, gsa_ref, gwm_ref, ggb_ref, gsb_ref, gwo_ref, ggc_ref, gsc_ref, total_ref,
):
    shares = mine_ref.shape[0]
    for k in range(shares):
        mine, other = mine_ref[k].astype(f32), other_ref[k].astype(f32)
        low = jnp.where(info[1] == 0, mine, other)
        high = jnp.where(info[1] == 0, other, mine)
        total_ref[k * share : (k + 1) * share, :] = low[0:share]
        total_ref[(shares + k) * share : (shares + k + 1) * share, :] = high[0:share]
    pixels = st1[2:3, :]
    mean, inv = moments(st1[0:1, :], st1[1:2, :], pixels)
    total = st5[0:1, :]
    dot = inv * (st5[1:2, :] - mean * total)
    gsa_ref[...] = total
    gga_ref[...] = dot
    gsb_ref[...] = small_ref[8:9, :]
    ggb_ref[...] = small_ref[9:10, :]
    gsc_ref[...] = wide(small_ref, 0)
    ggc_ref[...] = wide(small_ref, 4)
    gwm_ref[...] = total_ref[0:1152, :]
    for i in range(4):
        gwo_ref[:, i * 128 : (i + 1) * 128] = total_ref[1152 + i * 128 : 1280 + i * 128, :]
        v = jnp.transpose(total_ref[1664 + i * 128 : 1792 + i * 128, :])
        xz = jnp.transpose(total_ref[2176 + i * 128 : 2304 + i * 128, :])
        gwi_ref[i * 128 : (i + 1) * 128, :] = (ga[...] * inv) * (v - xz * (inv * dot / pixels))


def local(
    images, counts, w_in, gain_a, shift_a, w_mid, gain_b, shift_b, w_out, gain_c, shift_c, cotangent
):
    count, rows, columns, channels = images.shape
    steps = rows // 2
    info = jnp.stack([counts[0], lax.axis_index("rows").astype(jnp.int32)])
    images = jnp.transpose(images, (1, 2, 0, 3))
    cotangent = jnp.transpose(cotangent, (1, 2, 0, 3))
    ga, sa, gb, sb = (v.reshape(1, 128) for v in (gain_a, shift_a, gain_b, shift_b))
    gc, sc = gain_c.reshape(1, 512), shift_c.reshape(1, 512)
    small = whole_spec((1, 128))
    large = whole_spec((1, 512))
    eight = whole_spec((8, 128))
    taps = whole_spec((3, 3, 128, 128))

    def tile(lanes):
        return (2, columns, count, lanes)

    def edge(lanes):
        return (columns, count, lanes)

    def ahead(i):
        return jnp.minimum(i, steps - 1)

    def behind(i):
        return jnp.maximum(i - 1, 0)

    def frame_like():
        return pltpu.VMEM((rows + 2, columns + 2, count, 128), bf16)

    pixels = count * rows * columns

    z1, z1_edge, st1 = call(
        first_body,
        steps,
        [SMEM, step_spec(tile(512)), whole_spec((512, 128))],
        [
            step_out(rows, tile(128), f32),
            whole_out(edge(128)),
            whole_out((8, 128)),
        ],
        [pltpu.VMEM((2, 8, 128), f32)],
        "first_norm_sums",
        pixels * 512 * 128 * 2,
        pixels * 1536,
    )(info, images, w_in)
    z1_edge = partner(z1_edge, 1)
    st1 = summed_at_once(st1)
    xz = call(
        cross_body,
        steps,
        [step_spec(tile(512)), step_spec(tile(128))],
        [whole_out((512, 128))],
        [pltpu.VMEM((128, 512), f32)],
        "input_cross",
        pixels * 512 * 128 * 2,
        pixels * 1536,
    )(images, z1)[0]
    w_back = jnp.swapaxes(w_mid[::-1, ::-1], 2, 3)
    xz, w_back = lax.optimization_barrier((xz, w_back))

    shares = lax.axis_size("batch")
    span = max(8, 128 // shares)
    everyone = [list(range(lax.axis_size("batch")))]
    z2, act_a, st2 = call(
        middle_body,
        steps + 1,
        [
            SMEM, eight, small, small, step_spec(tile(128), ahead), whole_spec(edge(128)), taps,
            whole_spec((512, 128)),
        ],
        [
            step_out(rows, tile(128), f32, behind),
            step_out(rows, tile(128), bf16, ahead),
            whole_out((8, 128)),
        ],
        [
            frame_like(),
            pltpu.VMEM((1536, 256), bf16),
            pltpu.VMEM((8, 128), f32),
            pltpu.VMEM((2, 8, 128), f32),
        ],
        "middle_conv",
        pixels * 12 * 128 * 128 * 2,
        pixels * 1280,
    )(info, st1, ga, sa, z1, z1_edge, w_mid, xz)
    st2 = summed_by_swap(st2)

    act_b, slope_b, dotted_b, y_edge, z2_edge, head, kept, gram = call(
        second_body,
        steps,
        [SMEM, eight, eight, small, small, step_spec(tile(128)), whole_spec((128, 512))],
        [
            step_out(rows, tile(128), bf16),
            step_out(rows, tile(128), bf16),
            step_out(rows, tile(128), bf16),
            whole_out(edge(256), bf16),
            whole_out(edge(128)),
            whole_out((144, 128)),
            whole_out((128, 128)),
            whole_out((136, 128)),
        ],
        [pltpu.VMEM((8, 128), f32), pltpu.VMEM((128, 384), f32), pltpu.VMEM((3, 8, 128), f32)],
        "second_norm",
        pixels * 384 * 128 * 2,
        pixels * 1280,
        20,
    )(info, st1, st2, gb, sb, z2, w_out)
    arrived3 = swapped(
        call(
            spread_body,
            1,
            [whole_spec((144, 128)), whole_spec((144, 128)), whole_spec((128, 128))],
            [whole_out((shares, 16 + span, 128))],
            [],
            "spread_third",
            1e5,
            1e6,
        )(head, partner(head, 1), kept)[0]
    )

    block_out, e, t, t_edge, own4, st3, u_local, w_scaled = call(
        last_body,
        steps,
        [
            SMEM, eight, whole_spec((shares, 16 + span, 128)), large, large, step_spec(tile(128)),
            step_spec(tile(128)), step_spec(tile(128)), step_spec(tile(512)),
            step_spec(tile(512)), whole_spec((128, 512)),
        ],
        [
            step_out(rows, tile(512), bf16),
            step_out(rows, tile(512), bf16),
            step_out(rows, tile(128), bf16),
            whole_out(edge(128), bf16),
            whole_out((16 + span, 128)),
            whole_out((16, 128)),
            whole_out((128, 512)),
            whole_out((256, 512), bf16),
        ],
        [
            pltpu.VMEM((8, 512), f32),
            pltpu.VMEM((256, 512), bf16),
            pltpu.VMEM((512, 256), bf16),
            pltpu.VMEM(tile(512), f32),
            pltpu.VMEM((128, 512), f32),
            pltpu.VMEM((2, 8, 512), f32),
            pltpu.VMEM((2, 8, 128), f32),
        ],
        "last_norm",
        pixels * 512 * 128 * 10,
        pixels * 4864,
        36,
    )(info, st1, arrived3, gc, sc, act_b, slope_b, dotted_b, images, cotangent, w_out)

    other4, y_edge, z2_edge, t_edge = lax.optimization_barrier(
        tuple(
            partner(v, 1)
            for v in lax.optimization_barrier((own4, y_edge, z2_edge, t_edge))
        )
    )
    arrived4 = swapped(
        call(
            both_body,
            1,
            [SMEM, whole_spec((16 + span, 128)), whole_spec((16 + span, 128))],
            [whole_out((shares, 16 + 2 * span, 128))],
            [],
            "spread_fourth",
            1e5,
            1e6,
        )(info, own4, other4)[0]
    )

    share = -(-1344 // (8 * shares)) * 8
    half = share * shares
    block = -(-(share + 6) // 16) * 16
    h, mine, sent, small_sums = call(
        back_body,
        steps + 1,
        [
            SMEM, eight, eight, whole_spec((16, 128)), whole_spec((shares, 16 + 2 * span, 128)),
            whole_spec((16 + span, 128)),
            whole_spec((512, 128)), whole_spec((136, 128)),
            whole_spec((128, 512)), small, small, small, large, whole_spec((128, 512)),
            whole_spec((256, 512)), taps,
            step_spec(tile(128), ahead), step_spec(tile(128), ahead), whole_spec(edge(256)),
            step_spec(tile(128), ahead), whole_spec(edge(128)),
            step_spec(tile(128), ahead), whole_spec(edge(128)),
            step_spec(tile(128), behind), step_spec(tile(128), behind),
            step_spec(tile(512), behind),
        ],
        [
            step_out(rows, tile(128), bf16, behind),
            whole_out((half + 8, 128)),
            whole_out((half + 8, 128)),
            whole_out((16, 128)),
        ],
        [
            pltpu.VMEM((8, 128), f32),
            pltpu.VMEM((128, 256), bf16),
            pltpu.VMEM((1536, 256), bf16),
            frame_like(),
            pltpu.VMEM((256, 1536), f32),
            pltpu.VMEM((128, 512), f32),
            pltpu.VMEM((2, 8, 128), f32),
            pltpu.VMEM((2 * half, 128), f32),
            pltpu.VMEM((16, 128), f32),
            pltpu.VMEM((2, 128, 128), f32),
        ],
        "middle_back",
        pixels * 32 * 128 * 128 * 2,
        pixels * 4000,
        49,
    )(
        info, st1, st2, st3, arrived4, own4, xz, gram, u_local, ga, sa, gb, gc,
        w_out, w_scaled, w_back,
        act_b, slope_b, y_edge, z2, z2_edge, t, t_edge, act_a, z1, images,
    )
    arrived = partner(sent, 1)
    spread = call(
        pack_body,
        1,
        [whole_spec((half + 8, 128)), whole_spec((half + 8, 128))],
        [whole_out((shares, block, 128), bf16)],
        [],
        "pack_shares",
        1e6,
        2e6,
    )(mine, arrived)[0]
    spread = swapped(spread)
    st5, spread = call(
        functools.partial(share_body, share),
        1,
        [whole_spec((shares, block, 128))],
        [whole_out((8, 128)), whole_out((shares, block, 128), bf16)],
        [],
        "sum_shares",
        1e6,
        1e6,
    )(spread)
    gathered = swapped(spread)

    grad_images = call(
        input_body,
        steps,
        [
            SMEM, eight, eight, small, whole_spec((512, 128)),
            step_spec(tile(128)), step_spec(tile(128)), step_spec(tile(512)),
        ],
        [step_out(rows, tile(512), bf16)],
        [pltpu.VMEM((8, 128), f32), pltpu.VMEM((128, 512), bf16)],
        "input_grad",
        pixels * 512 * 128 * 2,
        pixels * 2816,
    )(info, st1, st5, ga, w_in, h, z1, e)[0]

    gathered, grad_images = lax.optimization_barrier((gathered, grad_images))
    shared = whole_spec((shares, block, 128))
    gwi, gga, gsa, gwm, ggb, gsb, gwo, ggc, gsc = call(
        functools.partial(final_body, share),
        1,
        [SMEM, eight, eight, small, whole_spec((16, 128)), shared, shared],
        [
            whole_out((512, 128)), whole_out((1, 128)), whole_out((1, 128)),
            whole_out((1152, 128)), whole_out((1, 128)), whole_out((1, 128)),
            whole_out((128, 512)), whole_out((1, 512)), whole_out((1, 512)),
        ],
        [pltpu.VMEM((2 * half, 128), f32)],
        "replicated_grads",
        1e6,
        3e6,
    )(info, st1, st5, ga, small_sums, gathered, partner(gathered, 1))
    return (
        jnp.transpose(block_out, (2, 0, 1, 3)),
        jnp.transpose(grad_images, (2, 0, 1, 3)),
        gwi,
        gga.reshape(128),
        gsa.reshape(128),
        gwm.reshape(3, 3, 128, 128),
        ggb.reshape(128),
        gsb.reshape(128),
        gwo,
        ggc.reshape(512),
        gsc.reshape(512),
    )


def solution(mesh):
    split = P("batch", "rows", None, None)
    placed = (split, P("batch"), P(), P(), P(), P(), P(), P(), P(), P(), P(), split)
    return jax.shard_map(
        local,
        mesh=mesh,
        in_specs=placed,
        out_specs=(split, split) + (P(),) * 9,
        check_vma=False,
    )
```

```python
import functools
import math

import jax
import jax.numpy as jnp
from jax import lax
from jax.experimental import pallas as pl
from jax.experimental.pallas import tpu as pltpu
from jax.sharding import PartitionSpec as P

epsilon = 1e-05
axes = ("batch", "rows")
f32 = jnp.float32
bf16 = jnp.bfloat16
C0 = math.sqrt(2.0 / math.pi)
C1 = C0 * 0.044715
K0 = -2.0 * C0 / math.log(2.0)
K1 = -2.0 * C1 / math.log(2.0)
K2 = -3.0 * math.log(2.0)
HIGH = lax.Precision.HIGHEST


def partner(block, mask):
    total = lax.axis_size("batch") * lax.axis_size("rows")
    return lax.ppermute(block, axes, [(i, i ^ mask) for i in range(total)])


def swapped_sum(block, groups):
    size = len(groups[0])
    spread = jnp.broadcast_to(block[None], (size,) + block.shape)
    arrived = lax.all_to_all(spread, "batch", 0, 0, axis_index_groups=groups, tiled=True)
    return jnp.sum(arrived, axis=0)


def swapped(spread):
    return lax.all_to_all(spread, "batch", 0, 0, tiled=True)


def summed_at_once(block):
    total = lax.axis_size("batch") * lax.axis_size("rows")
    spread = jnp.broadcast_to(block[None], (total,) + block.shape)
    return jnp.sum(lax.all_to_all(spread, axes, 0, 0, tiled=True), axis=0)


def summed_by_swap(block, near=None):
    block = block + partner(block, 1)
    count = lax.axis_size("batch")
    if near is None or count % near:
        return swapped_sum(block, [list(range(count))])
    block = swapped_sum(block, [list(range(i, i + near)) for i in range(0, count, near)])
    return swapped_sum(block, [list(range(i, count, near)) for i in range(near)])


def gate(u):
    inner = K0 + K1 * (u * u)
    return pltpu.reciprocal(1.0 + jnp.exp2(u * inner), approx=True), inner


def gelu_terms(u):
    half, inner = gate(u)
    value = u * half
    slope = half + value * (1.0 - half) * (K2 * inner - 4.0 * C0)
    return value, slope


def gelu_value(u):
    return u * gate(u)[0]


def moments(total, squares, pixels):
    mean = total / pixels
    return mean, lax.rsqrt(squares / pixels - mean * mean + epsilon)


def fold8(values):
    lanes = values.shape[-1]
    return jnp.sum(values.reshape(values.size // (8 * lanes), 8, lanes), axis=0)


def total_row(values):
    return jnp.sum(values, axis=0, keepdims=True)


def wide(ref, start):
    return jnp.concatenate([ref[start + i : start + i + 1, :] for i in range(4)], axis=1)


def put_wide(ref, start, row):
    for i in range(4):
        ref[start + i : start + i + 1, :] = row[:, i * 128 : (i + 1) * 128]


def dot_tn(a, b):
    return lax.dot_general(a, b, (((0,), (0,)), ((), ())), preferred_element_type=f32)


def dot_nt(a, b, precision=None):
    return lax.dot_general(
        a, b, (((1,), (1,)), ((), ())), preferred_element_type=f32, precision=precision
    )


def dot(a, b, precision=None):
    return jnp.dot(a, b, preferred_element_type=f32, precision=precision)


def split_two(values):
    high = values.astype(bf16)
    return high, (values - high.astype(f32)).astype(bf16)


def dot_halves(a, b):
    high, low = split_two(a)
    return dot(high, b) + dot(low, b)


def row_of_sums(values):
    high, low = split_two(values)
    one = jnp.ones((16, values.shape[1]), bf16)
    return (dot_nt(one, high) + dot_nt(one, low))[0:8, :]


def call(body, grid, ins, outs, scratch, name, flops, bytes_moved, vmem=52):
    return pl.pallas_call(
        body,
        grid=(grid,),
        in_specs=ins,
        out_specs=[spec for spec, _ in outs],
        out_shape=[shape for _, shape in outs],
        scratch_shapes=scratch,
        name=name,
        compiler_params=pltpu.CompilerParams(
            dimension_semantics=("arbitrary",), vmem_limit_bytes=vmem << 20
        ),
        cost_estimate=pl.CostEstimate(
            flops=int(flops), bytes_accessed=int(bytes_moved), transcendentals=0
        ),
    )


SMEM = pl.BlockSpec(memory_space=pltpu.SMEM)
ANY = pl.BlockSpec(memory_space=pl.ANY)


def whole_spec(shape):
    return pl.BlockSpec(tuple(shape), lambda i: (0,) * len(shape))


def step_spec(shape, place=lambda i: i):
    return pl.BlockSpec(tuple(shape), lambda i: (place(i),) + (0,) * (len(shape) - 1))


def whole_out(shape, dtype=f32):
    return (whole_spec(shape), jax.ShapeDtypeStruct(shape, dtype))


def step_out(count, shape, dtype, place=lambda i: i):
    return (
        step_spec(shape, place),
        jax.ShapeDtypeStruct((count,) + tuple(shape[1:]), dtype),
    )


def live(info, images, lanes):
    return lax.broadcasted_iota(jnp.int32, (images, lanes), 0) < info[0]


def groups(columns):
    return [(c, min(4, columns - c)) for c in range(0, columns, 4)]


def take_edge(info, edge_ref, ref):
    step = pl.program_id(0)

    @pl.when((step == 0) & (info[1] == 1))
    def _():
        edge_ref[...] = ref[0].astype(edge_ref.dtype)

    @pl.when((step == pl.num_programs(0) - 1) & (info[1] == 0))
    def _():
        edge_ref[...] = ref[ref.shape[0] - 1].astype(edge_ref.dtype)


def first_body(info, x_ref, w_ref, z_ref, edge_ref, stat_ref, zacc):
    step = pl.program_id(0)
    tall, columns, images = x_ref.shape[:3]
    area = columns * images

    @pl.when(step == 0)
    def _():
        zacc[...] = jnp.zeros_like(zacc)

    mask = live(info, images, 128)
    for r in range(tall):
        x = x_ref[r].reshape(area, 512)
        z = dot(x, w_ref[...]).reshape(columns, images, 128)
        z = jnp.where(mask, z, 0.0)
        z_ref[r] = z
        zacc[0] += fold8(z)
        zacc[1] += fold8(z * z)
    take_edge(info, edge_ref, z_ref)

    @pl.when(step == pl.num_programs(0) - 1)
    def _():
        pixels = (info[0] * (pl.num_programs(0) * tall * columns)).astype(f32)
        stat_ref[...] = jnp.zeros_like(stat_ref)
        stat_ref[0:1, :] = total_row(zacc[0])
        stat_ref[1:2, :] = total_row(zacc[1])
        stat_ref[2:3, :] = jnp.full((1, 128), pixels, f32)


def cross_body(x_ref, z_ref, xz_ref, acc):
    step = pl.program_id(0)
    tall, columns, images = x_ref.shape[:3]
    area = columns * images

    @pl.when(step == 0)
    def _():
        acc[...] = jnp.zeros_like(acc)

    for r in range(tall):
        z = z_ref[r].astype(bf16).reshape(area, 128)
        acc[...] += dot_tn(z, x_ref[r].reshape(area, 512))

    @pl.when(step == pl.num_programs(0) - 1)
    def _():
        for i in range(4):
            xz_ref[i * 128 : (i + 1) * 128, :] = acc[:, i * 128 : (i + 1) * 128]


def paired_weights(w_ref, target):
    for r in range(4):
        for u in range(3):
            for o in range(2):
                t = r - o
                base = (r * 3 + u) * 128
                if 0 <= t <= 2:
                    block = w_ref[t, u]
                else:
                    block = jnp.zeros((128, 128), bf16)
                target[base : base + 128, o * 128 : (o + 1) * 128] = block


def window(frame, pair):
    columns, images = frame.shape[1] - 2, frame.shape[2]
    parts = [
        frame[2 * pair + r, u : u + columns].reshape(columns * images, 128)
        for r in range(4)
        for u in range(3)
    ]
    return jnp.concatenate(parts, axis=1)


def clear_frame(frame):
    tall, wide_columns = frame.shape[:2]
    zero = jnp.zeros(frame.shape[2:], frame.dtype)
    for e in range(tall):
        frame[e, 0] = zero
        frame[e, wide_columns - 1] = zero
    for c in range(wide_columns):
        frame[0, c] = zero
        frame[tall - 1, c] = zero


def middle_body(
    info, st1, ga, sa, z_ref, edge_ref, w_ref, xz_ref,
    z2_ref, a_ref, stat_ref, frame, wide_w, coef, zacc,
):
    step = pl.program_id(0)
    last = pl.num_programs(0) - 1
    columns, images = z_ref.shape[1:3]
    area = columns * images

    def activated(z):
        return gelu_value(z * coef[0:1, :] + coef[1:2, :]).astype(bf16)

    @pl.when(step == 0)
    def _():
        mean, inv = moments(st1[0:1, :], st1[1:2, :], st1[2:3, :])
        scale = ga[...] * inv
        coef[0:1, :] = scale
        coef[1:2, :] = sa[...] - mean * scale
        paired_weights(w_ref, wide_w)
        zacc[...] = jnp.zeros_like(zacc)
        clear_frame(frame)
        place = (1 - info[1]) * (frame.shape[0] - 1)
        for c, n in groups(columns):
            frame[place, 1 + c : 1 + c + n] = activated(edge_ref[c : c + n])

    @pl.when(step < last)
    def _():
        for r in range(2):
            for c, n in groups(columns):
                value = activated(z_ref[r, c : c + n])
                frame[2 * step + 1 + r, 1 + c : 1 + c + n] = value
                a_ref[r, c : c + n] = value

    @pl.when(step > 0)
    def _():
        mask = live(info, images, 128)
        y = dot(window(frame, step - 1), wide_w[...])
        for r in range(2):
            z = y[:, r * 128 : (r + 1) * 128].reshape(columns, images, 128)
            z2_ref[r] = z
            zacc[0] += fold8(jnp.where(mask, jnp.sum(z, axis=0), 0.0))
            zacc[1] += fold8(jnp.where(mask, jnp.sum(z * z, axis=0), 0.0))

    @pl.when(step == last)
    def _():
        stat_ref[...] = jnp.zeros_like(stat_ref)
        for k in range(2):
            stat_ref[k : k + 1, :] = total_row(zacc[k])


def second_coef(st1, st2, gb, sb, coef):
    mean, inv = moments(st2[0:1, :], st2[1:2, :], st1[2:3, :])
    scale = gb[...] * inv
    coef[0:1, :] = scale
    coef[1:2, :] = sb[...] - mean * scale
    coef[2:3, :] = inv
    coef[3:4, :] = -mean * inv


def second_body(
    info, st1, st2, gb, sb, z_ref, wo_ref,
    act_ref, g_ref, gx_ref, ye_ref, ze_ref, st_ref, keep_ref, gram_ref, coef, cross, sums,
):
    step = pl.program_id(0)
    tall, columns, images = z_ref.shape[:3]
    area = columns * images

    @pl.when(step == 0)
    def _():
        second_coef(st1, st2, gb, sb, coef)
        cross[...] = jnp.zeros_like(cross)
        sums[...] = jnp.zeros_like(sums)

    mask = live(info, images, 128)
    scale, bias, inv, shift = (coef[i : i + 1, :] for i in range(4))
    edge_row = (1 - info[1]) * (tall - 1)
    at_edge = step == (1 - info[1]) * (pl.num_programs(0) - 1)
    totals = [jnp.zeros((images, 128), f32) for _ in range(3)]
    for r in range(tall):
        acts, others = [], []
        for c, n in groups(columns):
            z = z_ref[r, c : c + n]
            value, slope = gelu_terms(z * scale + bias)
            dotted = slope * (z * inv + shift)
            slope, dotted, value = (v.astype(bf16) for v in (slope, dotted, value))
            for k, part in enumerate((slope, dotted, value)):
                totals[k] += jnp.sum(part.astype(f32), axis=0)
            g_ref[r, c : c + n] = slope
            gx_ref[r, c : c + n] = dotted
            act_ref[r, c : c + n] = value
            value = jnp.where(mask, value, jnp.zeros((), bf16))
            acts.append(value.reshape(n * images, 128))
        acts = jnp.concatenate(acts, axis=0)
        cross[...] += dot_tn(
            acts,
            jnp.concatenate(
                [acts, g_ref[r].reshape(area, 128), gx_ref[r].reshape(area, 128)], axis=1
            ),
        )

        @pl.when(at_edge & (edge_row == r))
        def _():
            ye_ref[:, :, 0:128] = act_ref[r]
            ye_ref[:, :, 128:256] = g_ref[r]
            ze_ref[...] = z_ref[r]

    for k in range(3):
        sums[k] += fold8(jnp.where(mask, totals[k], 0.0))

    @pl.when(step == pl.num_programs(0) - 1)
    def _():
        gram = cross[:, 0:128]
        gram_ref[0:128, :] = gram
        st_ref[8:16, :] = jnp.zeros((8, 128), f32)
        st_ref[8:9, :] = total_row(sums[2])
        gram_ref[128:136, :] = st_ref[8:16, :]
        spread = dot_halves(gram_ref[...], wo_ref[...])
        put_wide(st_ref, 0, spread[128:129, :])
        put_wide(st_ref, 4, total_row(spread[0:128, :] * wo_ref[...].astype(f32)))
        st_ref[9:16, :] = jnp.zeros((7, 128), f32)
        for k in range(2):
            st_ref[9 + k : 10 + k, :] = total_row(sums[k])
        low = info[1] == 0
        keep_ref[...] = jnp.where(low, cross[:, 128:256], cross[:, 256:384])
        st_ref[16:144, :] = jnp.where(low, cross[:, 256:384], cross[:, 128:256])


def spread_body(head_ref, arrived_ref, keep_ref, out_ref):
    sums = head_ref[0:16, :] + arrived_ref[0:16, :]
    share = 128 // out_ref.shape[0]
    for k in range(out_ref.shape[0]):
        rows = slice(k * share, (k + 1) * share)
        out_ref[k, 0:16] = sums
        out_ref[k, 16 : 16 + share] = keep_ref[rows, :] + arrived_ref[16 + k * share : 16 + (k + 1) * share, :]
        if share < 8:
            out_ref[k, 16 + share :] = jnp.zeros((8 - share, 128), f32)


def both_body(info, own_ref, arrived_ref, out_ref):
    sums = own_ref[0:16, :] + arrived_ref[0:16, :]
    mine, other = own_ref[16:, :], arrived_ref[16:, :]
    low = info[1] == 0
    block = jnp.concatenate(
        [sums, jnp.where(low, mine, other), jnp.where(low, other, mine)], axis=0
    )
    for k in range(out_ref.shape[0]):
        out_ref[k] = block


def last_body(
    info, st1, in3, gc, sc, y_ref, g_ref, gx_ref, x_ref, cot_ref, wo_ref,
    out_ref, e_ref, t_ref, te_ref, st_ref, st3, u_ref, ws_ref,
    coef, w_two, w_turn, z_buf, cross, sums, sums_b,
):
    step = pl.program_id(0)
    tall, columns, images = x_ref.shape[:3]
    area = columns * images

    @pl.when(step == 0)
    def _():
        total = in3[0]
        for k in range(1, in3.shape[0]):
            total = total + in3[k]
        st3[...] = total[0:16]
        st_ref[16:, :] = total[16:]
        mean, inv = moments(wide(st3, 0), wide(st3, 4), st1[2:3, 0:1])
        scale = gc[...] * inv
        coef[0:1, :] = sc[...] - mean * scale
        high, low = split_two(wo_ref[...].astype(f32) * scale)
        w_two[0:128, :] = high
        w_two[128:256, :] = low
        ws_ref[...] = w_two[...]
        w_turn[:, 0:128] = jnp.transpose(w_two[0:128, :])
        w_turn[:, 128:256] = jnp.transpose(w_two[128:256, :])
        cross[...] = jnp.zeros_like(cross)
        sums[...] = jnp.zeros_like(sums)
        sums_b[...] = jnp.zeros_like(sums_b)

    mask = live(info, images, 512)
    bias = coef[0:1, :]
    zero = jnp.zeros((), bf16)
    piece = columns // 4
    parts = [(r, c) for r in range(tall) for c in range(0, columns, piece)]
    n = piece * images

    def product(r, c):
        act = y_ref[r, c : c + piece].reshape(n, 128)
        z = dot(jnp.concatenate([act, act], axis=1), w_two[...])
        z_buf[r, c : c + piece] = z.reshape(piece, images, 512)

    def pointwise(r, c):
        x = jnp.where(mask, x_ref[r, c], zero).astype(f32)
        value, slope = gelu_terms(z_buf[r, c] + (bias + x))
        out_ref[r, c] = value.astype(bf16)
        cot = jnp.where(mask, cot_ref[r, c], zero).astype(f32)
        e = slope * cot
        e_ref[r, c] = e.astype(bf16)
        return fold8(e), fold8(x)

    def collect(r, c):
        e = e_ref[r, c : c + piece].reshape(n, 512)
        cross[...] += dot_tn(y_ref[r, c : c + piece].reshape(n, 128), e)

    def through(r, c):
        y = dot(e_ref[r, c : c + piece].reshape(n, 512), w_turn[...])
        t = (y[:, 0:128] + y[:, 128:256]).reshape(piece, images, 128)
        t_ref[r, c : c + piece] = t.astype(bf16)
        sums_b[0] += fold8(t * g_ref[r, c : c + piece].astype(f32))
        sums_b[1] += fold8(t * gx_ref[r, c : c + piece].astype(f32))

    product(*parts[0])
    for k in range(len(parts) + 1):
        work = []
        if k + 1 < len(parts):
            work.append(functools.partial(product, *parts[k + 1]))
        if k > 0:
            work.append(functools.partial(through, *parts[k - 1]))
            work.append(functools.partial(collect, *parts[k - 1]))
        if k < len(parts):
            r, first = parts[k]
            total_e = jnp.zeros((8, 512), f32)
            total_x = jnp.zeros((8, 512), f32)
            for c in range(piece):
                if c % 2 == 0 and work:
                    work.pop(0)()
                add_e, add_x = pointwise(r, first + c)
                total_e += add_e
                total_x += add_x
            sums[0] += total_e
            sums[1] += total_x
        for rest in work:
            rest()
    take_edge(info, te_ref, t_ref)

    @pl.when(step == pl.num_programs(0) - 1)
    def _():
        u_ref[...] = cross[...]
        put_wide(st_ref, 0, total_row(sums[0]))
        put_wide(st_ref, 4, total_row(wo_ref[...].astype(f32) * cross[...]))
        put_wide(st_ref, 10, total_row(sums[1]))
        for k in range(2):
            st_ref[8 + k : 9 + k, :] = total_row(sums_b[k])
            st_ref[14 + k : 15 + k, :] = jnp.zeros((1, 128), f32)


def back_body(
    info, st1, st2, st3, in4, own4, xz_ref, gram_ref, u_ref, ga, sa, gb, gc, wo_ref, ws_ref, wt_ref,
    y_ref, s_ref, ye_ref, z2_ref, ze_ref, t_ref, te_ref, a_ref, z1_ref, x_ref,
    h_ref, mine_ref, sent_ref, small_ref,
    coef, mm, wide_w, frame, dacc, vacc, sums, packed, st4, pq,
):
    step = pl.program_id(0)
    last = pl.num_programs(0) - 1
    columns, images = z1_ref.shape[1:3]
    area = columns * images
    mask = live(info, images, 128)

    def second_back(t, product, slope, z):
        kappa, scale_b, beta, alpha = (coef[i : i + 1, :] for i in range(4))
        through = t.astype(f32) - kappa - product[..., 0:128] - product[..., 128:256]
        grad = scale_b * (slope.astype(f32) * through) - (alpha + beta * z)
        return jnp.where(mask, grad, 0.0).astype(bf16)

    @pl.when(step == 0)
    def _():
        pixels = st1[2:3, :]
        pixel = st1[2:3, 0:1]
        mean_a, inv_a = moments(st1[0:1, :], st1[1:2, :], pixels)
        mean_b, inv_b = moments(st2[0:1, :], st2[1:2, :], pixels)
        mean_c, inv_c = moments(wide(st3, 0), wide(st3, 4), pixel)
        total = in4[0, 0:16]
        share = 128 // in4.shape[0]
        span = (in4.shape[1] - 16) // 2
        for k in range(in4.shape[0]):
            if k > 0:
                total = total + in4[k, 0:16]
            rows = slice(k * share, (k + 1) * share)
            pq[0, rows] = in4[k, 16 : 16 + share]
            pq[1, rows] = in4[k, 16 + span : 16 + span + share]
        st4[...] = total
        total_c = wide(st4, 0)
        dot_c = inv_c * (wide(st4, 4) - mean_c * total_c)
        weights = wo_ref[...].astype(f32)
        scaled = ws_ref[0:128, :].astype(f32) + ws_ref[128:256, :].astype(f32)
        near, far = split_two(weights * (inv_c * dot_c / pixel))
        mat = dot_nt(near, ws_ref[0:128, :]) + dot_nt(near, ws_ref[128:256, :])
        mat = mat + dot_nt(far, ws_ref[0:128, :])
        high, low = split_two(mat)
        mm[:, 0:128] = high
        mm[:, 128:256] = low
        kappa = row_of_sums(scaled * (total_c / pixel))[0:1, :]
        mean_act = jnp.transpose(jnp.broadcast_to(st3[8:9, :] / pixels, (8, 128)))[:, 0:1]
        kappa = kappa - total_row(mean_act * mat)
        total_b = st4[8:9, :] - kappa * st3[9:10, :] - total_row(mat * pq[0])
        dot_b = st4[9:10, :] - kappa * st3[10:11, :] - total_row(mat * pq[1])
        scale_b = gb[...] * inv_b
        scale_a = ga[...] * inv_a
        coef[0:1, :] = kappa
        coef[1:2, :] = scale_b
        coef[2:3, :] = scale_b * inv_b * dot_b / pixels
        coef[3:4, :] = scale_b * (total_b - mean_b * inv_b * dot_b) / pixels
        coef[4:5, :] = scale_a
        coef[5:6, :] = sa[...] - mean_a * scale_a
        small_ref[...] = jnp.zeros_like(small_ref)
        put_wide(small_ref, 0, total_c)
        put_wide(small_ref, 4, dot_c)
        small_ref[8:9, :] = total_b
        small_ref[9:10, :] = dot_b
        column = jnp.transpose(gram_ref[128:136, :])[:, 0:1]
        product = dot_halves(gram_ref[0:128, :], wo_ref[...])
        grad = u_ref[...] - column * (total_c / pixel) - (product - column * mean_c) * (
            inv_c * dot_c / pixel
        )
        grad = grad * (gc[...] * inv_c)
        for i in range(4):
            packed[1152 + i * 128 : 1280 + i * 128, :] = grad[:, i * 128 : (i + 1) * 128]
        paired_weights(wt_ref, wide_w)
        dacc[...] = jnp.zeros_like(dacc)
        vacc[...] = jnp.zeros_like(vacc)
        sums[...] = jnp.zeros_like(sums)
        clear_frame(frame)
        place = (1 - info[1]) * (frame.shape[0] - 1)
        for c, n in groups(columns):
            act = ye_ref[c : c + n, :, 0:128].reshape(n * images, 128)
            extra = dot(act, mm[...]).reshape(n, images, 256)
            frame[place, 1 + c : 1 + c + n] = second_back(
                te_ref[c : c + n], extra, ye_ref[c : c + n, :, 128:256], ze_ref[c : c + n]
            )

    @pl.when(step < last)
    def _():
        for r in range(2):
            act = y_ref[r].reshape(area, 128)
            extra = dot(act, mm[...]).reshape(columns, images, 256)
            for c, n in groups(columns):
                frame[2 * step + 1 + r, 1 + c : 1 + c + n] = second_back(
                    t_ref[r, c : c + n],
                    extra[c : c + n],
                    s_ref[r, c : c + n],
                    z2_ref[r, c : c + n],
                )

    @pl.when(step > 0)
    def _():
        scale_a, bias_a = coef[4:5, :], coef[5:6, :]
        near = window(frame, step - 1)
        through = dot(near, wide_w[...])
        act = jnp.concatenate([a_ref[r].reshape(area, 128) for r in range(2)], axis=1)
        dacc[...] += dot_tn(act, near)
        total = jnp.zeros((8, 128), f32)
        dots = jnp.zeros((8, 128), f32)
        for r in range(2):
            part = through[:, r * 128 : (r + 1) * 128].reshape(columns, images, 128)
            for c, n in groups(columns):
                z = z1_ref[r, c : c + n]
                slope = gelu_terms(z * scale_a + bias_a)[1]
                grad = part[c : c + n] * slope
                total += fold8(grad)
                dots += fold8(grad * z)
                h_ref[r, c : c + n] = grad.astype(bf16)
        sums[0] += total
        sums[1] += dots
        vacc[...] += dot_tn(h_ref[...].reshape(2 * area, 128), x_ref[...].reshape(2 * area, 512))

    @pl.when(step == last)
    def _():
        pixels = st1[2:3, :]
        total_h, dot_h = total_row(sums[0]), total_row(sums[1])
        tail = jnp.concatenate(
            [total_h, dot_h, st1[0:1, :] / pixels, jnp.zeros((5, 128), f32)], axis=0
        )
        columns2 = jnp.transpose(tail)
        column_h, mean_a = columns2[:, 0:1], columns2[:, 2:3]
        for i in range(4):
            lanes = slice(i * 128, (i + 1) * 128)
            center = st4[10 + i : 11 + i, :] / pixels
            packed[1664 + i * 128 : 1792 + i * 128, :] = vacc[:, lanes] - column_h * center
            packed[2176 + i * 128 : 2304 + i * 128, :] = (
                xz_ref[lanes, :] - mean_a * own4[10 + i : 11 + i, :]
            )
        for t in range(3):
            for u in range(3):
                parts = []
                for o in range(2):
                    base = ((o + 2 - t) * 3 + 2 - u) * 128
                    parts.append(dacc[o * 128 : (o + 1) * 128, base : base + 128])
                packed[(t * 3 + u) * 128 : (t * 3 + u + 1) * 128, :] = parts[0] + parts[1]
        if packed.shape[0] > 2688:
            packed[2688:, :] = jnp.zeros((packed.shape[0] - 2688, 128), f32)
        half = packed.shape[0] // 2
        low = info[1] == 0
        mine_ref[0:half, :] = jnp.where(low, packed[0:half, :], packed[half:, :])
        sent_ref[0:half, :] = jnp.where(low, packed[half:, :], packed[0:half, :])
        mine_ref[half : half + 8, :] = tail
        sent_ref[half : half + 8, :] = tail


def pack_body(mine_ref, arrived_ref, out_ref):
    shares, block = out_ref.shape[:2]
    share = (mine_ref.shape[0] - 8) // shares
    small = mine_ref[shares * share :, :] + arrived_ref[shares * share :, :]
    high = small.astype(bf16).astype(f32)
    middle = (small - high).astype(bf16).astype(f32)
    low = small - high - middle
    tail = jnp.concatenate(
        [high[0:2], middle[0:2], low[0:2], jnp.zeros((block - share - 6, 128), f32)], axis=0
    )
    for k in range(shares):
        rows = slice(k * share, (k + 1) * share)
        total = mine_ref[rows, :] + arrived_ref[rows, :]
        out_ref[k] = jnp.concatenate([total, tail], axis=0).astype(bf16)


def share_body(share, in_ref, small_ref, out_ref):
    total = in_ref[0].astype(f32)
    for k in range(1, in_ref.shape[0]):
        total = total + in_ref[k].astype(f32)
    sums = total[share : share + 2] + total[share + 2 : share + 4] + total[share + 4 : share + 6]
    small_ref[...] = jnp.concatenate([sums, jnp.zeros((6, 128), f32)], axis=0)
    for k in range(out_ref.shape[0]):
        out_ref[k] = total.astype(bf16)


def input_body(info, st1, st5, ga, wi_ref, h_ref, z_ref, e_ref, g_ref, coef, w_turn):
    step = pl.program_id(0)
    tall, columns, images = z_ref.shape[:3]
    area = columns * images

    @pl.when(step == 0)
    def _():
        pixels = st1[2:3, :]
        mean, inv = moments(st1[0:1, :], st1[1:2, :], pixels)
        scale = ga[...] * inv
        w_turn[...] = jnp.transpose(wi_ref[...])
        total = st5[0:1, :]
        dot_a = inv * (st5[1:2, :] - mean * total)
        coef[0:1, :] = scale
        coef[1:2, :] = scale * inv * dot_a / pixels
        coef[2:3, :] = scale * (total - mean * inv * dot_a) / pixels

    mask = live(info, images, 128)
    scale, beta, alpha = (coef[i : i + 1, :] for i in range(3))
    for r in range(tall):
        parts = []
        for c, n in groups(columns):
            grad = scale * h_ref[r, c : c + n].astype(f32) - (alpha + beta * z_ref[r, c : c + n])
            parts.append(jnp.where(mask, grad, 0.0).astype(bf16).reshape(n * images, 128))
        through = dot(jnp.concatenate(parts, axis=0), w_turn[...])
        through = through.reshape(columns, images, 512)
        for c in range(columns):
            g_ref[r, c] = (through[c] + e_ref[r, c].astype(f32)).astype(bf16)


def final_body(
    share, info, st1, st5, ga, small_ref, mine_ref, other_ref,
    gwi_ref, gga_ref, gsa_ref, gwm_ref, ggb_ref, gsb_ref, gwo_ref, ggc_ref, gsc_ref, total_ref,
):
    shares = mine_ref.shape[0]
    for k in range(shares):
        mine, other = mine_ref[k].astype(f32), other_ref[k].astype(f32)
        low = jnp.where(info[1] == 0, mine, other)
        high = jnp.where(info[1] == 0, other, mine)
        total_ref[k * share : (k + 1) * share, :] = low[0:share]
        total_ref[(shares + k) * share : (shares + k + 1) * share, :] = high[0:share]
    pixels = st1[2:3, :]
    mean, inv = moments(st1[0:1, :], st1[1:2, :], pixels)
    total = st5[0:1, :]
    dot = inv * (st5[1:2, :] - mean * total)
    gsa_ref[...] = total
    gga_ref[...] = dot
    gsb_ref[...] = small_ref[8:9, :]
    ggb_ref[...] = small_ref[9:10, :]
    gsc_ref[...] = wide(small_ref, 0)
    ggc_ref[...] = wide(small_ref, 4)
    gwm_ref[...] = total_ref[0:1152, :]
    for i in range(4):
        gwo_ref[:, i * 128 : (i + 1) * 128] = total_ref[1152 + i * 128 : 1280 + i * 128, :]
        v = jnp.transpose(total_ref[1664 + i * 128 : 1792 + i * 128, :])
        xz = jnp.transpose(total_ref[2176 + i * 128 : 2304 + i * 128, :])
        gwi_ref[i * 128 : (i + 1) * 128, :] = (ga[...] * inv) * (v - xz * (inv * dot / pixels))


def local(
    images, counts, w_in, gain_a, shift_a, w_mid, gain_b, shift_b, w_out, gain_c, shift_c, cotangent
):
    count, rows, columns, channels = images.shape
    steps = rows // 2
    info = jnp.stack([counts[0], lax.axis_index("rows").astype(jnp.int32)])
    images = jnp.transpose(images, (1, 2, 0, 3))
    cotangent = jnp.transpose(cotangent, (1, 2, 0, 3))
    ga, sa, gb, sb = (v.reshape(1, 128) for v in (gain_a, shift_a, gain_b, shift_b))
    gc, sc = gain_c.reshape(1, 512), shift_c.reshape(1, 512)
    small = whole_spec((1, 128))
    large = whole_spec((1, 512))
    eight = whole_spec((8, 128))
    taps = whole_spec((3, 3, 128, 128))

    def tile(lanes):
        return (2, columns, count, lanes)

    def edge(lanes):
        return (columns, count, lanes)

    def ahead(i):
        return jnp.minimum(i, steps - 1)

    def behind(i):
        return jnp.maximum(i - 1, 0)

    def frame_like():
        return pltpu.VMEM((rows + 2, columns + 2, count, 128), bf16)

    pixels = count * rows * columns

    z1, z1_edge, st1 = call(
        first_body,
        steps,
        [SMEM, step_spec(tile(512)), whole_spec((512, 128))],
        [
            step_out(rows, tile(128), f32),
            whole_out(edge(128)),
            whole_out((8, 128)),
        ],
        [pltpu.VMEM((2, 8, 128), f32)],
        "first_norm_sums",
        pixels * 512 * 128 * 2,
        pixels * 1536,
    )(info, images, w_in)
    z1_edge = partner(z1_edge, 1)
    st1 = summed_at_once(st1)
    xz = call(
        cross_body,
        steps,
        [step_spec(tile(512)), step_spec(tile(128))],
        [whole_out((512, 128))],
        [pltpu.VMEM((128, 512), f32)],
        "input_cross",
        pixels * 512 * 128 * 2,
        pixels * 1536,
    )(images, z1)[0]
    w_back = jnp.swapaxes(w_mid[::-1, ::-1], 2, 3)
    xz, w_back = lax.optimization_barrier((xz, w_back))

    shares = lax.axis_size("batch")
    span = max(8, 128 // shares)
    everyone = [list(range(lax.axis_size("batch")))]
    z2, act_a, st2 = call(
        middle_body,
        steps + 1,
        [
            SMEM, eight, small, small, step_spec(tile(128), ahead), whole_spec(edge(128)), taps,
            whole_spec((512, 128)),
        ],
        [
            step_out(rows, tile(128), f32, behind),
            step_out(rows, tile(128), bf16, ahead),
            whole_out((8, 128)),
        ],
        [
            frame_like(),
            pltpu.VMEM((1536, 256), bf16),
            pltpu.VMEM((8, 128), f32),
            pltpu.VMEM((2, 8, 128), f32),
        ],
        "middle_conv",
        pixels * 12 * 128 * 128 * 2,
        pixels * 1280,
    )(info, st1, ga, sa, z1, z1_edge, w_mid, xz)
    st2 = summed_by_swap(st2)

    act_b, slope_b, dotted_b, y_edge, z2_edge, head, kept, gram = call(
        second_body,
        steps,
        [SMEM, eight, eight, small, small, step_spec(tile(128)), whole_spec((128, 512))],
        [
            step_out(rows, tile(128), bf16),
            step_out(rows, tile(128), bf16),
            step_out(rows, tile(128), bf16),
            whole_out(edge(256), bf16),
            whole_out(edge(128)),
            whole_out((144, 128)),
            whole_out((128, 128)),
            whole_out((136, 128)),
        ],
        [pltpu.VMEM((8, 128), f32), pltpu.VMEM((128, 384), f32), pltpu.VMEM((3, 8, 128), f32)],
        "second_norm",
        pixels * 384 * 128 * 2,
        pixels * 1280,
        42,
    )(info, st1, st2, gb, sb, z2, w_out)
    arrived3 = swapped(
        call(
            spread_body,
            1,
            [whole_spec((144, 128)), whole_spec((144, 128)), whole_spec((128, 128))],
            [whole_out((shares, 16 + span, 128))],
            [],
            "spread_third",
            1e5,
            1e6,
        )(head, partner(head, 1), kept)[0]
    )

    block_out, e, t, t_edge, own4, st3, u_local, w_scaled = call(
        last_body,
        steps,
        [
            SMEM, eight, whole_spec((shares, 16 + span, 128)), large, large, step_spec(tile(128)),
            step_spec(tile(128)), step_spec(tile(128)), step_spec(tile(512)),
            step_spec(tile(512)), whole_spec((128, 512)),
        ],
        [
            step_out(rows, tile(512), bf16),
            step_out(rows, tile(512), bf16),
            (step_spec(tile(128)), pltpu.HBM((rows, columns, count, 128), bf16)),
            whole_out(edge(128), bf16),
            whole_out((16 + span, 128)),
            whole_out((16, 128)),
            whole_out((128, 512)),
            whole_out((256, 512), bf16),
        ],
        [
            pltpu.VMEM((8, 512), f32),
            pltpu.VMEM((256, 512), bf16),
            pltpu.VMEM((512, 256), bf16),
            pltpu.VMEM(tile(512), f32),
            pltpu.VMEM((128, 512), f32),
            pltpu.VMEM((2, 8, 512), f32),
            pltpu.VMEM((2, 8, 128), f32),
        ],
        "last_norm",
        pixels * 512 * 128 * 10,
        pixels * 4864,
        36,
    )(info, st1, arrived3, gc, sc, act_b, slope_b, dotted_b, images, cotangent, w_out)

    other4, y_edge, z2_edge, t_edge = lax.optimization_barrier(
        tuple(
            partner(v, 1)
            for v in lax.optimization_barrier((own4, y_edge, z2_edge, t_edge))
        )
    )
    arrived4 = swapped(
        call(
            both_body,
            1,
            [SMEM, whole_spec((16 + span, 128)), whole_spec((16 + span, 128))],
            [whole_out((shares, 16 + 2 * span, 128))],
            [],
            "spread_fourth",
            1e5,
            1e6,
        )(info, own4, other4)[0]
    )

    share = -(-1344 // (8 * shares)) * 8
    half = share * shares
    block = -(-(share + 6) // 16) * 16
    h, mine, sent, small_sums = call(
        back_body,
        steps + 1,
        [
            SMEM, eight, eight, whole_spec((16, 128)), whole_spec((shares, 16 + 2 * span, 128)),
            whole_spec((16 + span, 128)),
            whole_spec((512, 128)), whole_spec((136, 128)),
            whole_spec((128, 512)), small, small, small, large, whole_spec((128, 512)),
            whole_spec((256, 512)), taps,
            step_spec(tile(128), ahead), step_spec(tile(128), ahead), whole_spec(edge(256)),
            step_spec(tile(128), ahead), whole_spec(edge(128)),
            step_spec(tile(128), ahead), whole_spec(edge(128)),
            step_spec(tile(128), behind), step_spec(tile(128), behind),
            step_spec(tile(512), behind),
        ],
        [
            step_out(rows, tile(128), bf16, behind),
            whole_out((half + 8, 128)),
            whole_out((half + 8, 128)),
            whole_out((16, 128)),
        ],
        [
            pltpu.VMEM((8, 128), f32),
            pltpu.VMEM((128, 256), bf16),
            pltpu.VMEM((1536, 256), bf16),
            frame_like(),
            pltpu.VMEM((256, 1536), f32),
            pltpu.VMEM((128, 512), f32),
            pltpu.VMEM((2, 8, 128), f32),
            pltpu.VMEM((2 * half, 128), f32),
            pltpu.VMEM((16, 128), f32),
            pltpu.VMEM((2, 128, 128), f32),
        ],
        "middle_back",
        pixels * 32 * 128 * 128 * 2,
        pixels * 4000,
        49,
    )(
        info, st1, st2, st3, arrived4, own4, xz, gram, u_local, ga, sa, gb, gc,
        w_out, w_scaled, w_back,
        act_b, slope_b, y_edge, z2, z2_edge, t, t_edge, act_a, z1, images,
    )
    arrived = partner(sent, 1)
    spread = call(
        pack_body,
        1,
        [whole_spec((half + 8, 128)), whole_spec((half + 8, 128))],
        [whole_out((shares, block, 128), bf16)],
        [],
        "pack_shares",
        1e6,
        2e6,
    )(mine, arrived)[0]
    spread = swapped(spread)
    st5, spread = call(
        functools.partial(share_body, share),
        1,
        [whole_spec((shares, block, 128))],
        [whole_out((8, 128)), whole_out((shares, block, 128), bf16)],
        [],
        "sum_shares",
        1e6,
        1e6,
    )(spread)
    gathered = swapped(spread)

    grad_images = call(
        input_body,
        steps,
        [
            SMEM, eight, eight, small, whole_spec((512, 128)),
            step_spec(tile(128)), step_spec(tile(128)), step_spec(tile(512)),
        ],
        [step_out(rows, tile(512), bf16)],
        [pltpu.VMEM((8, 128), f32), pltpu.VMEM((128, 512), bf16)],
        "input_grad",
        pixels * 512 * 128 * 2,
        pixels * 2816,
    )(info, st1, st5, ga, w_in, h, z1, e)[0]

    gathered, grad_images = lax.optimization_barrier((gathered, grad_images))
    shared = whole_spec((shares, block, 128))
    gwi, gga, gsa, gwm, ggb, gsb, gwo, ggc, gsc = call(
        functools.partial(final_body, share),
        1,
        [SMEM, eight, eight, small, whole_spec((16, 128)), shared, shared],
        [
            whole_out((512, 128)), whole_out((1, 128)), whole_out((1, 128)),
            whole_out((1152, 128)), whole_out((1, 128)), whole_out((1, 128)),
            whole_out((128, 512)), whole_out((1, 512)), whole_out((1, 512)),
        ],
        [pltpu.VMEM((2 * half, 128), f32)],
        "replicated_grads",
        1e6,
        3e6,
    )(info, st1, st5, ga, small_sums, gathered, partner(gathered, 1))
    return (
        jnp.transpose(block_out, (2, 0, 1, 3)),
        jnp.transpose(grad_images, (2, 0, 1, 3)),
        gwi,
        gga.reshape(128),
        gsa.reshape(128),
        gwm.reshape(3, 3, 128, 128),
        ggb.reshape(128),
        gsb.reshape(128),
        gwo,
        ggc.reshape(512),
        gsc.reshape(512),
    )


def solution(mesh):
    split = P("batch", "rows", None, None)
    placed = (split, P("batch"), P(), P(), P(), P(), P(), P(), P(), P(), P(), split)
    return jax.shard_map(
        local,
        mesh=mesh,
        in_specs=placed,
        out_specs=(split, split) + (P(),) * 9,
        check_vma=False,
    )
```

```python
import functools
import math

import jax
import jax.numpy as jnp
from jax import lax
from jax.experimental import pallas as pl
from jax.experimental.pallas import tpu as pltpu
from jax.sharding import PartitionSpec as P

epsilon = 1e-05
axes = ("batch", "rows")
f32 = jnp.float32
bf16 = jnp.bfloat16
C0 = math.sqrt(2.0 / math.pi)
C1 = C0 * 0.044715
K0 = -2.0 * C0 / math.log(2.0)
K1 = -2.0 * C1 / math.log(2.0)
K2 = -3.0 * math.log(2.0)
HIGH = lax.Precision.HIGHEST


def partner(block, mask):
    total = lax.axis_size("batch") * lax.axis_size("rows")
    return lax.ppermute(block, axes, [(i, i ^ mask) for i in range(total)])


def swapped_sum(block, groups):
    size = len(groups[0])
    spread = jnp.broadcast_to(block[None], (size,) + block.shape)
    arrived = lax.all_to_all(spread, "batch", 0, 0, axis_index_groups=groups, tiled=True)
    return jnp.sum(arrived, axis=0)


def swapped(spread):
    return lax.all_to_all(spread, "batch", 0, 0, tiled=True)


def summed_at_once(spread):
    return jnp.sum(lax.all_to_all(spread, axes, 0, 0, tiled=True), axis=0)


def summed_by_swap(block, near=None):
    block = block + partner(block, 1)
    count = lax.axis_size("batch")
    if near is None or count % near:
        return swapped_sum(block, [list(range(count))])
    block = swapped_sum(block, [list(range(i, i + near)) for i in range(0, count, near)])
    return swapped_sum(block, [list(range(i, count, near)) for i in range(near)])


def gate(u):
    inner = K0 + K1 * (u * u)
    return pltpu.reciprocal(1.0 + jnp.exp2(u * inner), approx=True), inner


def gelu_terms(u):
    half, inner = gate(u)
    value = u * half
    slope = half + value * (1.0 - half) * (K2 * inner - 4.0 * C0)
    return value, slope


def gelu_value(u):
    return u * gate(u)[0]


def moments(total, squares, pixels):
    mean = total / pixels
    return mean, lax.rsqrt(squares / pixels - mean * mean + epsilon)


def fold8(values):
    lanes = values.shape[-1]
    return jnp.sum(values.reshape(values.size // (8 * lanes), 8, lanes), axis=0)


def total_row(values):
    return jnp.sum(values, axis=0, keepdims=True)


def wide(ref, start):
    return jnp.concatenate([ref[start + i : start + i + 1, :] for i in range(4)], axis=1)


def put_wide(ref, start, row):
    for i in range(4):
        ref[start + i : start + i + 1, :] = row[:, i * 128 : (i + 1) * 128]


def dot_tn(a, b):
    return lax.dot_general(a, b, (((0,), (0,)), ((), ())), preferred_element_type=f32)


def dot_nt(a, b, precision=None):
    return lax.dot_general(
        a, b, (((1,), (1,)), ((), ())), preferred_element_type=f32, precision=precision
    )


def dot(a, b, precision=None):
    return jnp.dot(a, b, preferred_element_type=f32, precision=precision)


def split_two(values):
    high = values.astype(bf16)
    return high, (values - high.astype(f32)).astype(bf16)


def dot_halves(a, b):
    high, low = split_two(a)
    return dot(high, b) + dot(low, b)


def row_of_sums(values):
    high, low = split_two(values)
    one = jnp.ones((16, values.shape[1]), bf16)
    return (dot_nt(one, high) + dot_nt(one, low))[0:8, :]


def call(body, grid, ins, outs, scratch, name, flops, bytes_moved, vmem=52):
    return pl.pallas_call(
        body,
        grid=(grid,),
        in_specs=ins,
        out_specs=[spec for spec, _ in outs],
        out_shape=[shape for _, shape in outs],
        scratch_shapes=scratch,
        name=name,
        compiler_params=pltpu.CompilerParams(
            dimension_semantics=("arbitrary",), vmem_limit_bytes=vmem << 20
        ),
        cost_estimate=pl.CostEstimate(
            flops=int(flops), bytes_accessed=int(bytes_moved), transcendentals=0
        ),
    )


SMEM = pl.BlockSpec(memory_space=pltpu.SMEM)
ANY = pl.BlockSpec(memory_space=pl.ANY)


def whole_spec(shape):
    return pl.BlockSpec(tuple(shape), lambda i: (0,) * len(shape))


def step_spec(shape, place=lambda i: i):
    return pl.BlockSpec(tuple(shape), lambda i: (place(i),) + (0,) * (len(shape) - 1))


def whole_out(shape, dtype=f32):
    return (whole_spec(shape), jax.ShapeDtypeStruct(shape, dtype))


def step_out(count, shape, dtype, place=lambda i: i):
    return (
        step_spec(shape, place),
        jax.ShapeDtypeStruct((count,) + tuple(shape[1:]), dtype),
    )


def live(info, images, lanes):
    return lax.broadcasted_iota(jnp.int32, (images, lanes), 0) < info[0]


def groups(columns):
    return [(c, min(4, columns - c)) for c in range(0, columns, 4)]


def take_edge(info, edge_ref, ref):
    step = pl.program_id(0)

    @pl.when((step == 0) & (info[1] == 1))
    def _():
        edge_ref[...] = ref[0].astype(edge_ref.dtype)

    @pl.when((step == pl.num_programs(0) - 1) & (info[1] == 0))
    def _():
        edge_ref[...] = ref[ref.shape[0] - 1].astype(edge_ref.dtype)


def first_body(info, x_ref, w_ref, z_ref, edge_ref, stat_ref, zacc):
    step = pl.program_id(0)
    tall, columns, images = x_ref.shape[:3]
    area = columns * images

    @pl.when(step == 0)
    def _():
        zacc[...] = jnp.zeros_like(zacc)

    mask = live(info, images, 128)
    for r in range(tall):
        x = x_ref[r].reshape(area, 512)
        z = dot(x, w_ref[...]).reshape(columns, images, 128)
        z = jnp.where(mask, z, 0.0)
        z_ref[r] = z
        zacc[0] += fold8(z)
        zacc[1] += fold8(z * z)
    take_edge(info, edge_ref, z_ref)

    @pl.when(step == pl.num_programs(0) - 1)
    def _():
        pixels = (info[0] * (pl.num_programs(0) * tall * columns)).astype(f32)
        block = jnp.concatenate(
            [
                total_row(zacc[0]),
                total_row(zacc[1]),
                jnp.full((1, 128), pixels, f32),
                jnp.zeros((5, 128), f32),
            ],
            axis=0,
        )
        for k in range(stat_ref.shape[0]):
            stat_ref[k] = block


def cross_body(x_ref, z_ref, xz_ref, acc):
    step = pl.program_id(0)
    tall, columns, images = x_ref.shape[:3]
    area = columns * images

    @pl.when(step == 0)
    def _():
        acc[...] = jnp.zeros_like(acc)

    for r in range(tall):
        z = z_ref[r].astype(bf16).reshape(area, 128)
        acc[...] += dot_tn(z, x_ref[r].reshape(area, 512))

    @pl.when(step == pl.num_programs(0) - 1)
    def _():
        for i in range(4):
            xz_ref[i * 128 : (i + 1) * 128, :] = acc[:, i * 128 : (i + 1) * 128]


def paired_weights(w_ref, target):
    for r in range(4):
        for u in range(3):
            for o in range(2):
                t = r - o
                base = (r * 3 + u) * 128
                if 0 <= t <= 2:
                    block = w_ref[t, u]
                else:
                    block = jnp.zeros((128, 128), bf16)
                target[base : base + 128, o * 128 : (o + 1) * 128] = block


def window(frame, pair):
    columns, images = frame.shape[1] - 2, frame.shape[2]
    parts = [
        frame[2 * pair + r, u : u + columns].reshape(columns * images, 128)
        for r in range(4)
        for u in range(3)
    ]
    return jnp.concatenate(parts, axis=1)


def clear_frame(frame):
    tall, wide_columns = frame.shape[:2]
    zero = jnp.zeros(frame.shape[2:], frame.dtype)
    for e in range(tall):
        frame[e, 0] = zero
        frame[e, wide_columns - 1] = zero
    for c in range(wide_columns):
        frame[0, c] = zero
        frame[tall - 1, c] = zero


def middle_body(
    info, st1, ga, sa, z_ref, edge_ref, w_ref, xz_ref,
    z2_ref, a_ref, stat_ref, frame, wide_w, coef, zacc,
):
    step = pl.program_id(0)
    last = pl.num_programs(0) - 1
    columns, images = z_ref.shape[1:3]
    area = columns * images

    def activated(z):
        return gelu_value(z * coef[0:1, :] + coef[1:2, :]).astype(bf16)

    @pl.when(step == 0)
    def _():
        mean, inv = moments(st1[0:1, :], st1[1:2, :], st1[2:3, :])
        scale = ga[...] * inv
        coef[0:1, :] = scale
        coef[1:2, :] = sa[...] - mean * scale
        paired_weights(w_ref, wide_w)
        zacc[...] = jnp.zeros_like(zacc)
        clear_frame(frame)
        place = (1 - info[1]) * (frame.shape[0] - 1)
        for c, n in groups(columns):
            frame[place, 1 + c : 1 + c + n] = activated(edge_ref[c : c + n])

    @pl.when(step < last)
    def _():
        for r in range(2):
            for c, n in groups(columns):
                value = activated(z_ref[r, c : c + n])
                frame[2 * step + 1 + r, 1 + c : 1 + c + n] = value
                a_ref[r, c : c + n] = value

    @pl.when(step > 0)
    def _():
        mask = live(info, images, 128)
        y = dot(window(frame, step - 1), wide_w[...])
        for r in range(2):
            z = y[:, r * 128 : (r + 1) * 128].reshape(columns, images, 128)
            z2_ref[r] = z
            zacc[0] += fold8(jnp.where(mask, jnp.sum(z, axis=0), 0.0))
            zacc[1] += fold8(jnp.where(mask, jnp.sum(z * z, axis=0), 0.0))

    @pl.when(step == last)
    def _():
        stat_ref[...] = jnp.zeros_like(stat_ref)
        for k in range(2):
            stat_ref[k : k + 1, :] = total_row(zacc[k])


def second_coef(st1, st2, gb, sb, coef):
    mean, inv = moments(st2[0:1, :], st2[1:2, :], st1[2:3, :])
    scale = gb[...] * inv
    coef[0:1, :] = scale
    coef[1:2, :] = sb[...] - mean * scale
    coef[2:3, :] = inv
    coef[3:4, :] = -mean * inv


def second_body(
    info, st1, st2, gb, sb, z_ref, wo_ref,
    act_ref, g_ref, gx_ref, ye_ref, ze_ref, st_ref, keep_ref, gram_ref, coef, cross, sums,
):
    step = pl.program_id(0)
    tall, columns, images = z_ref.shape[:3]
    area = columns * images

    @pl.when(step == 0)
    def _():
        second_coef(st1, st2, gb, sb, coef)
        cross[...] = jnp.zeros_like(cross)
        sums[...] = jnp.zeros_like(sums)

    mask = live(info, images, 128)
    scale, bias, inv, shift = (coef[i : i + 1, :] for i in range(4))
    edge_row = (1 - info[1]) * (tall - 1)
    at_edge = step == (1 - info[1]) * (pl.num_programs(0) - 1)
    totals = [jnp.zeros((images, 128), f32) for _ in range(3)]
    for r in range(tall):
        acts, others = [], []
        for c, n in groups(columns):
            z = z_ref[r, c : c + n]
            value, slope = gelu_terms(z * scale + bias)
            dotted = slope * (z * inv + shift)
            slope, dotted, value = (v.astype(bf16) for v in (slope, dotted, value))
            for k, part in enumerate((slope, dotted, value)):
                totals[k] += jnp.sum(part.astype(f32), axis=0)
            g_ref[r, c : c + n] = slope
            gx_ref[r, c : c + n] = dotted
            act_ref[r, c : c + n] = value
            value = jnp.where(mask, value, jnp.zeros((), bf16))
            acts.append(value.reshape(n * images, 128))
        acts = jnp.concatenate(acts, axis=0)
        cross[...] += dot_tn(
            acts,
            jnp.concatenate(
                [acts, g_ref[r].reshape(area, 128), gx_ref[r].reshape(area, 128)], axis=1
            ),
        )

        @pl.when(at_edge & (edge_row == r))
        def _():
            ye_ref[:, :, 0:128] = act_ref[r]
            ye_ref[:, :, 128:256] = g_ref[r]
            ze_ref[...] = z_ref[r]

    for k in range(3):
        sums[k] += fold8(jnp.where(mask, totals[k], 0.0))

    @pl.when(step == pl.num_programs(0) - 1)
    def _():
        gram = cross[:, 0:128]
        gram_ref[0:128, :] = gram
        st_ref[8:16, :] = jnp.zeros((8, 128), f32)
        st_ref[8:9, :] = total_row(sums[2])
        gram_ref[128:136, :] = st_ref[8:16, :]
        spread = dot_halves(gram_ref[...], wo_ref[...])
        put_wide(st_ref, 0, spread[128:129, :])
        put_wide(st_ref, 4, total_row(spread[0:128, :] * wo_ref[...].astype(f32)))
        st_ref[9:16, :] = jnp.zeros((7, 128), f32)
        for k in range(2):
            st_ref[9 + k : 10 + k, :] = total_row(sums[k])
        low = info[1] == 0
        keep_ref[...] = jnp.where(low, cross[:, 128:256], cross[:, 256:384])
        st_ref[16:144, :] = jnp.where(low, cross[:, 256:384], cross[:, 128:256])


def spread_body(head_ref, arrived_ref, keep_ref, out_ref):
    sums = head_ref[0:16, :] + arrived_ref[0:16, :]
    share = 128 // out_ref.shape[0]
    for k in range(out_ref.shape[0]):
        rows = slice(k * share, (k + 1) * share)
        out_ref[k, 0:16] = sums
        out_ref[k, 16 : 16 + share] = keep_ref[rows, :] + arrived_ref[16 + k * share : 16 + (k + 1) * share, :]
        if share < 8:
            out_ref[k, 16 + share :] = jnp.zeros((8 - share, 128), f32)


def both_body(info, own_ref, arrived_ref, out_ref):
    sums = own_ref[0:16, :] + arrived_ref[0:16, :]
    mine, other = own_ref[16:, :], arrived_ref[16:, :]
    low = info[1] == 0
    block = jnp.concatenate(
        [sums, jnp.where(low, mine, other), jnp.where(low, other, mine)], axis=0
    )
    for k in range(out_ref.shape[0]):
        out_ref[k] = block


def last_body(
    info, st1, in3, gc, sc, y_ref, g_ref, gx_ref, x_ref, cot_ref, wo_ref,
    out_ref, e_ref, t_ref, te_ref, st_ref, st3, u_ref, ws_ref,
    coef, w_two, w_turn, z_buf, cross, sums, sums_b,
):
    step = pl.program_id(0)
    tall, columns, images = x_ref.shape[:3]
    area = columns * images

    @pl.when(step == 0)
    def _():
        total = in3[0]
        for k in range(1, in3.shape[0]):
            total = total + in3[k]
        st3[...] = total[0:16]
        st_ref[16:, :] = total[16:]
        mean, inv = moments(wide(st3, 0), wide(st3, 4), st1[2:3, 0:1])
        scale = gc[...] * inv
        coef[0:1, :] = sc[...] - mean * scale
        high, low = split_two(wo_ref[...].astype(f32) * scale)
        w_two[0:128, :] = high
        w_two[128:256, :] = low
        ws_ref[...] = w_two[...]
        w_turn[:, 0:128] = jnp.transpose(w_two[0:128, :])
        w_turn[:, 128:256] = jnp.transpose(w_two[128:256, :])
        cross[...] = jnp.zeros_like(cross)
        sums[...] = jnp.zeros_like(sums)
        sums_b[...] = jnp.zeros_like(sums_b)

    mask = live(info, images, 512)
    bias = coef[0:1, :]
    zero = jnp.zeros((), bf16)
    piece = columns // 4
    parts = [(r, c) for r in range(tall) for c in range(0, columns, piece)]
    n = piece * images

    def product(r, c):
        act = y_ref[r, c : c + piece].reshape(n, 128)
        z = dot(jnp.concatenate([act, act], axis=1), w_two[...])
        z_buf[r, c : c + piece] = z.reshape(piece, images, 512)

    def pointwise(r, c):
        x = jnp.where(mask, x_ref[r, c], zero).astype(f32)
        value, slope = gelu_terms(z_buf[r, c] + (bias + x))
        out_ref[r, c] = value.astype(bf16)
        cot = jnp.where(mask, cot_ref[r, c], zero).astype(f32)
        e = slope * cot
        e_ref[r, c] = e.astype(bf16)
        return fold8(e), fold8(x)

    def collect(r, c):
        e = e_ref[r, c : c + piece].reshape(n, 512)
        cross[...] += dot_tn(y_ref[r, c : c + piece].reshape(n, 128), e)

    def through(r, c):
        y = dot(e_ref[r, c : c + piece].reshape(n, 512), w_turn[...])
        t = (y[:, 0:128] + y[:, 128:256]).reshape(piece, images, 128)
        t_ref[r, c : c + piece] = t.astype(bf16)
        sums_b[0] += fold8(t * g_ref[r, c : c + piece].astype(f32))
        sums_b[1] += fold8(t * gx_ref[r, c : c + piece].astype(f32))

    product(*parts[0])
    for k in range(len(parts) + 1):
        work = []
        if k + 1 < len(parts):
            work.append(functools.partial(product, *parts[k + 1]))
        if k > 0:
            work.append(functools.partial(through, *parts[k - 1]))
            work.append(functools.partial(collect, *parts[k - 1]))
        if k < len(parts):
            r, first = parts[k]
            total_e = jnp.zeros((8, 512), f32)
            total_x = jnp.zeros((8, 512), f32)
            for c in range(piece):
                if c % 2 == 0 and work:
                    work.pop(0)()
                add_e, add_x = pointwise(r, first + c)
                total_e += add_e
                total_x += add_x
            sums[0] += total_e
            sums[1] += total_x
        for rest in work:
            rest()
    take_edge(info, te_ref, t_ref)

    @pl.when(step == pl.num_programs(0) - 1)
    def _():
        u_ref[...] = cross[...]
        put_wide(st_ref, 0, total_row(sums[0]))
        put_wide(st_ref, 4, total_row(wo_ref[...].astype(f32) * cross[...]))
        put_wide(st_ref, 10, total_row(sums[1]))
        for k in range(2):
            st_ref[8 + k : 9 + k, :] = total_row(sums_b[k])
            st_ref[14 + k : 15 + k, :] = jnp.zeros((1, 128), f32)


def back_body(
    info, st1, st2, st3, in4, own4, xz_ref, gram_ref, u_ref, ga, sa, gb, gc, wo_ref, ws_ref, wt_ref,
    y_ref, s_ref, ye_ref, z2_ref, ze_ref, t_ref, te_ref, a_ref, z1_ref, x_ref,
    h_ref, mine_ref, sent_ref, small_ref,
    coef, mm, wide_w, frame, dacc, vacc, sums, packed, st4, pq,
):
    step = pl.program_id(0)
    last = pl.num_programs(0) - 1
    columns, images = z1_ref.shape[1:3]
    area = columns * images
    mask = live(info, images, 128)

    def second_back(t, product, slope, z):
        kappa, scale_b, beta, alpha = (coef[i : i + 1, :] for i in range(4))
        through = t.astype(f32) - kappa - product[..., 0:128] - product[..., 128:256]
        grad = scale_b * (slope.astype(f32) * through) - (alpha + beta * z)
        return jnp.where(mask, grad, 0.0).astype(bf16)

    @pl.when(step == 0)
    def _():
        pixels = st1[2:3, :]
        pixel = st1[2:3, 0:1]
        mean_a, inv_a = moments(st1[0:1, :], st1[1:2, :], pixels)
        mean_b, inv_b = moments(st2[0:1, :], st2[1:2, :], pixels)
        mean_c, inv_c = moments(wide(st3, 0), wide(st3, 4), pixel)
        total = in4[0, 0:16]
        share = 128 // in4.shape[0]
        span = (in4.shape[1] - 16) // 2
        for k in range(in4.shape[0]):
            if k > 0:
                total = total + in4[k, 0:16]
            rows = slice(k * share, (k + 1) * share)
            pq[0, rows] = in4[k, 16 : 16 + share]
            pq[1, rows] = in4[k, 16 + span : 16 + span + share]
        st4[...] = total
        total_c = wide(st4, 0)
        dot_c = inv_c * (wide(st4, 4) - mean_c * total_c)
        weights = wo_ref[...].astype(f32)
        scaled = ws_ref[0:128, :].astype(f32) + ws_ref[128:256, :].astype(f32)
        near, far = split_two(weights * (inv_c * dot_c / pixel))
        mat = dot_nt(near, ws_ref[0:128, :]) + dot_nt(near, ws_ref[128:256, :])
        mat = mat + dot_nt(far, ws_ref[0:128, :])
        high, low = split_two(mat)
        mm[:, 0:128] = high
        mm[:, 128:256] = low
        kappa = row_of_sums(scaled * (total_c / pixel))[0:1, :]
        mean_act = jnp.transpose(jnp.broadcast_to(st3[8:9, :] / pixels, (8, 128)))[:, 0:1]
        kappa = kappa - total_row(mean_act * mat)
        total_b = st4[8:9, :] - kappa * st3[9:10, :] - total_row(mat * pq[0])
        dot_b = st4[9:10, :] - kappa * st3[10:11, :] - total_row(mat * pq[1])
        scale_b = gb[...] * inv_b
        scale_a = ga[...] * inv_a
        coef[0:1, :] = kappa
        coef[1:2, :] = scale_b
        coef[2:3, :] = scale_b * inv_b * dot_b / pixels
        coef[3:4, :] = scale_b * (total_b - mean_b * inv_b * dot_b) / pixels
        coef[4:5, :] = scale_a
        coef[5:6, :] = sa[...] - mean_a * scale_a
        small_ref[...] = jnp.zeros_like(small_ref)
        put_wide(small_ref, 0, total_c)
        put_wide(small_ref, 4, dot_c)
        small_ref[8:9, :] = total_b
        small_ref[9:10, :] = dot_b
        column = jnp.transpose(gram_ref[128:136, :])[:, 0:1]
        product = dot_halves(gram_ref[0:128, :], wo_ref[...])
        grad = u_ref[...] - column * (total_c / pixel) - (product - column * mean_c) * (
            inv_c * dot_c / pixel
        )
        grad = grad * (gc[...] * inv_c)
        for i in range(4):
            packed[1152 + i * 128 : 1280 + i * 128, :] = grad[:, i * 128 : (i + 1) * 128]
        paired_weights(wt_ref, wide_w)
        dacc[...] = jnp.zeros_like(dacc)
        vacc[...] = jnp.zeros_like(vacc)
        sums[...] = jnp.zeros_like(sums)
        clear_frame(frame)
        place = (1 - info[1]) * (frame.shape[0] - 1)
        for c, n in groups(columns):
            act = ye_ref[c : c + n, :, 0:128].reshape(n * images, 128)
            extra = dot(act, mm[...]).reshape(n, images, 256)
            frame[place, 1 + c : 1 + c + n] = second_back(
                te_ref[c : c + n], extra, ye_ref[c : c + n, :, 128:256], ze_ref[c : c + n]
            )

    @pl.when(step < last)
    def _():
        for r in range(2):
            act = y_ref[r].reshape(area, 128)
            extra = dot(act, mm[...]).reshape(columns, images, 256)
            for c, n in groups(columns):
                frame[2 * step + 1 + r, 1 + c : 1 + c + n] = second_back(
                    t_ref[r, c : c + n],
                    extra[c : c + n],
                    s_ref[r, c : c + n],
                    z2_ref[r, c : c + n],
                )

    @pl.when(step > 0)
    def _():
        scale_a, bias_a = coef[4:5, :], coef[5:6, :]
        near = window(frame, step - 1)
        through = dot(near, wide_w[...])
        act = jnp.concatenate([a_ref[r].reshape(area, 128) for r in range(2)], axis=1)
        dacc[...] += dot_tn(act, near)
        total = jnp.zeros((8, 128), f32)
        dots = jnp.zeros((8, 128), f32)
        for r in range(2):
            part = through[:, r * 128 : (r + 1) * 128].reshape(columns, images, 128)
            for c, n in groups(columns):
                z = z1_ref[r, c : c + n]
                slope = gelu_terms(z * scale_a + bias_a)[1]
                grad = part[c : c + n] * slope
                total += fold8(grad)
                dots += fold8(grad * z)
                h_ref[r, c : c + n] = grad.astype(bf16)
        sums[0] += total
        sums[1] += dots
        vacc[...] += dot_tn(h_ref[...].reshape(2 * area, 128), x_ref[...].reshape(2 * area, 512))

    @pl.when(step == last)
    def _():
        pixels = st1[2:3, :]
        total_h, dot_h = total_row(sums[0]), total_row(sums[1])
        tail = jnp.concatenate(
            [total_h, dot_h, st1[0:1, :] / pixels, jnp.zeros((5, 128), f32)], axis=0
        )
        columns2 = jnp.transpose(tail)
        column_h, mean_a = columns2[:, 0:1], columns2[:, 2:3]
        for i in range(4):
            lanes = slice(i * 128, (i + 1) * 128)
            center = st4[10 + i : 11 + i, :] / pixels
            packed[1664 + i * 128 : 1792 + i * 128, :] = vacc[:, lanes] - column_h * center
            packed[2176 + i * 128 : 2304 + i * 128, :] = (
                xz_ref[lanes, :] - mean_a * own4[10 + i : 11 + i, :]
            )
        for t in range(3):
            for u in range(3):
                parts = []
                for o in range(2):
                    base = ((o + 2 - t) * 3 + 2 - u) * 128
                    parts.append(dacc[o * 128 : (o + 1) * 128, base : base + 128])
                packed[(t * 3 + u) * 128 : (t * 3 + u + 1) * 128, :] = parts[0] + parts[1]
        if packed.shape[0] > 2688:
            packed[2688:, :] = jnp.zeros((packed.shape[0] - 2688, 128), f32)
        half = packed.shape[0] // 2
        low = info[1] == 0
        mine_ref[0:half, :] = jnp.where(low, packed[0:half, :], packed[half:, :])
        sent_ref[0:half, :] = jnp.where(low, packed[half:, :], packed[0:half, :])
        mine_ref[half : half + 8, :] = tail
        sent_ref[half : half + 8, :] = tail


def pack_body(mine_ref, arrived_ref, out_ref):
    shares, block = out_ref.shape[:2]
    share = (mine_ref.shape[0] - 8) // shares
    small = mine_ref[shares * share :, :] + arrived_ref[shares * share :, :]
    high = small.astype(bf16).astype(f32)
    middle = (small - high).astype(bf16).astype(f32)
    low = small - high - middle
    tail = jnp.concatenate(
        [high[0:2], middle[0:2], low[0:2], jnp.zeros((block - share - 6, 128), f32)], axis=0
    )
    for k in range(shares):
        rows = slice(k * share, (k + 1) * share)
        total = mine_ref[rows, :] + arrived_ref[rows, :]
        out_ref[k] = jnp.concatenate([total, tail], axis=0).astype(bf16)


def share_body(share, in_ref, small_ref, out_ref):
    total = in_ref[0].astype(f32)
    for k in range(1, in_ref.shape[0]):
        total = total + in_ref[k].astype(f32)
    sums = total[share : share + 2] + total[share + 2 : share + 4] + total[share + 4 : share + 6]
    small_ref[...] = jnp.concatenate([sums, jnp.zeros((6, 128), f32)], axis=0)
    for k in range(out_ref.shape[0]):
        out_ref[k] = total.astype(bf16)


def input_body(info, st1, st5, ga, wi_ref, h_ref, z_ref, e_ref, g_ref, coef, w_turn):
    step = pl.program_id(0)
    tall, columns, images = z_ref.shape[:3]
    area = columns * images

    @pl.when(step == 0)
    def _():
        pixels = st1[2:3, :]
        mean, inv = moments(st1[0:1, :], st1[1:2, :], pixels)
        scale = ga[...] * inv
        w_turn[...] = jnp.transpose(wi_ref[...])
        total = st5[0:1, :]
        dot_a = inv * (st5[1:2, :] - mean * total)
        coef[0:1, :] = scale
        coef[1:2, :] = scale * inv * dot_a / pixels
        coef[2:3, :] = scale * (total - mean * inv * dot_a) / pixels

    mask = live(info, images, 128)
    scale, beta, alpha = (coef[i : i + 1, :] for i in range(3))
    for r in range(tall):
        parts = []
        for c, n in groups(columns):
            grad = scale * h_ref[r, c : c + n].astype(f32) - (alpha + beta * z_ref[r, c : c + n])
            parts.append(jnp.where(mask, grad, 0.0).astype(bf16).reshape(n * images, 128))
        through = dot(jnp.concatenate(parts, axis=0), w_turn[...])
        through = through.reshape(columns, images, 512)
        for c in range(columns):
            g_ref[r, c] = (through[c] + e_ref[r, c].astype(f32)).astype(bf16)


def final_body(
    share, info, st1, st5, ga, small_ref, mine_ref, other_ref,
    gwi_ref, gga_ref, gsa_ref, gwm_ref, ggb_ref, gsb_ref, gwo_ref, ggc_ref, gsc_ref, total_ref,
):
    shares = mine_ref.shape[0]
    for k in range(shares):
        mine, other = mine_ref[k].astype(f32), other_ref[k].astype(f32)
        low = jnp.where(info[1] == 0, mine, other)
        high = jnp.where(info[1] == 0, other, mine)
        total_ref[k * share : (k + 1) * share, :] = low[0:share]
        total_ref[(shares + k) * share : (shares + k + 1) * share, :] = high[0:share]
    pixels = st1[2:3, :]
    mean, inv = moments(st1[0:1, :], st1[1:2, :], pixels)
    total = st5[0:1, :]
    dot = inv * (st5[1:2, :] - mean * total)
    gsa_ref[...] = total
    gga_ref[...] = dot
    gsb_ref[...] = small_ref[8:9, :]
    ggb_ref[...] = small_ref[9:10, :]
    gsc_ref[...] = wide(small_ref, 0)
    ggc_ref[...] = wide(small_ref, 4)
    gwm_ref[...] = total_ref[0:1152, :]
    for i in range(4):
        gwo_ref[:, i * 128 : (i + 1) * 128] = total_ref[1152 + i * 128 : 1280 + i * 128, :]
        v = jnp.transpose(total_ref[1664 + i * 128 : 1792 + i * 128, :])
        xz = jnp.transpose(total_ref[2176 + i * 128 : 2304 + i * 128, :])
        gwi_ref[i * 128 : (i + 1) * 128, :] = (ga[...] * inv) * (v - xz * (inv * dot / pixels))


def local(
    images, counts, w_in, gain_a, shift_a, w_mid, gain_b, shift_b, w_out, gain_c, shift_c, cotangent
):
    count, rows, columns, channels = images.shape
    steps = rows // 2
    info = jnp.stack([counts[0], lax.axis_index("rows").astype(jnp.int32)])
    images = jnp.transpose(images, (1, 2, 0, 3))
    cotangent = jnp.transpose(cotangent, (1, 2, 0, 3))
    ga, sa, gb, sb = (v.reshape(1, 128) for v in (gain_a, shift_a, gain_b, shift_b))
    gc, sc = gain_c.reshape(1, 512), shift_c.reshape(1, 512)
    small = whole_spec((1, 128))
    large = whole_spec((1, 512))
    eight = whole_spec((8, 128))
    taps = whole_spec((3, 3, 128, 128))

    def tile(lanes):
        return (2, columns, count, lanes)

    def edge(lanes):
        return (columns, count, lanes)

    def ahead(i):
        return jnp.minimum(i, steps - 1)

    def behind(i):
        return jnp.maximum(i - 1, 0)

    def frame_like():
        return pltpu.VMEM((rows + 2, columns + 2, count, 128), bf16)

    pixels = count * rows * columns
    shares = lax.axis_size("batch")

    z1, z1_edge, st1 = call(
        first_body,
        steps,
        [SMEM, step_spec(tile(512)), whole_spec((512, 128))],
        [
            step_out(rows, tile(128), f32),
            whole_out(edge(128)),
            whole_out((shares * lax.axis_size("rows"), 8, 128)),
        ],
        [pltpu.VMEM((2, 8, 128), f32)],
        "first_norm_sums",
        pixels * 512 * 128 * 2,
        pixels * 1536,
        58,
    )(info, images, w_in)
    z1_edge = partner(z1_edge, 1)
    st1 = summed_at_once(st1)
    xz = call(
        cross_body,
        steps,
        [step_spec(tile(512)), step_spec(tile(128))],
        [whole_out((512, 128))],
        [pltpu.VMEM((128, 512), f32)],
        "input_cross",
        pixels * 512 * 128 * 2,
        pixels * 1536,
    )(images, z1)[0]
    w_back = jnp.swapaxes(w_mid[::-1, ::-1], 2, 3)
    xz, w_back = lax.optimization_barrier((xz, w_back))

    span = max(8, 128 // shares)
    everyone = [list(range(lax.axis_size("batch")))]
    z2, act_a, st2 = call(
        middle_body,
        steps + 1,
        [
            SMEM, eight, small, small, step_spec(tile(128), ahead), whole_spec(edge(128)), taps,
            whole_spec((512, 128)),
        ],
        [
            step_out(rows, tile(128), f32, behind),
            step_out(rows, tile(128), bf16, ahead),
            whole_out((8, 128)),
        ],
        [
            frame_like(),
            pltpu.VMEM((1536, 256), bf16),
            pltpu.VMEM((8, 128), f32),
            pltpu.VMEM((2, 8, 128), f32),
        ],
        "middle_conv",
        pixels * 12 * 128 * 128 * 2,
        pixels * 1280,
    )(info, st1, ga, sa, z1, z1_edge, w_mid, xz)
    st2 = summed_by_swap(st2)

    act_b, slope_b, dotted_b, y_edge, z2_edge, head, kept, gram = call(
        second_body,
        steps,
        [SMEM, eight, eight, small, small, step_spec(tile(128)), whole_spec((128, 512))],
        [
            step_out(rows, tile(128), bf16),
            step_out(rows, tile(128), bf16),
            step_out(rows, tile(128), bf16),
            whole_out(edge(256), bf16),
            whole_out(edge(128)),
            whole_out((144, 128)),
            whole_out((128, 128)),
            whole_out((136, 128)),
        ],
        [pltpu.VMEM((8, 128), f32), pltpu.VMEM((128, 384), f32), pltpu.VMEM((3, 8, 128), f32)],
        "second_norm",
        pixels * 384 * 128 * 2,
        pixels * 1280,
        42,
    )(info, st1, st2, gb, sb, z2, w_out)
    arrived3 = swapped(
        call(
            spread_body,
            1,
            [whole_spec((144, 128)), whole_spec((144, 128)), whole_spec((128, 128))],
            [whole_out((shares, 16 + span, 128))],
            [],
            "spread_third",
            1e5,
            1e6,
        )(head, partner(head, 1), kept)[0]
    )

    block_out, e, t, t_edge, own4, st3, u_local, w_scaled = call(
        last_body,
        steps,
        [
            SMEM, eight, whole_spec((shares, 16 + span, 128)), large, large, step_spec(tile(128)),
            step_spec(tile(128)), step_spec(tile(128)), step_spec(tile(512)),
            step_spec(tile(512)), whole_spec((128, 512)),
        ],
        [
            step_out(rows, tile(512), bf16),
            step_out(rows, tile(512), bf16),
            (step_spec(tile(128)), pltpu.HBM((rows, columns, count, 128), bf16)),
            whole_out(edge(128), bf16),
            whole_out((16 + span, 128)),
            whole_out((16, 128)),
            whole_out((128, 512)),
            whole_out((256, 512), bf16),
        ],
        [
            pltpu.VMEM((8, 512), f32),
            pltpu.VMEM((256, 512), bf16),
            pltpu.VMEM((512, 256), bf16),
            pltpu.VMEM(tile(512), f32),
            pltpu.VMEM((128, 512), f32),
            pltpu.VMEM((2, 8, 512), f32),
            pltpu.VMEM((2, 8, 128), f32),
        ],
        "last_norm",
        pixels * 512 * 128 * 10,
        pixels * 4864,
        36,
    )(info, st1, arrived3, gc, sc, act_b, slope_b, dotted_b, images, cotangent, w_out)

    other4, y_edge, z2_edge, t_edge = lax.optimization_barrier(
        tuple(
            partner(v, 1)
            for v in lax.optimization_barrier((own4, y_edge, z2_edge, t_edge))
        )
    )
    arrived4 = swapped(
        call(
            both_body,
            1,
            [SMEM, whole_spec((16 + span, 128)), whole_spec((16 + span, 128))],
            [whole_out((shares, 16 + 2 * span, 128))],
            [],
            "spread_fourth",
            1e5,
            1e6,
        )(info, own4, other4)[0]
    )

    share = -(-1344 // (8 * shares)) * 8
    half = share * shares
    block = -(-(share + 6) // 16) * 16
    h, mine, sent, small_sums = call(
        back_body,
        steps + 1,
        [
            SMEM, eight, eight, whole_spec((16, 128)), whole_spec((shares, 16 + 2 * span, 128)),
            whole_spec((16 + span, 128)),
            whole_spec((512, 128)), whole_spec((136, 128)),
            whole_spec((128, 512)), small, small, small, large, whole_spec((128, 512)),
            whole_spec((256, 512)), taps,
            step_spec(tile(128), ahead), step_spec(tile(128), ahead), whole_spec(edge(256)),
            step_spec(tile(128), ahead), whole_spec(edge(128)),
            step_spec(tile(128), ahead), whole_spec(edge(128)),
            step_spec(tile(128), behind), step_spec(tile(128), behind),
            step_spec(tile(512), behind),
        ],
        [
            step_out(rows, tile(128), bf16, behind),
            whole_out((half + 8, 128)),
            whole_out((half + 8, 128)),
            whole_out((16, 128)),
        ],
        [
            pltpu.VMEM((8, 128), f32),
            pltpu.VMEM((128, 256), bf16),
            pltpu.VMEM((1536, 256), bf16),
            frame_like(),
            pltpu.VMEM((256, 1536), f32),
            pltpu.VMEM((128, 512), f32),
            pltpu.VMEM((2, 8, 128), f32),
            pltpu.VMEM((2 * half, 128), f32),
            pltpu.VMEM((16, 128), f32),
            pltpu.VMEM((2, 128, 128), f32),
        ],
        "middle_back",
        pixels * 32 * 128 * 128 * 2,
        pixels * 4000,
        49,
    )(
        info, st1, st2, st3, arrived4, own4, xz, gram, u_local, ga, sa, gb, gc,
        w_out, w_scaled, w_back,
        act_b, slope_b, y_edge, z2, z2_edge, t, t_edge, act_a, z1, images,
    )
    arrived = partner(sent, 1)
    spread = call(
        pack_body,
        1,
        [whole_spec((half + 8, 128)), whole_spec((half + 8, 128))],
        [whole_out((shares, block, 128), bf16)],
        [],
        "pack_shares",
        1e6,
        2e6,
    )(mine, arrived)[0]
    spread = swapped(spread)
    st5, spread = call(
        functools.partial(share_body, share),
        1,
        [whole_spec((shares, block, 128))],
        [whole_out((8, 128)), whole_out((shares, block, 128), bf16)],
        [],
        "sum_shares",
        1e6,
        1e6,
    )(spread)
    gathered = swapped(spread)

    grad_images = call(
        input_body,
        steps,
        [
            SMEM, eight, eight, small, whole_spec((512, 128)),
            step_spec(tile(128)), step_spec(tile(128)), step_spec(tile(512)),
        ],
        [step_out(rows, tile(512), bf16)],
        [pltpu.VMEM((8, 128), f32), pltpu.VMEM((128, 512), bf16)],
        "input_grad",
        pixels * 512 * 128 * 2,
        pixels * 2816,
    )(info, st1, st5, ga, w_in, h, z1, e)[0]

    gathered, grad_images = lax.optimization_barrier((gathered, grad_images))
    shared = whole_spec((shares, block, 128))
    gwi, gga, gsa, gwm, ggb, gsb, gwo, ggc, gsc = call(
        functools.partial(final_body, share),
        1,
        [SMEM, eight, eight, small, whole_spec((16, 128)), shared, shared],
        [
            whole_out((512, 128)), whole_out((1, 128)), whole_out((1, 128)),
            whole_out((1152, 128)), whole_out((1, 128)), whole_out((1, 128)),
            whole_out((128, 512)), whole_out((1, 512)), whole_out((1, 512)),
        ],
        [pltpu.VMEM((2 * half, 128), f32)],
        "replicated_grads",
        1e6,
        3e6,
    )(info, st1, st5, ga, small_sums, gathered, partner(gathered, 1))
    return (
        jnp.transpose(block_out, (2, 0, 1, 3)),
        jnp.transpose(grad_images, (2, 0, 1, 3)),
        gwi,
        gga.reshape(128),
        gsa.reshape(128),
        gwm.reshape(3, 3, 128, 128),
        ggb.reshape(128),
        gsb.reshape(128),
        gwo,
        ggc.reshape(512),
        gsc.reshape(512),
    )


def solution(mesh):
    split = P("batch", "rows", None, None)
    placed = (split, P("batch"), P(), P(), P(), P(), P(), P(), P(), P(), P(), split)
    return jax.shard_map(
        local,
        mesh=mesh,
        in_specs=placed,
        out_specs=(split, split) + (P(),) * 9,
        check_vma=False,
    )
```

```python
import functools
import math

import jax
import jax.numpy as jnp
from jax import lax
from jax.experimental import pallas as pl
from jax.experimental.pallas import tpu as pltpu
from jax.sharding import PartitionSpec as P

epsilon = 1e-05
axes = ("batch", "rows")
f32 = jnp.float32
bf16 = jnp.bfloat16
C0 = math.sqrt(2.0 / math.pi)
C1 = C0 * 0.044715
K0 = -2.0 * C0 / math.log(2.0)
K1 = -2.0 * C1 / math.log(2.0)
K2 = -3.0 * math.log(2.0)
HIGH = lax.Precision.HIGHEST


def partner(block, mask):
    total = lax.axis_size("batch") * lax.axis_size("rows")
    return lax.ppermute(block, axes, [(i, i ^ mask) for i in range(total)])


def swapped_sum(block, groups):
    size = len(groups[0])
    spread = jnp.broadcast_to(block[None], (size,) + block.shape)
    arrived = lax.all_to_all(spread, "batch", 0, 0, axis_index_groups=groups, tiled=True)
    return jnp.sum(arrived, axis=0)


def swapped(spread):
    return lax.all_to_all(spread, "batch", 0, 0, tiled=True)


def summed_at_once(spread):
    return jnp.sum(lax.all_to_all(spread, axes, 0, 0, tiled=True), axis=0)


def summed_by_swap(block, near=None):
    block = block + partner(block, 1)
    count = lax.axis_size("batch")
    if near is None or count % near:
        return swapped_sum(block, [list(range(count))])
    block = swapped_sum(block, [list(range(i, i + near)) for i in range(0, count, near)])
    return swapped_sum(block, [list(range(i, count, near)) for i in range(near)])


def gate(u):
    inner = K0 + K1 * (u * u)
    return pltpu.reciprocal(1.0 + jnp.exp2(u * inner), approx=True), inner


def gelu_terms(u):
    half, inner = gate(u)
    value = u * half
    slope = half + value * (1.0 - half) * (K2 * inner - 4.0 * C0)
    return value, slope


def gelu_value(u):
    return u * gate(u)[0]


def moments(total, squares, pixels):
    mean = total / pixels
    return mean, lax.rsqrt(squares / pixels - mean * mean + epsilon)


def fold8(values):
    lanes = values.shape[-1]
    return jnp.sum(values.reshape(values.size // (8 * lanes), 8, lanes), axis=0)


def total_row(values):
    return jnp.sum(values, axis=0, keepdims=True)


def wide(ref, start):
    return jnp.concatenate([ref[start + i : start + i + 1, :] for i in range(4)], axis=1)


def put_wide(ref, start, row):
    for i in range(4):
        ref[start + i : start + i + 1, :] = row[:, i * 128 : (i + 1) * 128]


def dot_tn(a, b):
    return lax.dot_general(a, b, (((0,), (0,)), ((), ())), preferred_element_type=f32)


def dot_nt(a, b, precision=None):
    return lax.dot_general(
        a, b, (((1,), (1,)), ((), ())), preferred_element_type=f32, precision=precision
    )


def dot(a, b, precision=None):
    return jnp.dot(a, b, preferred_element_type=f32, precision=precision)


def split_two(values):
    high = values.astype(bf16)
    return high, (values - high.astype(f32)).astype(bf16)


def dot_halves(a, b):
    high, low = split_two(a)
    return dot(high, b) + dot(low, b)


def row_of_sums(values):
    high, low = split_two(values)
    one = jnp.ones((16, values.shape[1]), bf16)
    return (dot_nt(one, high) + dot_nt(one, low))[0:8, :]


def call(body, grid, ins, outs, scratch, name, flops, bytes_moved, vmem=52):
    return pl.pallas_call(
        body,
        grid=(grid,),
        in_specs=ins,
        out_specs=[spec for spec, _ in outs],
        out_shape=[shape for _, shape in outs],
        scratch_shapes=scratch,
        name=name,
        compiler_params=pltpu.CompilerParams(
            dimension_semantics=("arbitrary",), vmem_limit_bytes=vmem << 20
        ),
        cost_estimate=pl.CostEstimate(
            flops=int(flops), bytes_accessed=int(bytes_moved), transcendentals=0
        ),
    )


SMEM = pl.BlockSpec(memory_space=pltpu.SMEM)
ANY = pl.BlockSpec(memory_space=pl.ANY)


def whole_spec(shape):
    return pl.BlockSpec(tuple(shape), lambda i: (0,) * len(shape))


def step_spec(shape, place=lambda i: i):
    return pl.BlockSpec(tuple(shape), lambda i: (place(i),) + (0,) * (len(shape) - 1))


def whole_out(shape, dtype=f32):
    return (whole_spec(shape), jax.ShapeDtypeStruct(shape, dtype))


def step_out(count, shape, dtype, place=lambda i: i):
    return (
        step_spec(shape, place),
        jax.ShapeDtypeStruct((count,) + tuple(shape[1:]), dtype),
    )


def live(info, images, lanes):
    return lax.broadcasted_iota(jnp.int32, (images, lanes), 0) < info[0]


def groups(columns):
    return [(c, min(4, columns - c)) for c in range(0, columns, 4)]


def take_edge(info, edge_ref, ref):
    step = pl.program_id(0)

    @pl.when((step == 0) & (info[1] == 1))
    def _():
        edge_ref[...] = ref[0].astype(edge_ref.dtype)

    @pl.when((step == pl.num_programs(0) - 1) & (info[1] == 0))
    def _():
        edge_ref[...] = ref[ref.shape[0] - 1].astype(edge_ref.dtype)


def first_body(info, x_ref, w_ref, z_ref, edge_ref, stat_ref, zacc):
    step = pl.program_id(0)
    tall, columns, images = x_ref.shape[:3]
    area = columns * images

    @pl.when(step == 0)
    def _():
        zacc[...] = jnp.zeros_like(zacc)

    mask = live(info, images, 128)
    for r in range(tall):
        x = x_ref[r].reshape(area, 512)
        z = dot(x, w_ref[...]).reshape(columns, images, 128)
        z = jnp.where(mask, z, 0.0)
        z_ref[r] = z
        zacc[0] += fold8(z)
        zacc[1] += fold8(z * z)
    take_edge(info, edge_ref, z_ref)

    @pl.when(step == pl.num_programs(0) - 1)
    def _():
        pixels = (info[0] * (pl.num_programs(0) * tall * columns)).astype(f32)
        block = jnp.concatenate(
            [
                total_row(zacc[0]),
                total_row(zacc[1]),
                jnp.full((1, 128), pixels, f32),
                jnp.zeros((5, 128), f32),
            ],
            axis=0,
        )
        for k in range(stat_ref.shape[0]):
            stat_ref[k] = block


def cross_body(x_ref, z_ref, xz_ref, acc):
    step = pl.program_id(0)
    tall, columns, images = x_ref.shape[:3]
    area = columns * images

    @pl.when(step == 0)
    def _():
        acc[...] = jnp.zeros_like(acc)

    for r in range(tall):
        z = z_ref[r].astype(bf16).reshape(area, 128)
        acc[...] += dot_tn(z, x_ref[r].reshape(area, 512))

    @pl.when(step == pl.num_programs(0) - 1)
    def _():
        for i in range(4):
            xz_ref[i * 128 : (i + 1) * 128, :] = acc[:, i * 128 : (i + 1) * 128]


def paired_weights(w_ref, target):
    for r in range(4):
        for u in range(3):
            for o in range(2):
                t = r - o
                base = (r * 3 + u) * 128
                if 0 <= t <= 2:
                    block = w_ref[t, u]
                else:
                    block = jnp.zeros((128, 128), bf16)
                target[base : base + 128, o * 128 : (o + 1) * 128] = block


def window(frame, pair):
    columns, images = frame.shape[1] - 2, frame.shape[2]
    parts = [
        frame[2 * pair + r, u : u + columns].reshape(columns * images, 128)
        for r in range(4)
        for u in range(3)
    ]
    return jnp.concatenate(parts, axis=1)


def clear_frame(frame):
    tall, wide_columns = frame.shape[:2]
    zero = jnp.zeros(frame.shape[2:], frame.dtype)
    for e in range(tall):
        frame[e, 0] = zero
        frame[e, wide_columns - 1] = zero
    for c in range(wide_columns):
        frame[0, c] = zero
        frame[tall - 1, c] = zero


def middle_body(
    info, st1, ga, sa, z_ref, edge_ref, w_ref, xz_ref,
    z2_ref, a_ref, stat_ref, frame, wide_w, coef, zacc,
):
    step = pl.program_id(0)
    last = pl.num_programs(0) - 1
    columns, images = z_ref.shape[1:3]
    area = columns * images

    def activated(z):
        return gelu_value(z * coef[0:1, :] + coef[1:2, :]).astype(bf16)

    @pl.when(step == 0)
    def _():
        mean, inv = moments(st1[0:1, :], st1[1:2, :], st1[2:3, :])
        scale = ga[...] * inv
        coef[0:1, :] = scale
        coef[1:2, :] = sa[...] - mean * scale
        paired_weights(w_ref, wide_w)
        zacc[...] = jnp.zeros_like(zacc)
        clear_frame(frame)
        place = (1 - info[1]) * (frame.shape[0] - 1)
        for c, n in groups(columns):
            frame[place, 1 + c : 1 + c + n] = activated(edge_ref[c : c + n])

    @pl.when(step < last)
    def _():
        for r in range(2):
            for c, n in groups(columns):
                value = activated(z_ref[r, c : c + n])
                frame[2 * step + 1 + r, 1 + c : 1 + c + n] = value
                a_ref[r, c : c + n] = value

    @pl.when(step > 0)
    def _():
        mask = live(info, images, 128)
        y = dot(window(frame, step - 1), wide_w[...])
        for r in range(2):
            z = y[:, r * 128 : (r + 1) * 128].reshape(columns, images, 128)
            z2_ref[r] = z
            zacc[0] += fold8(jnp.where(mask, jnp.sum(z, axis=0), 0.0))
            zacc[1] += fold8(jnp.where(mask, jnp.sum(z * z, axis=0), 0.0))

    @pl.when(step == last)
    def _():
        stat_ref[...] = jnp.zeros_like(stat_ref)
        for k in range(2):
            stat_ref[k : k + 1, :] = total_row(zacc[k])


def second_coef(st1, st2, gb, sb, coef):
    mean, inv = moments(st2[0:1, :], st2[1:2, :], st1[2:3, :])
    scale = gb[...] * inv
    coef[0:1, :] = scale
    coef[1:2, :] = sb[...] - mean * scale
    coef[2:3, :] = inv
    coef[3:4, :] = -mean * inv


def second_body(
    info, st1, st2, gb, sb, z_ref, wo_ref,
    act_ref, g_ref, gx_ref, ye_ref, ze_ref, st_ref, keep_ref, gram_ref, coef, cross, sums,
):
    step = pl.program_id(0)
    tall, columns, images = z_ref.shape[:3]
    area = columns * images

    @pl.when(step == 0)
    def _():
        second_coef(st1, st2, gb, sb, coef)
        cross[...] = jnp.zeros_like(cross)
        sums[...] = jnp.zeros_like(sums)

    mask = live(info, images, 128)
    scale, bias, inv, shift = (coef[i : i + 1, :] for i in range(4))
    edge_row = (1 - info[1]) * (tall - 1)
    at_edge = step == (1 - info[1]) * (pl.num_programs(0) - 1)
    totals = [jnp.zeros((images, 128), f32) for _ in range(3)]
    for r in range(tall):
        acts, others = [], []
        for c, n in groups(columns):
            z = z_ref[r, c : c + n]
            value, slope = gelu_terms(z * scale + bias)
            dotted = slope * (z * inv + shift)
            slope, dotted, value = (v.astype(bf16) for v in (slope, dotted, value))
            for k, part in enumerate((slope, dotted, value)):
                totals[k] += jnp.sum(part.astype(f32), axis=0)
            g_ref[r, c : c + n] = slope
            gx_ref[r, c : c + n] = dotted
            act_ref[r, c : c + n] = value
            value = jnp.where(mask, value, jnp.zeros((), bf16))
            acts.append(value.reshape(n * images, 128))
        acts = jnp.concatenate(acts, axis=0)
        cross[...] += dot_tn(
            acts,
            jnp.concatenate(
                [acts, g_ref[r].reshape(area, 128), gx_ref[r].reshape(area, 128)], axis=1
            ),
        )

        @pl.when(at_edge & (edge_row == r))
        def _():
            ye_ref[:, :, 0:128] = act_ref[r]
            ye_ref[:, :, 128:256] = g_ref[r]
            ze_ref[...] = z_ref[r]

    for k in range(3):
        sums[k] += fold8(jnp.where(mask, totals[k], 0.0))

    @pl.when(step == pl.num_programs(0) - 1)
    def _():
        gram = cross[:, 0:128]
        gram_ref[0:128, :] = gram
        st_ref[8:16, :] = jnp.zeros((8, 128), f32)
        st_ref[8:9, :] = total_row(sums[2])
        gram_ref[128:136, :] = st_ref[8:16, :]
        spread = dot_halves(gram_ref[...], wo_ref[...])
        put_wide(st_ref, 0, spread[128:129, :])
        put_wide(st_ref, 4, total_row(spread[0:128, :] * wo_ref[...].astype(f32)))
        st_ref[9:16, :] = jnp.zeros((7, 128), f32)
        for k in range(2):
            st_ref[9 + k : 10 + k, :] = total_row(sums[k])
        low = info[1] == 0
        keep_ref[...] = jnp.where(low, cross[:, 128:256], cross[:, 256:384])
        st_ref[16:144, :] = jnp.where(low, cross[:, 256:384], cross[:, 128:256])


def spread_body(head_ref, arrived_ref, keep_ref, out_ref):
    sums = head_ref[0:16, :] + arrived_ref[0:16, :]
    share = 128 // out_ref.shape[0]
    for k in range(out_ref.shape[0]):
        rows = slice(k * share, (k + 1) * share)
        out_ref[k, 0:16] = sums
        out_ref[k, 16 : 16 + share] = keep_ref[rows, :] + arrived_ref[16 + k * share : 16 + (k + 1) * share, :]
        if share < 8:
            out_ref[k, 16 + share :] = jnp.zeros((8 - share, 128), f32)


def both_body(info, own_ref, arrived_ref, out_ref):
    sums = own_ref[0:16, :] + arrived_ref[0:16, :]
    mine, other = own_ref[16:, :], arrived_ref[16:, :]
    low = info[1] == 0
    block = jnp.concatenate(
        [sums, jnp.where(low, mine, other), jnp.where(low, other, mine)], axis=0
    )
    for k in range(out_ref.shape[0]):
        out_ref[k] = block


def last_body(
    info, st1, in3, gc, sc, y_ref, g_ref, gx_ref, x_ref, cot_ref, wo_ref,
    out_ref, e_ref, t_ref, te_ref, st_ref, st3, u_ref, ws_ref,
    coef, w_two, w_turn, z_buf, cross, sums, sums_b,
):
    step = pl.program_id(0)
    tall, columns, images = x_ref.shape[:3]
    area = columns * images

    @pl.when(step == 0)
    def _():
        total = in3[0]
        for k in range(1, in3.shape[0]):
            total = total + in3[k]
        st3[...] = total[0:16]
        st_ref[16:, :] = total[16:]
        mean, inv = moments(wide(st3, 0), wide(st3, 4), st1[2:3, 0:1])
        scale = gc[...] * inv
        coef[0:1, :] = sc[...] - mean * scale
        high, low = split_two(wo_ref[...].astype(f32) * scale)
        w_two[0:128, :] = high
        w_two[128:256, :] = low
        ws_ref[...] = w_two[...]
        w_turn[:, 0:128] = jnp.transpose(w_two[0:128, :])
        w_turn[:, 128:256] = jnp.transpose(w_two[128:256, :])
        cross[...] = jnp.zeros_like(cross)
        sums[...] = jnp.zeros_like(sums)
        sums_b[...] = jnp.zeros_like(sums_b)

    mask = live(info, images, 512)
    bias = coef[0:1, :]
    zero = jnp.zeros((), bf16)
    piece = columns
    parts = [(r, c) for r in range(tall) for c in range(0, columns, piece)]
    n = piece * images

    def product(r, c):
        act = y_ref[r, c : c + piece].reshape(n, 128)
        z = dot(jnp.concatenate([act, act], axis=1), w_two[...])
        z_buf[r, c : c + piece] = z.reshape(piece, images, 512)

    def pointwise(r, c):
        x = jnp.where(mask, x_ref[r, c], zero).astype(f32)
        value, slope = gelu_terms(z_buf[r, c] + (bias + x))
        out_ref[r, c] = value.astype(bf16)
        cot = jnp.where(mask, cot_ref[r, c], zero).astype(f32)
        e = slope * cot
        e_ref[r, c] = e.astype(bf16)
        return fold8(e), fold8(x)

    def collect(r, c):
        e = e_ref[r, c : c + piece].reshape(n, 512)
        cross[...] += dot_tn(y_ref[r, c : c + piece].reshape(n, 128), e)

    def through(r, c):
        y = dot(e_ref[r, c : c + piece].reshape(n, 512), w_turn[...])
        t = (y[:, 0:128] + y[:, 128:256]).reshape(piece, images, 128)
        t_ref[r, c : c + piece] = t.astype(bf16)
        sums_b[0] += fold8(t * g_ref[r, c : c + piece].astype(f32))
        sums_b[1] += fold8(t * gx_ref[r, c : c + piece].astype(f32))

    product(*parts[0])
    for k in range(len(parts) + 1):
        work = []
        if k + 1 < len(parts):
            work.append(functools.partial(product, *parts[k + 1]))
        if k > 0:
            work.append(functools.partial(through, *parts[k - 1]))
            work.append(functools.partial(collect, *parts[k - 1]))
        if k < len(parts):
            r, first = parts[k]
            total_e = jnp.zeros((8, 512), f32)
            total_x = jnp.zeros((8, 512), f32)
            for c in range(piece):
                if c % 2 == 0 and work:
                    work.pop(0)()
                add_e, add_x = pointwise(r, first + c)
                total_e += add_e
                total_x += add_x
            sums[0] += total_e
            sums[1] += total_x
        for rest in work:
            rest()
    take_edge(info, te_ref, t_ref)

    @pl.when(step == pl.num_programs(0) - 1)
    def _():
        u_ref[...] = cross[...]
        put_wide(st_ref, 0, total_row(sums[0]))
        put_wide(st_ref, 4, total_row(wo_ref[...].astype(f32) * cross[...]))
        put_wide(st_ref, 10, total_row(sums[1]))
        for k in range(2):
            st_ref[8 + k : 9 + k, :] = total_row(sums_b[k])
            st_ref[14 + k : 15 + k, :] = jnp.zeros((1, 128), f32)


def back_body(
    info, st1, st2, st3, in4, own4, xz_ref, gram_ref, u_ref, ga, sa, gb, gc, wo_ref, ws_ref, wt_ref,
    y_ref, s_ref, ye_ref, z2_ref, ze_ref, t_ref, te_ref, a_ref, z1_ref, x_ref,
    h_ref, mine_ref, sent_ref, small_ref,
    coef, mm, wide_w, frame, dacc, vacc, sums, packed, st4, pq,
):
    step = pl.program_id(0)
    last = pl.num_programs(0) - 1
    columns, images = z1_ref.shape[1:3]
    area = columns * images
    mask = live(info, images, 128)

    def second_back(t, product, slope, z):
        kappa, scale_b, beta, alpha = (coef[i : i + 1, :] for i in range(4))
        through = t.astype(f32) - kappa - product[..., 0:128] - product[..., 128:256]
        grad = scale_b * (slope.astype(f32) * through) - (alpha + beta * z)
        return jnp.where(mask, grad, 0.0).astype(bf16)

    @pl.when(step == 0)
    def _():
        pixels = st1[2:3, :]
        pixel = st1[2:3, 0:1]
        mean_a, inv_a = moments(st1[0:1, :], st1[1:2, :], pixels)
        mean_b, inv_b = moments(st2[0:1, :], st2[1:2, :], pixels)
        mean_c, inv_c = moments(wide(st3, 0), wide(st3, 4), pixel)
        total = in4[0, 0:16]
        share = 128 // in4.shape[0]
        span = (in4.shape[1] - 16) // 2
        for k in range(in4.shape[0]):
            if k > 0:
                total = total + in4[k, 0:16]
            rows = slice(k * share, (k + 1) * share)
            pq[0, rows] = in4[k, 16 : 16 + share]
            pq[1, rows] = in4[k, 16 + span : 16 + span + share]
        st4[...] = total
        total_c = wide(st4, 0)
        dot_c = inv_c * (wide(st4, 4) - mean_c * total_c)
        weights = wo_ref[...].astype(f32)
        scaled = ws_ref[0:128, :].astype(f32) + ws_ref[128:256, :].astype(f32)
        near, far = split_two(weights * (inv_c * dot_c / pixel))
        mat = dot_nt(near, ws_ref[0:128, :]) + dot_nt(near, ws_ref[128:256, :])
        mat = mat + dot_nt(far, ws_ref[0:128, :])
        high, low = split_two(mat)
        mm[:, 0:128] = high
        mm[:, 128:256] = low
        kappa = row_of_sums(scaled * (total_c / pixel))[0:1, :]
        mean_act = jnp.transpose(jnp.broadcast_to(st3[8:9, :] / pixels, (8, 128)))[:, 0:1]
        kappa = kappa - total_row(mean_act * mat)
        total_b = st4[8:9, :] - kappa * st3[9:10, :] - total_row(mat * pq[0])
        dot_b = st4[9:10, :] - kappa * st3[10:11, :] - total_row(mat * pq[1])
        scale_b = gb[...] * inv_b
        scale_a = ga[...] * inv_a
        coef[0:1, :] = kappa
        coef[1:2, :] = scale_b
        coef[2:3, :] = scale_b * inv_b * dot_b / pixels
        coef[3:4, :] = scale_b * (total_b - mean_b * inv_b * dot_b) / pixels
        coef[4:5, :] = scale_a
        coef[5:6, :] = sa[...] - mean_a * scale_a
        small_ref[...] = jnp.zeros_like(small_ref)
        put_wide(small_ref, 0, total_c)
        put_wide(small_ref, 4, dot_c)
        small_ref[8:9, :] = total_b
        small_ref[9:10, :] = dot_b
        column = jnp.transpose(gram_ref[128:136, :])[:, 0:1]
        product = dot_halves(gram_ref[0:128, :], wo_ref[...])
        grad = u_ref[...] - column * (total_c / pixel) - (product - column * mean_c) * (
            inv_c * dot_c / pixel
        )
        grad = grad * (gc[...] * inv_c)
        for i in range(4):
            packed[1152 + i * 128 : 1280 + i * 128, :] = grad[:, i * 128 : (i + 1) * 128]
        paired_weights(wt_ref, wide_w)
        dacc[...] = jnp.zeros_like(dacc)
        vacc[...] = jnp.zeros_like(vacc)
        sums[...] = jnp.zeros_like(sums)
        clear_frame(frame)
        place = (1 - info[1]) * (frame.shape[0] - 1)
        for c, n in groups(columns):
            act = ye_ref[c : c + n, :, 0:128].reshape(n * images, 128)
            extra = dot(act, mm[...]).reshape(n, images, 256)
            frame[place, 1 + c : 1 + c + n] = second_back(
                te_ref[c : c + n], extra, ye_ref[c : c + n, :, 128:256], ze_ref[c : c + n]
            )

    @pl.when(step < last)
    def _():
        for r in range(2):
            act = y_ref[r].reshape(area, 128)
            extra = dot(act, mm[...]).reshape(columns, images, 256)
            for c, n in groups(columns):
                frame[2 * step + 1 + r, 1 + c : 1 + c + n] = second_back(
                    t_ref[r, c : c + n],
                    extra[c : c + n],
                    s_ref[r, c : c + n],
                    z2_ref[r, c : c + n],
                )

    @pl.when(step > 0)
    def _():
        scale_a, bias_a = coef[4:5, :], coef[5:6, :]
        near = window(frame, step - 1)
        through = dot(near, wide_w[...])
        act = jnp.concatenate([a_ref[r].reshape(area, 128) for r in range(2)], axis=1)
        dacc[...] += dot_tn(act, near)
        total = jnp.zeros((8, 128), f32)
        dots = jnp.zeros((8, 128), f32)
        for r in range(2):
            part = through[:, r * 128 : (r + 1) * 128].reshape(columns, images, 128)
            for c, n in groups(columns):
                z = z1_ref[r, c : c + n]
                slope = gelu_terms(z * scale_a + bias_a)[1]
                grad = part[c : c + n] * slope
                total += fold8(grad)
                dots += fold8(grad * z)
                h_ref[r, c : c + n] = grad.astype(bf16)
        sums[0] += total
        sums[1] += dots
        vacc[...] += dot_tn(h_ref[...].reshape(2 * area, 128), x_ref[...].reshape(2 * area, 512))

    @pl.when(step == last)
    def _():
        pixels = st1[2:3, :]
        total_h, dot_h = total_row(sums[0]), total_row(sums[1])
        tail = jnp.concatenate(
            [total_h, dot_h, st1[0:1, :] / pixels, jnp.zeros((5, 128), f32)], axis=0
        )
        columns2 = jnp.transpose(tail)
        column_h, mean_a = columns2[:, 0:1], columns2[:, 2:3]
        for i in range(4):
            lanes = slice(i * 128, (i + 1) * 128)
            center = st4[10 + i : 11 + i, :] / pixels
            packed[1664 + i * 128 : 1792 + i * 128, :] = vacc[:, lanes] - column_h * center
            packed[2176 + i * 128 : 2304 + i * 128, :] = (
                xz_ref[lanes, :] - mean_a * own4[10 + i : 11 + i, :]
            )
        for t in range(3):
            for u in range(3):
                parts = []
                for o in range(2):
                    base = ((o + 2 - t) * 3 + 2 - u) * 128
                    parts.append(dacc[o * 128 : (o + 1) * 128, base : base + 128])
                packed[(t * 3 + u) * 128 : (t * 3 + u + 1) * 128, :] = parts[0] + parts[1]
        if packed.shape[0] > 2688:
            packed[2688:, :] = jnp.zeros((packed.shape[0] - 2688, 128), f32)
        half = packed.shape[0] // 2
        low = info[1] == 0
        mine_ref[0:half, :] = jnp.where(low, packed[0:half, :], packed[half:, :])
        sent_ref[0:half, :] = jnp.where(low, packed[half:, :], packed[0:half, :])
        mine_ref[half : half + 8, :] = tail
        sent_ref[half : half + 8, :] = tail


def pack_body(mine_ref, arrived_ref, out_ref):
    shares, block = out_ref.shape[:2]
    share = (mine_ref.shape[0] - 8) // shares
    small = mine_ref[shares * share :, :] + arrived_ref[shares * share :, :]
    high = small.astype(bf16).astype(f32)
    middle = (small - high).astype(bf16).astype(f32)
    low = small - high - middle
    tail = jnp.concatenate(
        [high[0:2], middle[0:2], low[0:2], jnp.zeros((block - share - 6, 128), f32)], axis=0
    )
    for k in range(shares):
        rows = slice(k * share, (k + 1) * share)
        total = mine_ref[rows, :] + arrived_ref[rows, :]
        out_ref[k] = jnp.concatenate([total, tail], axis=0).astype(bf16)


def share_body(share, in_ref, small_ref, out_ref):
    total = in_ref[0].astype(f32)
    for k in range(1, in_ref.shape[0]):
        total = total + in_ref[k].astype(f32)
    sums = total[share : share + 2] + total[share + 2 : share + 4] + total[share + 4 : share + 6]
    small_ref[...] = jnp.concatenate([sums, jnp.zeros((6, 128), f32)], axis=0)
    for k in range(out_ref.shape[0]):
        out_ref[k] = total.astype(bf16)


def input_body(info, st1, st5, ga, wi_ref, h_ref, z_ref, e_ref, g_ref, coef, w_turn):
    step = pl.program_id(0)
    tall, columns, images = z_ref.shape[:3]
    area = columns * images

    @pl.when(step == 0)
    def _():
        pixels = st1[2:3, :]
        mean, inv = moments(st1[0:1, :], st1[1:2, :], pixels)
        scale = ga[...] * inv
        w_turn[...] = jnp.transpose(wi_ref[...])
        total = st5[0:1, :]
        dot_a = inv * (st5[1:2, :] - mean * total)
        coef[0:1, :] = scale
        coef[1:2, :] = scale * inv * dot_a / pixels
        coef[2:3, :] = scale * (total - mean * inv * dot_a) / pixels

    mask = live(info, images, 128)
    scale, beta, alpha = (coef[i : i + 1, :] for i in range(3))
    for r in range(tall):
        parts = []
        for c, n in groups(columns):
            grad = scale * h_ref[r, c : c + n].astype(f32) - (alpha + beta * z_ref[r, c : c + n])
            parts.append(jnp.where(mask, grad, 0.0).astype(bf16).reshape(n * images, 128))
        through = dot(jnp.concatenate(parts, axis=0), w_turn[...])
        through = through.reshape(columns, images, 512)
        for c in range(columns):
            g_ref[r, c] = (through[c] + e_ref[r, c].astype(f32)).astype(bf16)


def final_body(
    share, info, st1, st5, ga, small_ref, mine_ref, other_ref,
    gwi_ref, gga_ref, gsa_ref, gwm_ref, ggb_ref, gsb_ref, gwo_ref, ggc_ref, gsc_ref, total_ref,
):
    shares = mine_ref.shape[0]
    for k in range(shares):
        mine, other = mine_ref[k].astype(f32), other_ref[k].astype(f32)
        low = jnp.where(info[1] == 0, mine, other)
        high = jnp.where(info[1] == 0, other, mine)
        total_ref[k * share : (k + 1) * share, :] = low[0:share]
        total_ref[(shares + k) * share : (shares + k + 1) * share, :] = high[0:share]
    pixels = st1[2:3, :]
    mean, inv = moments(st1[0:1, :], st1[1:2, :], pixels)
    total = st5[0:1, :]
    dot = inv * (st5[1:2, :] - mean * total)
    gsa_ref[...] = total
    gga_ref[...] = dot
    gsb_ref[...] = small_ref[8:9, :]
    ggb_ref[...] = small_ref[9:10, :]
    gsc_ref[...] = wide(small_ref, 0)
    ggc_ref[...] = wide(small_ref, 4)
    gwm_ref[...] = total_ref[0:1152, :]
    for i in range(4):
        gwo_ref[:, i * 128 : (i + 1) * 128] = total_ref[1152 + i * 128 : 1280 + i * 128, :]
        v = jnp.transpose(total_ref[1664 + i * 128 : 1792 + i * 128, :])
        xz = jnp.transpose(total_ref[2176 + i * 128 : 2304 + i * 128, :])
        gwi_ref[i * 128 : (i + 1) * 128, :] = (ga[...] * inv) * (v - xz * (inv * dot / pixels))


def local(
    images, counts, w_in, gain_a, shift_a, w_mid, gain_b, shift_b, w_out, gain_c, shift_c, cotangent
):
    count, rows, columns, channels = images.shape
    steps = rows // 2
    info = jnp.stack([counts[0], lax.axis_index("rows").astype(jnp.int32)])
    images = jnp.transpose(images, (1, 2, 0, 3))
    cotangent = jnp.transpose(cotangent, (1, 2, 0, 3))
    ga, sa, gb, sb = (v.reshape(1, 128) for v in (gain_a, shift_a, gain_b, shift_b))
    gc, sc = gain_c.reshape(1, 512), shift_c.reshape(1, 512)
    small = whole_spec((1, 128))
    large = whole_spec((1, 512))
    eight = whole_spec((8, 128))
    taps = whole_spec((3, 3, 128, 128))

    def tile(lanes):
        return (2, columns, count, lanes)

    def edge(lanes):
        return (columns, count, lanes)

    def ahead(i):
        return jnp.minimum(i, steps - 1)

    def behind(i):
        return jnp.maximum(i - 1, 0)

    def frame_like():
        return pltpu.VMEM((rows + 2, columns + 2, count, 128), bf16)

    pixels = count * rows * columns
    shares = lax.axis_size("batch")

    z1, z1_edge, st1 = call(
        first_body,
        steps,
        [SMEM, step_spec(tile(512)), whole_spec((512, 128))],
        [
            step_out(rows, tile(128), f32),
            whole_out(edge(128)),
            whole_out((shares * lax.axis_size("rows"), 8, 128)),
        ],
        [pltpu.VMEM((2, 8, 128), f32)],
        "first_norm_sums",
        pixels * 512 * 128 * 2,
        pixels * 1536,
        58,
    )(info, images, w_in)
    z1_edge = partner(z1_edge, 1)
    st1 = summed_at_once(st1)
    xz = call(
        cross_body,
        steps,
        [step_spec(tile(512)), step_spec(tile(128))],
        [whole_out((512, 128))],
        [pltpu.VMEM((128, 512), f32)],
        "input_cross",
        pixels * 512 * 128 * 2,
        pixels * 1536,
    )(images, z1)[0]
    w_back = jnp.swapaxes(w_mid[::-1, ::-1], 2, 3)
    xz, w_back = lax.optimization_barrier((xz, w_back))

    span = max(8, 128 // shares)
    everyone = [list(range(lax.axis_size("batch")))]
    z2, act_a, st2 = call(
        middle_body,
        steps + 1,
        [
            SMEM, eight, small, small, step_spec(tile(128), ahead), whole_spec(edge(128)), taps,
            whole_spec((512, 128)),
        ],
        [
            step_out(rows, tile(128), f32, behind),
            step_out(rows, tile(128), bf16, ahead),
            whole_out((8, 128)),
        ],
        [
            frame_like(),
            pltpu.VMEM((1536, 256), bf16),
            pltpu.VMEM((8, 128), f32),
            pltpu.VMEM((2, 8, 128), f32),
        ],
        "middle_conv",
        pixels * 12 * 128 * 128 * 2,
        pixels * 1280,
    )(info, st1, ga, sa, z1, z1_edge, w_mid, xz)
    st2 = summed_by_swap(st2)

    act_b, slope_b, dotted_b, y_edge, z2_edge, head, kept, gram = call(
        second_body,
        steps,
        [SMEM, eight, eight, small, small, step_spec(tile(128)), whole_spec((128, 512))],
        [
            step_out(rows, tile(128), bf16),
            step_out(rows, tile(128), bf16),
            step_out(rows, tile(128), bf16),
            whole_out(edge(256), bf16),
            whole_out(edge(128)),
            whole_out((144, 128)),
            whole_out((128, 128)),
            whole_out((136, 128)),
        ],
        [pltpu.VMEM((8, 128), f32), pltpu.VMEM((128, 384), f32), pltpu.VMEM((3, 8, 128), f32)],
        "second_norm",
        pixels * 384 * 128 * 2,
        pixels * 1280,
        42,
    )(info, st1, st2, gb, sb, z2, w_out)
    arrived3 = swapped(
        call(
            spread_body,
            1,
            [whole_spec((144, 128)), whole_spec((144, 128)), whole_spec((128, 128))],
            [whole_out((shares, 16 + span, 128))],
            [],
            "spread_third",
            1e5,
            1e6,
        )(head, partner(head, 1), kept)[0]
    )

    block_out, e, t, t_edge, own4, st3, u_local, w_scaled = call(
        last_body,
        steps,
        [
            SMEM, eight, whole_spec((shares, 16 + span, 128)), large, large, step_spec(tile(128)),
            step_spec(tile(128)), step_spec(tile(128)), step_spec(tile(512)),
            step_spec(tile(512)), whole_spec((128, 512)),
        ],
        [
            step_out(rows, tile(512), bf16),
            step_out(rows, tile(512), bf16),
            (step_spec(tile(128)), pltpu.HBM((rows, columns, count, 128), bf16)),
            whole_out(edge(128), bf16),
            whole_out((16 + span, 128)),
            whole_out((16, 128)),
            whole_out((128, 512)),
            whole_out((256, 512), bf16),
        ],
        [
            pltpu.VMEM((8, 512), f32),
            pltpu.VMEM((256, 512), bf16),
            pltpu.VMEM((512, 256), bf16),
            pltpu.VMEM(tile(512), f32),
            pltpu.VMEM((128, 512), f32),
            pltpu.VMEM((2, 8, 512), f32),
            pltpu.VMEM((2, 8, 128), f32),
        ],
        "last_norm",
        pixels * 512 * 128 * 10,
        pixels * 4864,
        36,
    )(info, st1, arrived3, gc, sc, act_b, slope_b, dotted_b, images, cotangent, w_out)

    other4, y_edge, z2_edge, t_edge = lax.optimization_barrier(
        tuple(
            partner(v, 1)
            for v in lax.optimization_barrier((own4, y_edge, z2_edge, t_edge))
        )
    )
    arrived4 = swapped(
        call(
            both_body,
            1,
            [SMEM, whole_spec((16 + span, 128)), whole_spec((16 + span, 128))],
            [whole_out((shares, 16 + 2 * span, 128))],
            [],
            "spread_fourth",
            1e5,
            1e6,
        )(info, own4, other4)[0]
    )

    share = -(-1344 // (8 * shares)) * 8
    half = share * shares
    block = -(-(share + 6) // 16) * 16
    h, mine, sent, small_sums = call(
        back_body,
        steps + 1,
        [
            SMEM, eight, eight, whole_spec((16, 128)), whole_spec((shares, 16 + 2 * span, 128)),
            whole_spec((16 + span, 128)),
            whole_spec((512, 128)), whole_spec((136, 128)),
            whole_spec((128, 512)), small, small, small, large, whole_spec((128, 512)),
            whole_spec((256, 512)), taps,
            step_spec(tile(128), ahead), step_spec(tile(128), ahead), whole_spec(edge(256)),
            step_spec(tile(128), ahead), whole_spec(edge(128)),
            step_spec(tile(128), ahead), whole_spec(edge(128)),
            step_spec(tile(128), behind), step_spec(tile(128), behind),
            step_spec(tile(512), behind),
        ],
        [
            step_out(rows, tile(128), bf16, behind),
            whole_out((half + 8, 128)),
            whole_out((half + 8, 128)),
            whole_out((16, 128)),
        ],
        [
            pltpu.VMEM((8, 128), f32),
            pltpu.VMEM((128, 256), bf16),
            pltpu.VMEM((1536, 256), bf16),
            frame_like(),
            pltpu.VMEM((256, 1536), f32),
            pltpu.VMEM((128, 512), f32),
            pltpu.VMEM((2, 8, 128), f32),
            pltpu.VMEM((2 * half, 128), f32),
            pltpu.VMEM((16, 128), f32),
            pltpu.VMEM((2, 128, 128), f32),
        ],
        "middle_back",
        pixels * 32 * 128 * 128 * 2,
        pixels * 4000,
        49,
    )(
        info, st1, st2, st3, arrived4, own4, xz, gram, u_local, ga, sa, gb, gc,
        w_out, w_scaled, w_back,
        act_b, slope_b, y_edge, z2, z2_edge, t, t_edge, act_a, z1, images,
    )
    arrived = partner(sent, 1)
    spread = call(
        pack_body,
        1,
        [whole_spec((half + 8, 128)), whole_spec((half + 8, 128))],
        [whole_out((shares, block, 128), bf16)],
        [],
        "pack_shares",
        1e6,
        2e6,
    )(mine, arrived)[0]
    spread = swapped(spread)
    st5, spread = call(
        functools.partial(share_body, share),
        1,
        [whole_spec((shares, block, 128))],
        [whole_out((8, 128)), whole_out((shares, block, 128), bf16)],
        [],
        "sum_shares",
        1e6,
        1e6,
    )(spread)
    gathered = swapped(spread)

    grad_images = call(
        input_body,
        steps,
        [
            SMEM, eight, eight, small, whole_spec((512, 128)),
            step_spec(tile(128)), step_spec(tile(128)), step_spec(tile(512)),
        ],
        [step_out(rows, tile(512), bf16)],
        [pltpu.VMEM((8, 128), f32), pltpu.VMEM((128, 512), bf16)],
        "input_grad",
        pixels * 512 * 128 * 2,
        pixels * 2816,
    )(info, st1, st5, ga, w_in, h, z1, e)[0]

    gathered, grad_images = lax.optimization_barrier((gathered, grad_images))
    shared = whole_spec((shares, block, 128))
    gwi, gga, gsa, gwm, ggb, gsb, gwo, ggc, gsc = call(
        functools.partial(final_body, share),
        1,
        [SMEM, eight, eight, small, whole_spec((16, 128)), shared, shared],
        [
            whole_out((512, 128)), whole_out((1, 128)), whole_out((1, 128)),
            whole_out((1152, 128)), whole_out((1, 128)), whole_out((1, 128)),
            whole_out((128, 512)), whole_out((1, 512)), whole_out((1, 512)),
        ],
        [pltpu.VMEM((2 * half, 128), f32)],
        "replicated_grads",
        1e6,
        3e6,
    )(info, st1, st5, ga, small_sums, gathered, partner(gathered, 1))
    return (
        jnp.transpose(block_out, (2, 0, 1, 3)),
        jnp.transpose(grad_images, (2, 0, 1, 3)),
        gwi,
        gga.reshape(128),
        gsa.reshape(128),
        gwm.reshape(3, 3, 128, 128),
        ggb.reshape(128),
        gsb.reshape(128),
        gwo,
        ggc.reshape(512),
        gsc.reshape(512),
    )


def solution(mesh):
    split = P("batch", "rows", None, None)
    placed = (split, P("batch"), P(), P(), P(), P(), P(), P(), P(), P(), P(), split)
    return jax.shard_map(
        local,
        mesh=mesh,
        in_specs=placed,
        out_specs=(split, split) + (P(),) * 9,
        check_vma=False,
    )
```
